32 devices in a mesh: seq: 8 (over z, x), head: 4 (over y, core).
Axes of the slice: x: 2, y: 2, z: 4, core: 2. Of those that a mesh axis runs over, the one named last changes fastest.
Arguments:
- hidden: bfloat16 [2, 4096, 1536], P(None, 'seq', 'head'), may hold values from -6 to 6
- output_grad: bfloat16 [2, 4096, 1536], P(None, 'seq', 'head'), may hold values from -6 to 6
- lengths: int32 [2, 4], replicated, may hold values from 1 to 3840, 4096 in all within a row
- seq_order: int32 [2, 4], replicated, may hold values from 0 to 3, each once within a row
- routes: int32 [2, 4096, 6], P(None, 'seq'), may hold values from 0 to 31, all different within a row; in each aligned block of 512 rows (0 to 511, 512 to 1023, ..., all dimensions but the last counted through in order) at most 192 rows name the same one
- mix_gain: float32 [1536], P('head'), may hold values from 0.5 to 1.5
- input_proj: bfloat16 [2, 1536, 3072], P(None, 'seq', 'head'), may hold values from -0.15309311 to 0.15309311
- state_proj: bfloat16 [1536, 256], P('seq'), may hold values from -0.15309311 to 0.15309311
- step_proj: bfloat16 [1536, 48], P('seq', 'head'), may hold values from -0.15309311 to 0.15309311
- conv_inner: float32 [4, 3072], P(None, 'head'), may hold values from -3 to 3
- conv_state: float32 [4, 256], replicated, may hold values from -3 to 3
- inner_bias: float32 [3072], P('head'), may hold values from -1.2 to 1.2
- state_bias: float32 [256], replicated, may hold values from -1.2 to 1.2
- step_bias: float32 [48], P('head'), may hold values from -2 to 0.5
- decay_rate: float32 [48], P('head'), may hold values from 6.1035156e-05 to 0.08
- skip_gain: float32 [48], P('head'), may hold values from 0.5 to 1.5
- gate_gain: float32 [3072], P('head'), may hold values from 0.5 to 1.5
- output_proj: bfloat16 [3072, 1536], P('head', 'seq'), may hold values from -0.108253175 to 0.108253175
- moe_gain: float32 [1536], P('head'), may hold values from 0.5 to 1.5
- router: bfloat16 [1536, 32], P('seq'), may hold values from -0.076546554 to 0.076546554
- expert_up: bfloat16 [32, 1536, 1024], P('head', 'seq'), may hold values from -0.15309311 to 0.15309311
- expert_down: bfloat16 [32, 512, 1536], P('head', None, 'seq'), may hold values from -0.53033009 to 0.53033009
- shared_up: bfloat16 [1536, 2, 1024], P('seq', None, 'head'), may hold values from -0.15309311 to 0.15309311
- shared_down: bfloat16 [1024, 1536], P('head', 'seq'), may hold values from -0.1875 to 0.1875
Outputs:
- output: bfloat16 [2, 4096, 1536], P(None, 'seq', 'head')
- hidden_grad: float32 [2, 4096, 1536], P(None, 'seq', 'head')
- mix_gain_grad: float32 [1536], P('head')
- input_proj_grad: float32 [2, 1536, 3072], P(None, 'seq', 'head')
- state_proj_grad: float32 [1536, 256], P('seq')
- step_proj_grad: float32 [1536, 48], P('seq', 'head')
- conv_inner_grad: float32 [4, 3072], P(None, 'head')
- conv_state_grad: float32 [4, 256], replicated
- inner_bias_grad: float32 [3072], P('head')
- state_bias_grad: float32 [256], replicated
- step_bias_grad: float32 [48], P('head')
- decay_rate_grad: float32 [48], P('head')
- skip_gain_grad: float32 [48], P('head')
- gate_gain_grad: float32 [3072], P('head')
- output_proj_grad: float32 [3072, 1536], P('head', 'seq')
- moe_gain_grad: float32 [1536], P('head')
- router_grad: float32 [1536, 32], P('seq')
- expert_up_grad: float32 [32, 1536, 1024], P('head', 'seq')
- expert_down_grad: float32 [32, 512, 1536], P('head', None, 'seq')
- shared_up_grad: float32 [1536, 2, 1024], P('seq', None, 'head')
- shared_down_grad: float32 [1024, 1536], P('head', 'seq')
The draws below stay inside these ranges and needn't reach their ends.
Inputs may be any that keep to these rules, and one draw needn't show every extreme that they name: The 4 lengths of a micro-batch sum to 4096, and the largest is 3840. Each row names each of the 4 sequences once; seq_order[m, k] is the sequence packed k-th in micro-batch m. `routes`: A token's 6 experts are distinct. In each aligned block of 512 rows of a micro-batch (the rows of one index of seq) no expert is named by more than 192 rows, a bound that some block reaches.
All inputs are finite; a program needn't handle non-finite values.
Results may differ from the reference program's by a relative error of at most 0.03.
Values may be sent and summed in bfloat16 or wider, within the bound.
A program may use at most 320 MiB of HBM per device.

```python
import math
from functools import partial
import jax
import jax.numpy as jnp
import numpy as np
from jax import lax

D = 1536
HEADS = 48
HEAD_DIM = 64
STATE = 128
CONV = 4
TOPK = 6
EFF = 512
SFF = 1024
TOK_MB = 512
MB = 2
NSEQ = 4
GROUP = 256
EXPERTS = 32
INNER = 3072
PACKED = 4096
LONGEST = 3840
CAP = 192
N_SEQ = 8


def drawn_draw(key, shape, scale, bound):
    return jnp.clip(jax.random.normal(key, shape, jnp.float32) * scale, -bound * scale, bound * scale)


def draw_hidden(key, part):
    return drawn_draw(jax.random.fold_in(key, 1), (MB, PACKED, D), 1.0, 6.0).astype(jnp.bfloat16)


def draw_output_grad(key, part):
    return drawn_draw(jax.random.fold_in(key, 2), (MB, PACKED, D), 1.0, 6.0).astype(jnp.bfloat16)


def draw_input_proj(key, part):
    return drawn_draw(jax.random.fold_in(key, 3), (2, D, INNER), D ** (-0.5), 6.0).astype(jnp.bfloat16)


def draw_state_proj(key, part):
    return drawn_draw(jax.random.fold_in(key, 4), (D, 2 * STATE), D ** (-0.5), 6.0).astype(jnp.bfloat16)


def draw_step_proj(key, part):
    return drawn_draw(jax.random.fold_in(key, 5), (D, HEADS), D ** (-0.5), 6.0).astype(jnp.bfloat16)


def draw_conv_inner(key, part):
    return drawn_draw(jax.random.fold_in(key, 6), (CONV, INNER), CONV ** (-0.5), 6.0)


def draw_conv_state(key, part):
    return drawn_draw(jax.random.fold_in(key, 7), (CONV, 2 * STATE), CONV ** (-0.5), 6.0)


def draw_inner_bias(key, part):
    return drawn_draw(jax.random.fold_in(key, 8), (INNER,), 0.3, 4.0)


def draw_state_bias(key, part):
    return drawn_draw(jax.random.fold_in(key, 9), (2 * STATE,), 0.3, 4.0)


def draw_output_proj(key, part):
    return drawn_draw(jax.random.fold_in(key, 10), (INNER, D), INNER ** (-0.5), 6.0).astype(jnp.bfloat16)


def draw_router(key, part):
    return drawn_draw(jax.random.fold_in(key, 11), (D, EXPERTS), (4 * D) ** (-0.5), 6.0).astype(jnp.bfloat16)


def draw_expert_up(key, part):
    return drawn_draw(jax.random.fold_in(key, 12), (EXPERTS, D, 2 * EFF), D ** (-0.5), 6.0).astype(jnp.bfloat16)


def draw_expert_down(key, part):
    return drawn_draw(jax.random.fold_in(key, 13), (EXPERTS, EFF, D), (EFF // 4) ** (-0.5), 6.0).astype(jnp.bfloat16)


def draw_shared_up(key, part):
    return drawn_draw(jax.random.fold_in(key, 14), (D, 2, SFF), D ** (-0.5), 6.0).astype(jnp.bfloat16)


def draw_shared_down(key, part):
    return drawn_draw(jax.random.fold_in(key, 15), (SFF, D), SFF ** (-0.5), 6.0).astype(jnp.bfloat16)


def level_of(own_key, shape, cuts, smallest, high):
    def one(dim, blocks):
        heights = jax.random.uniform(jax.random.fold_in(jax.random.fold_in(own_key, 6), dim), (blocks,), jnp.float32, smallest / len(cuts), high / len(cuts))
        return jnp.repeat(jnp.exp(heights), shape[dim] // blocks).reshape((-1,) + (1,) * (len(shape) - dim - 1))

    gain = one(*cuts[0])
    for cut in cuts[1:]:
        gain = gain * one(*cut)
    return gain


def length_profile(amount, total, most, skew):
    portions = [(1 << 20) // math.isqrt(grade ** skew) + 1 for grade in range(2, amount + 1)]
    spare, holding = total - most - (amount - 1), [1] * (amount - 1)
    while spare > 0:
        movable = [i for i in range(amount - 1) if holding[i] < most]
        whole, left = sum([portions[i] for i in movable]), spare
        for i in movable:
            addition = min(most - holding[i], max(1, left * portions[i] // whole), spare)
            holding[i] = holding[i] + addition
            spare = spare - addition
    return np.array([most] + holding)


def uneven_parts(stream_key, amount, total, most, skew):
    if amount == 2:
        one = jax.random.randint(stream_key, (), max(1, total - most), min(most, total - 1) + 1)
        return jnp.stack([one, total - one])
    sizes = jnp.asarray(length_profile(amount, total, most, skew), jnp.int32)
    pairs = (amount - 1) // 2
    source_of, sink = sizes[1:1 + 2 * pairs:2], sizes[2:2 + 2 * pairs:2]
    margin = jnp.minimum(source_of - 1, most - sink)
    shifted = jax.random.randint(jax.random.fold_in(stream_key, 1), (pairs,), 0, 1 << 20) % (margin + 1)
    sizes = sizes.at[1:1 + 2 * pairs:2].set(source_of - shifted).at[2:2 + 2 * pairs:2].set(sink + shifted)
    return sizes[jax.random.permutation(jax.random.fold_in(stream_key, 2), amount)]


def assign_block(key, own, number, rows, number_of, top, reach, lean):
    sequence = jax.random.permutation(key, number_of)
    crowded, common = load_shares(number_of, rows * top, reach, lean, True), load_shares(number_of, rows * top, reach, lean, False)
    places = jnp.arange(number_of)

    def named(tallies, offset_by):
        used = int((tallies > 0).sum())
        fixed = max(1, used // 4)
        shifted = fixed + (places - fixed + offset_by * (used - fixed)) % max(1, number_of - fixed)
        return jnp.zeros((number_of,), jnp.int32).at[sequence[jnp.where(places < fixed, places, shifted)]].set(jnp.asarray(tallies, jnp.int32))

    tallies = jnp.where(number % 4 == 0, named(crowded, number // 4), named(common, number - number // 4 - 1))
    mixed = jax.random.permutation(jax.random.fold_in(own, 3), number_of)
    donor, taker = mixed[0:number_of // 2 * 2:2], mixed[1:number_of // 2 * 2:2]
    margin = jnp.minimum(tallies[donor] - 1, reach - tallies[taker]) // 2
    margin = jnp.where((donor == sequence[0]) | (taker == sequence[0]) | (tallies[taker] == 0), 0, jnp.maximum(margin, 0))
    shifted = jax.random.randint(jax.random.fold_in(own, 4), (number_of // 2,), 0, 1 << 20) % (margin + 1)
    tallies = tallies.at[donor].add(-shifted).at[taker].add(shifted)
    labels = jnp.searchsorted(jnp.cumsum(tallies), jnp.arange(rows * top), side="right").astype(jnp.int32)
    listing = labels.reshape(top, rows).T
    listing = listing[jax.random.permutation(jax.random.fold_in(own, 1), rows)]
    offset_by = jax.random.randint(jax.random.fold_in(own, 2), (rows, 1), 0, top)
    return jnp.take_along_axis(listing, (jnp.arange(top)[None, :] + offset_by) % top, axis=1)


def load_shares(count, total, reach, skew, full):
    portions = [(1 << 20) // math.isqrt(standing ** skew) + 1 for standing in range(1, count + 1)]
    largest = reach if full else min(reach, max(-(-total // count), total * portions[0] // sum(portions)))
    least = 1 if total - largest >= count - 1 else 0
    given, spare = [largest] + [least] * (count - 1), total - largest - least * (count - 1)
    while spare > 0:
        free = [i for i in range(1, count) if given[i] < largest] or [i for i in range(1, count) if given[i] < reach]
        whole, remaining = sum([portions[i] for i in free]), spare
        for i in free:
            extra = min(reach - given[i], max(1, remaining * portions[i] // whole), spare)
            given[i] = given[i] + extra
            spare = spare - extra
    return np.array(given)


def setup_inputs(seed: int = 0) -> dict:
    key_list = jax.random.split(jax.random.key(seed), 25)
    hidden = draw_hidden(jax.random.fold_in(key_list[24], 71), 0)
    output_grad = draw_output_grad(jax.random.fold_in(key_list[24], 71), 0)
    lengths = jax.vmap(lambda own: uneven_parts(own, NSEQ, PACKED, LONGEST, 1))(jax.random.split(key_list[2], MB)).reshape((MB, NSEQ)).astype(jnp.int32)
    seq_order = jax.vmap(lambda own: jax.random.permutation(own, NSEQ))(jax.random.split(key_list[3], MB)).reshape((MB, NSEQ)).astype(jnp.int32)
    routes_keys = jax.random.split(jax.random.fold_in(key_list[4], 1), MB * PACKED // TOK_MB)
    routes_turns = jax.random.permutation(jax.random.fold_in(key_list[4], 3), MB * PACKED // TOK_MB)
    routes = jax.vmap(lambda own, number: assign_block(jax.random.fold_in(key_list[4], 2), own, number, TOK_MB, EXPERTS, TOPK, CAP, 2))(routes_keys, routes_turns).reshape((MB, PACKED, TOPK))
    mix_gain = jnp.clip(1.0 + 0.1 * jax.random.normal(key_list[5], (D,), jnp.float32), 0.5, 1.5)
    input_proj = draw_input_proj(jax.random.fold_in(key_list[24], 71), 0)
    state_proj = draw_state_proj(jax.random.fold_in(key_list[24], 71), 0)
    step_proj = draw_step_proj(jax.random.fold_in(key_list[24], 71), 0)
    conv_inner = draw_conv_inner(jax.random.fold_in(key_list[24], 71), 0)
    conv_state = draw_conv_state(jax.random.fold_in(key_list[24], 71), 0)
    inner_bias = draw_inner_bias(jax.random.fold_in(key_list[24], 71), 0)
    state_bias = draw_state_bias(jax.random.fold_in(key_list[24], 71), 0)
    step_bias = jnp.clip(-2.0 + 2.5 * jax.random.uniform(key_list[13], (HEADS,), jnp.float32) ** level_of(key_list[13], (HEADS,), ((0, 4),), -0.2, 0.2), -2.0, 0.5)
    decay_rate = jnp.clip(jnp.exp(math.log(0.08) - 7.178332 * jax.random.uniform(key_list[14], (HEADS,), jnp.float32) ** level_of(key_list[14], (HEADS,), ((0, 4),), -0.2, 0.2)), 6.103515625e-05, 0.08)
    skip_gain = jnp.clip(0.5 + 1.0 * jax.random.uniform(key_list[15], (HEADS,), jnp.float32) ** level_of(key_list[15], (HEADS,), ((0, 4),), -0.2, 0.2), 0.5, 1.5)
    gate_gain = jnp.clip(1.0 + 0.1 * jax.random.normal(key_list[16], (INNER,), jnp.float32), 0.5, 1.5)
    output_proj = draw_output_proj(jax.random.fold_in(key_list[24], 71), 0)
    moe_gain = jnp.clip(1.0 + 0.1 * jax.random.normal(key_list[18], (D,), jnp.float32), 0.5, 1.5)
    router = draw_router(jax.random.fold_in(key_list[24], 71), 0)
    expert_up = draw_expert_up(jax.random.fold_in(key_list[24], 71), 0)
    expert_down = draw_expert_down(jax.random.fold_in(key_list[24], 71), 0)
    shared_up = draw_shared_up(jax.random.fold_in(key_list[24], 71), 0)
    shared_down = draw_shared_down(jax.random.fold_in(key_list[24], 71), 0)
    return dict(hidden=hidden, output_grad=output_grad, lengths=lengths, seq_order=seq_order, routes=routes, mix_gain=mix_gain, input_proj=input_proj, state_proj=state_proj, step_proj=step_proj, conv_inner=conv_inner, conv_state=conv_state, inner_bias=inner_bias, state_bias=state_bias, step_bias=step_bias, decay_rate=decay_rate, skip_gain=skip_gain, gate_gain=gate_gain, output_proj=output_proj, moe_gain=moe_gain, router=router, expert_up=expert_up, expert_down=expert_down, shared_up=shared_up, shared_down=shared_down)


EPSILON = 1e-05
HIGHEST = lax.Precision.HIGHEST

@jax.custom_vjp
def low(v):
    return lax.optimization_barrier(v.astype(jnp.bfloat16)).astype(jnp.float32)

@jax.custom_vjp
def low_back(v):
    return v

def low_keep(v):
    return (low(v), None)

def low_pass(kept, grad):
    return (grad,)

def back_keep(v):
    return (v, None)

def back_low(kept, grad):
    return (low(grad),)
low.defvjp(low_keep, low_pass)
low_back.defvjp(back_keep, back_low)

def matmul(left_side, right_side):
    return jnp.dot(left_side, right_side, precision=HIGHEST, preferred_element_type=jnp.float32)

def squash_norm(values, norm_gain):
    norm_scale = lax.rsqrt(lax.optimization_barrier(jnp.mean(values * values, axis=-1, keepdims=True)) + EPSILON)
    return values * norm_scale * norm_gain

def segment_numbers(length_row, order_row, positions):
    seq_count = length_row.shape[0]
    seq_index = jnp.arange(seq_count, dtype=jnp.int32)
    picked = (order_row[:, None] == seq_index[None, :]).astype(jnp.int32)
    placed = lax.optimization_barrier(jnp.sum(picked * length_row[None, :], axis=1))
    earlier = (seq_index[:, None] > seq_index[None, :]).astype(jnp.int32)
    begins = lax.optimization_barrier(jnp.sum(earlier * placed[None, :], axis=1))
    return lax.optimization_barrier(jnp.sum((begins[None, :] <= positions[:, None]).astype(jnp.int32), axis=1)).astype(jnp.int32)

def conv_extended(padded, conv_weight, conv_offset, segment_padded):
    conv_taps = conv_weight.shape[0]
    length = padded.shape[0] - (conv_taps - 1)
    current = segment_padded[conv_taps - 1:]
    summed = conv_offset + padded[conv_taps - 1:] * conv_weight[0]
    for offset in range(1, conv_taps):
        begin_at = conv_taps - 1 - offset
        keep_mask = (segment_padded[begin_at:begin_at + length] == current).astype(jnp.float32)
        summed = summed + padded[begin_at:begin_at + length] * conv_weight[offset] * keep_mask[:, None]
    return summed

def ssd_block(carry_state, block_in):
    signal, write_keys, read_keys, step_sizes, log_decay, segments, segment_before = block_in
    length = log_decay.shape[0]
    row_index = jnp.arange(length, dtype=jnp.int32)
    lower_ones = (row_index[:, None] >= row_index[None, :]).astype(jnp.float32)
    running = jnp.einsum('ij,jh->ih', lower_ones, log_decay, precision=HIGHEST)
    within = (row_index[:, None] >= row_index[None, :]) & (segments[:, None] == segments[None, :])
    spread = running[:, None, :] - running[None, :, :]
    decays = jnp.where(within[:, :, None], jnp.exp(jnp.where(within[:, :, None], spread, 0.0)), 0.0)
    scores = jnp.einsum('in,jn->ij', read_keys, write_keys, precision=HIGHEST)
    mixing = decays * scores[:, :, None] * step_sizes[None, :, :]
    local_out = jnp.einsum('ijh,jhp->ihp', mixing, signal, precision=HIGHEST)
    carried = jnp.where((segments == segment_before)[:, None], jnp.exp(running), 0.0)
    from_state = jnp.einsum('in,hpn->ihp', read_keys, carry_state, precision=HIGHEST) * carried[:, :, None]
    last_keep = jnp.where((segments == segments[-1])[:, None], jnp.exp(running[-1][None, :] - running), 0.0) * step_sizes
    through = jnp.where(segments[-1] == segment_before, jnp.exp(running[-1]), 0.0)
    new_state = carry_state * through[:, None, None] + jnp.einsum('jh,jhp,jn->hpn', last_keep, signal, write_keys, precision=HIGHEST)
    return (new_state, local_out + from_state)

def slot_table(route_rows, first_expert, expert_count, capacity):
    pair_count = route_rows.shape[0] * route_rows.shape[1]
    flat_local = route_rows.reshape(-1) - first_expert
    matches = (flat_local[:, None] == jnp.arange(expert_count, dtype=jnp.int32)[None, :]).astype(jnp.int32)
    slot_ranks = lax.optimization_barrier(jnp.sum((jnp.cumsum(matches, axis=0) - 1) * matches, axis=1))
    inside = (flat_local >= 0) & (flat_local < expert_count)
    target = jnp.where(inside, flat_local * capacity + slot_ranks, expert_count * capacity).astype(jnp.int32)
    empty_table = jnp.full((expert_count * capacity,), pair_count, jnp.int32)
    return empty_table.at[target].set(jnp.arange(pair_count, dtype=jnp.int32), mode='drop')

def block_forward(resid_in, params, segments, route_rows):
    mix_gain, input_proj, state_proj, step_proj, conv_inner, conv_state, inner_bias, state_bias, step_bias, decay_rate, skip_gain, gate_gain, output_proj, moe_gain, router, expert_up, expert_down, shared_up, shared_down = params
    length = resid_in.shape[0]
    normed = low(squash_norm(resid_in, mix_gain))
    gate_pre = low_back(matmul(normed, input_proj[0]))
    inner_pre = low_back(matmul(normed, input_proj[1]))
    state_pre = low_back(matmul(normed, state_proj))
    step_raw = low_back(matmul(normed, step_proj))
    conv_in = jnp.concatenate([inner_pre, state_pre], axis=1)
    padded = jnp.concatenate([jnp.zeros((CONV - 1, conv_in.shape[1]), jnp.float32), conv_in], axis=0)
    segment_padded = jnp.concatenate([jnp.full((CONV - 1,), -1, jnp.int32), segments])
    conv_weight = jnp.concatenate([conv_inner, conv_state], axis=1)
    conv_offset = jnp.concatenate([inner_bias, state_bias])
    activated = jax.nn.silu(conv_extended(padded, conv_weight, conv_offset, segment_padded))
    signal = activated[:, :INNER].reshape(length, HEADS, HEAD_DIM)
    write_keys = activated[:, INNER:INNER + STATE]
    read_keys = activated[:, INNER + STATE:]
    step_sizes = jax.nn.softplus(step_raw + step_bias)
    log_decay = -step_sizes * decay_rate
    blocks = length // GROUP
    before = jnp.concatenate([jnp.zeros((1,), jnp.int32), segments[:-1]]).reshape(blocks, GROUP)[:, 0]
    block_parts = (signal.reshape(blocks, GROUP, HEADS, HEAD_DIM), write_keys.reshape(blocks, GROUP, STATE), read_keys.reshape(blocks, GROUP, STATE), step_sizes.reshape(blocks, GROUP, HEADS), log_decay.reshape(blocks, GROUP, HEADS), segments.reshape(blocks, GROUP), before)
    unused, mixed_out = lax.scan(jax.checkpoint(ssd_block), jnp.zeros((HEADS, HEAD_DIM, STATE), jnp.float32), block_parts)
    mixed_out = mixed_out.reshape(length, HEADS, HEAD_DIM) + skip_gain[None, :, None] * signal
    gated_rows = mixed_out.reshape(length, INNER) * jax.nn.silu(gate_pre)
    gate_normed = low(squash_norm(gated_rows, gate_gain))
    resid_mid = resid_in + low_back(matmul(gate_normed, output_proj))
    moe_normed = low(squash_norm(resid_mid, moe_gain))
    logits = low_back(matmul(moe_normed, router))
    gate_weights = jax.nn.softmax(jnp.take_along_axis(logits, route_rows, axis=1), axis=1)
    tables = jax.vmap(partial(slot_table, first_expert=0, expert_count=EXPERTS, capacity=CAP))(route_rows.reshape(N_SEQ, TOK_MB, TOPK))
    offsets = (jnp.arange(N_SEQ, dtype=jnp.int32) * (TOK_MB * TOPK))[:, None]
    slot_pairs = jnp.where(tables < TOK_MB * TOPK, tables + offsets, -1)
    slot_pairs = slot_pairs.reshape(N_SEQ, EXPERTS, CAP).transpose(1, 0, 2).reshape(EXPERTS, N_SEQ * CAP)
    gate_flat = gate_weights.reshape(-1)

    def expert_pass(moe_sum, member):
        weight_up, weight_down, pair_ids = member
        filled = pair_ids >= 0
        safe_pair = jnp.where(filled, pair_ids, 0)
        token_ids = safe_pair // TOPK
        slot_rows = jnp.take(moe_normed, token_ids, axis=0)
        gate_up = low_back(matmul(slot_rows, weight_up))
        hidden_act = low(jax.nn.silu(gate_up[:, :EFF]) * gate_up[:, EFF:])
        expert_out = low_back(matmul(hidden_act, weight_down))
        slot_gate = jnp.where(filled, jnp.take(gate_flat, safe_pair), 0.0)
        return (moe_sum.at[token_ids].add(expert_out * slot_gate[:, None]), None)
    moe_sum, unused = lax.scan(jax.checkpoint(expert_pass), jnp.zeros((length, D), jnp.float32), (expert_up, expert_down, slot_pairs))
    shared_both = low_back(matmul(moe_normed, shared_up.reshape(D, 2 * SFF)))
    shared_act = low(jax.nn.silu(shared_both[:, :SFF]) * shared_both[:, SFF:])
    ffn_out = low_back(moe_sum + matmul(shared_act, shared_down))
    return resid_mid + ffn_out

def reference(hidden, output_grad, lengths, seq_order, routes, mix_gain, input_proj, state_proj, step_proj, conv_inner, conv_state, inner_bias, state_bias, step_bias, decay_rate, skip_gain, gate_gain, output_proj, moe_gain, router, expert_up, expert_down, shared_up, shared_down):
    params = tuple((member.astype(jnp.float32) for member in (mix_gain, input_proj, state_proj, step_proj, conv_inner, conv_state, inner_bias, state_bias, step_bias, decay_rate, skip_gain, gate_gain, output_proj, moe_gain, router, expert_up, expert_down, shared_up, shared_down)))
    positions = jnp.arange(PACKED, dtype=jnp.int32)
    outputs = []
    input_grads = []
    totals = None
    for micro_index in range(MB):
        segments = segment_numbers(lengths[micro_index], seq_order[micro_index], positions)
        forward = partial(block_forward, segments=segments, route_rows=routes[micro_index])
        result, pullback = jax.vjp(forward, hidden[micro_index].astype(jnp.float32), params)
        grad_in, grad_params = pullback(output_grad[micro_index].astype(jnp.float32))
        outputs.append(result.astype(jnp.bfloat16))
        input_grads.append(grad_in)
        totals = grad_params if totals is None else jax.tree.map(jnp.add, totals, grad_params)
    return (jnp.stack(outputs), jnp.stack(input_grads), totals[0], totals[1], totals[2], totals[3], totals[4], totals[5], totals[6], totals[7], totals[8], totals[9], totals[10], totals[11], totals[12], totals[13], totals[14], totals[15], totals[16], totals[17], totals[18])
```

```python
import functools
from functools import partial

import jax
import jax.numpy as jnp
from jax import lax
from jax.experimental import pallas as pl
from jax.experimental.pallas import tpu as pltpu
from jax.sharding import PartitionSpec as P

D = 1536
HEAD_DIM = 64
STATE = 128
CONV = 4
TOPK = 6
EFF = 512
INNER = 3072
MEMBERS = 4
EDGE = 8
CHUNK = 128

EPSILON = 1e-05
HIGHEST = lax.Precision.HIGHEST
BF = jnp.bfloat16
F32 = jnp.float32
MESH = pl.DeviceIdType.MESH

def flips(bits):
    found = [(0, 0)]
    for axis, mask in bits:
        found += [(a ^ (mask * (axis == "seq")), b ^ (mask * (axis == "head"))) for a, b in found]
    return found


def joined(left, right):
    return (left[0] ^ right[0], left[1] ^ right[1])


def flip_of(bit):
    axis, mask = bit
    return (mask, 0) if axis == "seq" else (0, mask)


def toggled(place, mask):
    found, bit = place, 1
    while bit <= mask:
        if mask & bit:
            found = found + bit * (1 - 2 * lax.rem(lax.div(place, bit), 2))
        bit = 2 * bit
    return found


def across(me, masks):
    return (toggled(me[0], masks[0]), toggled(me[1], masks[1]))


def greet(jobs, me):
    bits = sorted({bit for job in jobs for bit in job.parts[0][2]})
    barrier = pltpu.get_barrier_semaphore()
    for bit in bits:
        pl.semaphore_signal(
            barrier, inc=1, device_id=across(me, flip_of(bit)), device_id_type=MESH
        )
    pl.semaphore_wait(barrier, len(bits))


class Job:
    def __init__(self, parts, slot_of, wide=False):
        self.parts, self.slot_of, self.wide = parts, slot_of, wide
        self.depth = len(parts[0][2])
        self.count = 1 << self.depth

    def view(self, ref, place, rows, columns, width):
        slot = self.slot_of(*place)
        if self.wide:
            at = columns[0] + slot * width
            if columns[0] % 128 == 0 and width % 128 == 0:
                at = pl.multiple_of(at, 128)
            return ref.at[:, pl.ds(*rows), pl.ds(at, columns[1])]
        return ref.at[:, slot, pl.ds(*rows), pl.ds(*columns)]

    def whole_shape(self, shape):
        lead, rows, columns = shape
        if self.wide:
            return (lead, rows, self.count * columns)
        return (lead, self.count, rows, columns)


def gather_kernel(jobs, *refs):
    me = (lax.axis_index("seq"), lax.axis_index("head"))
    number = len(jobs)
    x_refs, o_refs, sems = refs[:number], refs[number : 2 * number], refs[2 * number :]
    greet(jobs, me)
    owns, copies, waited = [], {}, set()
    for step in range(max(job.depth for job in jobs)):
        for j, job in enumerate(jobs):
            if step >= job.depth:
                continue
            send_sem, recv_sem, own_sem = sems[3 * j : 3 * j + 3]
            x_ref, o_ref = x_refs[j], o_refs[j]
            width = x_ref.shape[2]
            for p, (rows, columns, order) in enumerate(job.parts):
                other = flip_of(order[step])
                for place, held in enumerate(flips(order[:step])):
                    if place and (j, p, place) not in waited:
                        copies[j, p, place].wait_recv()
                        waited.add((j, p, place))
                    dst = job.view(o_ref, across(me, held), rows, columns, width)
                    src = dst if place else x_ref.at[:, pl.ds(*rows), pl.ds(*columns)]
                    arriving = place + (1 << step)
                    copy = pltpu.make_async_remote_copy(
                        src_ref=src,
                        dst_ref=dst,
                        send_sem=send_sem.at[p, arriving],
                        recv_sem=recv_sem.at[p, arriving],
                        device_id=across(me, other),
                        device_id_type=MESH,
                    )
                    copy.start()
                    copies[j, p, arriving] = copy
            if step == 0:
                whole = ((0, x_ref.shape[1]), (0, width))
                own = pltpu.make_async_copy(x_ref, job.view(o_ref, me, *whole, width), own_sem)
                own.start()
                owns.append(own)
    for key, copy in copies.items():
        if key not in waited:
            copy.wait_recv()
    for copy in copies.values():
        copy.wait_send()
    for own in owns:
        own.wait()


def cube_gather(jobs, arrays, collective_id, weight=100 << 20):
    anywhere = pl.BlockSpec(memory_space=pl.ANY)
    scratch = []
    for job in jobs:
        for shape in ((len(job.parts), job.count),) * 2 + ((),):
            scratch.append(pltpu.SemaphoreType.DMA(shape) if shape else pltpu.SemaphoreType.DMA)
    return pl.pallas_call(
        functools.partial(gather_kernel, jobs),
        out_shape=tuple(
            jax.ShapeDtypeStruct(job.whole_shape(x.shape), x.dtype)
            for job, x in zip(jobs, arrays, strict=True)
        ),
        in_specs=[anywhere] * len(jobs),
        out_specs=(anywhere,) * len(jobs),
        scratch_shapes=scratch,
        compiler_params=pltpu.CompilerParams(collective_id=collective_id, has_side_effects=True),
        cost_estimate=pl.CostEstimate(flops=0, bytes_accessed=weight, transcendentals=0),
    )(*arrays)


def reduce_kernel(jobs, *refs):
    me = (lax.axis_index("seq"), lax.axis_index("head"))
    number = len(jobs)
    x_refs, o_refs, scratch = refs[:number], refs[number : 2 * number], refs[2 * number :]
    greet(jobs, me)
    loads, flying = {}, {}

    def base(job, step):
        return sum(1 << (job.depth - 1 - i) for i in range(step))

    def send(j, p, step, place):
        job, x_ref = jobs[j], x_refs[j]
        kept, stage, send_sem, recv_sem, own_sem = scratch[5 * j : 5 * j + 5]
        rows, columns, order = job.parts[p]
        other = flip_of(order[step])
        gone = joined(flips(order[step + 1 :])[place], other)
        if step == 0:
            src = job.view(x_ref, across(me, gone), rows, columns, stage.shape[3])
        else:
            source = base(job, step - 1) + flips(order[step:]).index(gone)
            src = stage.at[source, :, pl.ds(*rows), pl.ds(*columns)]
        target = base(job, step) + place
        copy = pltpu.make_async_remote_copy(
            src_ref=src,
            dst_ref=stage.at[target, :, pl.ds(*rows), pl.ds(*columns)],
            send_sem=send_sem.at[p, target],
            recv_sem=recv_sem.at[p, target],
            device_id=across(me, other),
            device_id_type=MESH,
        )
        copy.start()
        flying[j, p, step, place] = copy

    def add(j, p, step, place):
        job, o_ref = jobs[j], o_refs[j]
        kept, stage = scratch[5 * j : 5 * j + 2]
        rows, columns, order = job.parts[p]
        tile = 16 if rows[1] % 16 == 0 else 8
        target = base(job, step) + place
        left = flips(order[step + 1 :])[place]
        source = base(job, step - 1) + flips(order[step:]).index(left) if step else 0

        def one(i, carry):
            here = pl.ds(pl.multiple_of(rows[0] + i * tile, tile), tile)
            for m in range(stage.shape[1]):
                got = stage[target, m, here, pl.ds(*columns)].astype(F32)
                if step == 0:
                    mine = kept[place, m, here, pl.ds(*columns)]
                else:
                    mine = stage[source, m, here, pl.ds(*columns)]
                total = got + mine.astype(F32)
                if step + 1 == job.depth:
                    o_ref[m, here, pl.ds(*columns)] = total
                else:
                    stage[target, m, here, pl.ds(*columns)] = total.astype(stage.dtype)
            return carry

        lax.fori_loop(0, rows[1] // tile, one, 0)

    def sequence(job, p, step):
        order = job.parts[p][2]
        found = flips(order[step + 1 :])
        if step + 1 == job.depth:
            return [0]
        other, later = flip_of(order[step + 1]), flips(order[step + 2 :])
        return [found.index(joined(left, other)) for left in later] + [
            found.index(left) for left in later
        ]

    for j, job in enumerate(jobs):
        for p in range(len(job.parts)):
            for place in sequence(job, p, 0):
                send(j, p, 0, place)
    for j, job in enumerate(jobs):
        kept, stage, send_sem, recv_sem, own_sem = scratch[5 * j : 5 * j + 5]
        for p, (rows, columns, order) in enumerate(job.parts):
            for place, held in enumerate(flips(order[1:])):
                load = pltpu.make_async_copy(
                    job.view(x_refs[j], across(me, held), rows, columns, stage.shape[3]),
                    kept.at[place, :, pl.ds(*rows), pl.ds(*columns)],
                    own_sem.at[p, place],
                )
                load.start()
                loads[j, p, place] = load
    for step in range(max(job.depth for job in jobs)):
        for j, job in enumerate(jobs):
            if step >= job.depth:
                continue
            for p, (rows, columns, order) in enumerate(job.parts):
                places = sequence(job, p, step)
                for at, place in enumerate(places):
                    if step == 0:
                        loads[j, p, place].wait()
                    flying[j, p, step, place].wait_recv()
                    add(j, p, step, place)
                    if step + 1 < job.depth and at < len(places) // 2:
                        send(j, p, step + 1, at)
    for copy in flying.values():
        copy.wait_send()


def cube_reduce(jobs, arrays, collective_id, weight=100 << 20):
    out_shape, scratch = [], []
    for job, x in zip(jobs, arrays, strict=True):
        if job.wide:
            lead, rows, columns = x.shape[0], x.shape[1], x.shape[2] // job.count
        else:
            lead, _, rows, columns = x.shape
        out_shape.append(jax.ShapeDtypeStruct((lead, rows, columns), F32))
        scratch += [
            pltpu.VMEM((job.count // 2, lead, rows, columns), x.dtype),
            pltpu.VMEM((job.count - 1, lead, rows, columns), x.dtype),
            pltpu.SemaphoreType.DMA((len(job.parts), job.count - 1)),
            pltpu.SemaphoreType.DMA((len(job.parts), job.count - 1)),
            pltpu.SemaphoreType.DMA((len(job.parts), job.count // 2)),
        ]
    return pl.pallas_call(
        functools.partial(reduce_kernel, jobs),
        out_shape=tuple(out_shape),
        in_specs=[pl.BlockSpec(memory_space=pl.ANY)] * len(jobs),
        out_specs=(pl.BlockSpec(memory_space=pltpu.VMEM),) * len(jobs),
        scratch_shapes=scratch,
        compiler_params=pltpu.CompilerParams(
            collective_id=collective_id, has_side_effects=True, vmem_limit_bytes=52 << 20
        ),
        cost_estimate=pl.CostEstimate(flops=0, bytes_accessed=weight, transcendentals=0),
    )(*arrays)


def bits_in(axis, size):
    return [(axis, 1 << i) for i in range(size.bit_length() - 1)]


def thirds(rows, columns):
    if columns % 384:
        return [((0, rows), (0, columns))]
    third = columns // 3
    return [((0, rows), (i * third, third)) for i in range(3)]


def slot_in_head(s, h):
    return h


def slot_in_seq(s, h):
    return s


def slot_in_members(s, h):
    return lax.rem(s, MEMBERS)


def slot_in_group(s, h):
    return lax.rem(s, MEMBERS) * lax.axis_size("head") + h


def group_job(rows, columns, way):
    core = ("head", 1)
    links = bits_in("head", lax.axis_size("head"))[1:] + bits_in("seq", MEMBERS)
    parts = []
    for i, (r, c) in enumerate(thirds(rows, columns)):
        turned = links[i:] + links[:i]
        parts.append((r, c, (turned + [core])[::way]))
    return Job(parts, slot_in_group)


def head_job(rows, columns, way, wide=False):
    bits = bits_in("head", lax.axis_size("head"))
    order = (bits[1:] + bits[:1])[::way]
    return Job([(r, c, order) for r, c in thirds(rows, columns)], slot_in_head, wide)


def seq_job(rows, columns, way):
    bits = bits_in("seq", lax.axis_size("seq"))
    cut = rows * 5 // 6 // 16 * 16
    parts = [
        ((0, cut), (0, columns), bits[::-1][::way]),
        ((cut, rows - cut), (0, columns), (bits[:1] + bits[:0:-1])[::way]),
    ]
    return Job(parts, slot_in_seq)


def members_job(rows, columns):
    return Job([((0, rows), (0, columns), bits_in("seq", MEMBERS))], slot_in_members)


RUN, STEP, SEG = 0, 2, 4


def dot(a, b, dims):
    return lax.dot_general(
        a.astype(BF), b.astype(BF), (dims, ((), ())), preferred_element_type=F32
    )


def split_low(a):
    high = a.astype(BF)
    return high, (a - high.astype(F32)).astype(BF)


def dot_fine(a, b, dims):
    (a_high, a_low), (b_high, b_low) = split_low(a), split_low(b)
    return dot(a_high, b_high, dims) + (dot(a_high, b_low, dims) + dot(a_low, b_high, dims))


NN = ((1,), (0,))
NT = ((1,), (1,))
TN = ((0,), (0,))


def chunk_parts(cols_ref, rows_ref, begin):
    here = pl.ds(begin, CHUNK)
    cols, rows = cols_ref[0, 0, here, :], rows_ref[0, 0, :, here]
    last = slice(CHUNK - 1, CHUNK)
    seg_c, seg_r, seg_end = cols[:, SEG : SEG + 1], rows[SEG : SEG + 1], cols[last, SEG : SEG + 1]
    if begin:
        before = cols_ref[0, 0, pl.ds(begin - 8, 8), :][7:8]
        seg_before, run_before = before[:, SEG : SEG + 1], [before[:, RUN + k : RUN + k + 1] for k in range(2)]
    else:
        seg_before, run_before = cols[:1, SEG + 1 : SEG + 2], [jnp.zeros((1, 1), F32)] * 2
    row = lax.broadcasted_iota(jnp.int32, (CHUNK, CHUNK), 0)
    column = lax.broadcasted_iota(jnp.int32, (CHUNK, CHUNK), 1)
    within = (row >= column) & (seg_c == seg_r)
    heads = []
    for k in range(2):
        run_c, run_r = cols[:, RUN + k : RUN + k + 1], rows[RUN + k : RUN + k + 1]
        run_end = run_c[CHUNK - 1 :]
        decay = jnp.where(within, jnp.exp(jnp.where(within, run_c - run_r, 0.0)), 0.0)
        enter = jnp.where(seg_c == seg_before, jnp.exp(run_c - run_before[k]), 0.0)
        leave = jnp.where(seg_c == seg_end, jnp.exp(run_end - run_c), 0.0)
        through = jnp.where(seg_end == seg_before, jnp.exp(run_end - run_before[k]), 0.0)
        heads.append((decay, enter, leave, through, cols[:, STEP + k : STEP + k + 1], rows[STEP + k : STEP + k + 1]))
    return heads


def of_pair(first, second, axis):
    shape = (first.shape[0], 2 * HEAD_DIM) if axis == 1 else (2 * HEAD_DIM, first.shape[1])
    return jnp.where(
        lax.broadcasted_iota(jnp.int32, shape, axis) < HEAD_DIM,
        jnp.broadcast_to(first, shape),
        jnp.broadcast_to(second, shape),
    )


def halves(value):
    low = lax.broadcasted_iota(jnp.int32, value.shape, 1) < HEAD_DIM
    return jnp.where(low, value, 0.0), jnp.where(low, 0.0, value)


def forward_kernel(x_ref, keys_ref, cols_ref, rows_ref, y_ref):
    state = jnp.zeros((2 * HEAD_DIM, STATE), F32)
    tokens = x_ref.shape[1]
    for begin in range(0, tokens, CHUNK):
        here = pl.ds(begin, CHUNK)
        x, write, read = x_ref[0, here, :], keys_ref[0, here, :STATE], keys_ref[0, here, STATE:]
        heads = chunk_parts(cols_ref, rows_ref, begin)
        scores = dot_fine(read, write, NT)
        split = halves(x)
        y = 0.0
        for k, (decay, enter, leave, through, step_c, step_r) in enumerate(heads):
            y = y + dot_fine(scores * decay * step_r, split[k], NN)
        if begin:
            y = y + of_pair(heads[0][1], heads[1][1], 1) * dot_fine(read, state, NT)
        y_ref[0, here, :] = y
        if begin + CHUNK < tokens:
            keep = of_pair(heads[0][2] * heads[0][4], heads[1][2] * heads[1][4], 1)
            state = of_pair(heads[0][3], heads[1][3], 0) * state + dot_fine(
                keep * x, write, TN
            )


def scan_forward(x, keys, cols, rows):
    micro, tokens, width = x.shape
    pairs = width // (2 * HEAD_DIM)
    wide = pl.BlockSpec((1, tokens, 2 * HEAD_DIM), lambda m, p: (m, 0, p))
    return pl.pallas_call(
        forward_kernel,
        grid=(micro, pairs),
        out_shape=jax.ShapeDtypeStruct((micro, tokens, width), F32),
        in_specs=[
            wide,
            pl.BlockSpec((1, tokens, 2 * STATE), lambda m, p: (m, 0, 0)),
            pl.BlockSpec((1, 1, tokens, 8), lambda m, p: (m, p, 0, 0)),
            pl.BlockSpec((1, 1, 8, tokens), lambda m, p: (m, p, 0, 0)),
        ],
        out_specs=wide,
        compiler_params=pltpu.CompilerParams(vmem_limit_bytes=32 << 20),
        cost_estimate=pl.CostEstimate(
            flops=micro * pairs * tokens * CHUNK * 2 * 700, bytes_accessed=micro * tokens * width * 12, transcendentals=0
        ),
    )(x, keys, cols, rows)


def backward_kernel(
    x_ref, keys_ref, cols_ref, rows_ref, dy_ref, state_ref, next_ref,
    dx_ref, dkeys_ref, dcols_ref, drows_ref, states
):
    tokens = x_ref.shape[1]
    chunks = tokens // CHUNK
    pair = pl.program_id(1)

    @pl.when(pair == 0)
    def _():
        dkeys_ref[...] = jnp.zeros_like(dkeys_ref)

    state = state_ref[0]
    for c in range(chunks):
        states[c] = state
        if c + 1 < chunks:
            here = pl.ds(c * CHUNK, CHUNK)
            heads = chunk_parts(cols_ref, rows_ref, c * CHUNK)
            keep = of_pair(heads[0][2] * heads[0][4], heads[1][2] * heads[1][4], 1)
            state = of_pair(heads[0][3], heads[1][3], 0) * state + dot_fine(
                keep * x_ref[0, here, :], keys_ref[0, here, :STATE], TN
            )
    later = next_ref[0]
    pending = [jnp.zeros((1, 1), F32)] * 2
    end_row = lax.broadcasted_iota(jnp.int32, (CHUNK, 1), 0) == CHUNK - 1
    lane8 = lax.broadcasted_iota(jnp.int32, (CHUNK, 8), 1)
    sub8 = lax.broadcasted_iota(jnp.int32, (8, CHUNK), 0)
    for c in reversed(range(chunks)):
        begin = c * CHUNK
        here = pl.ds(begin, CHUNK)
        x, write, read = x_ref[0, here, :], keys_ref[0, here, :STATE], keys_ref[0, here, STATE:]
        dy = dy_ref[0, here, :]
        state = states[c]
        heads = chunk_parts(cols_ref, rows_ref, begin)
        scores = dot_fine(read, write, NT)
        x_split, dy_split = halves(x), halves(dy)
        enter = of_pair(heads[0][1], heads[1][1], 1)
        leave = of_pair(heads[0][2], heads[1][2], 1)
        step = of_pair(heads[0][4], heads[1][4], 1)
        through = of_pair(heads[0][3], heads[1][3], 0)
        entered = enter * dy
        kept = leave * step * x
        from_later = dot_fine(write, later, NT)
        dx = leave * step * from_later
        dread = dot_fine(entered, state, NN)
        dwrite = dot_fine(kept, later, NN)
        weight_grad = halves(from_later * x)
        entry_grad = halves(entered * dot_fine(read, state, NT))
        kept_state = later * state * through
        dscores = 0.0
        dcols = jnp.zeros((CHUNK, 8), F32)
        drows = jnp.zeros((8, CHUNK), F32)
        for k, (decay, _, leave_k, through_k, step_c, step_r) in enumerate(heads):
            products = dot_fine(dy, x_split[k], NT)
            weighted = products * decay
            dx = dx + dot(scores * decay * step_r, dy_split[k], TN)
            dscores = dscores + weighted * step_r
            q = weighted * scores
            r = q * step_r
            dw = jnp.sum(weight_grad[k], axis=1, keepdims=True) * leave_k
            de = jnp.sum(entry_grad[k], axis=1, keepdims=True)
            drun = jnp.sum(r, axis=1, keepdims=True) + de - dw * step_c
            half = slice(k * HEAD_DIM, (k + 1) * HEAD_DIM)
            passed = jnp.sum(jnp.sum(kept_state[half], axis=1, keepdims=True), axis=0, keepdims=True)
            at_end = passed + jnp.sum(dw * step_c, axis=0, keepdims=True) + pending[k]
            pending[k] = -passed - jnp.sum(de, axis=0, keepdims=True)
            drun = drun + jnp.where(end_row, at_end, 0.0)
            dcols = dcols + jnp.where(lane8 == RUN + k, drun, 0.0) + jnp.where(lane8 == STEP + k, dw, 0.0)
            q_sum = jnp.sum(q, axis=0, keepdims=True)
            drows = drows + jnp.where(sub8 == STEP + k, q_sum, 0.0)
            drows = drows + jnp.where(sub8 == RUN + k, -q_sum * step_r, 0.0)
        dread = dread + dot_fine(dscores, write, NN)
        dwrite = dwrite + dot_fine(dscores, read, TN)
        later = through * later + dot_fine(entered, read, TN)
        dx_ref[0, here, :] = dx
        dkeys_ref[0, here, :STATE] += dwrite
        dkeys_ref[0, here, STATE:] += dread
        dcols_ref[0, 0, here, :] = dcols
        drows_ref[0, 0, :, here] = drows


def scan_backward(x, keys, cols, rows, dy, state, later):
    micro, tokens, width = x.shape
    pairs = width // (2 * HEAD_DIM)
    wide = pl.BlockSpec((1, tokens, 2 * HEAD_DIM), lambda m, p: (m, 0, p))
    key = pl.BlockSpec((1, tokens, 2 * STATE), lambda m, p: (m, 0, 0))
    col = pl.BlockSpec((1, 1, tokens, 8), lambda m, p: (m, p, 0, 0))
    row = pl.BlockSpec((1, 1, 8, tokens), lambda m, p: (m, p, 0, 0))
    hold = pl.BlockSpec((1, 2 * HEAD_DIM, STATE), lambda m, p: (m, p, 0))
    return pl.pallas_call(
        backward_kernel,
        grid=(micro, pairs),
        out_shape=(
            jax.ShapeDtypeStruct(x.shape, F32),
            jax.ShapeDtypeStruct(keys.shape, F32),
            jax.ShapeDtypeStruct(cols.shape, F32),
            jax.ShapeDtypeStruct(rows.shape, F32),
        ),
        in_specs=[wide, key, col, row, wide, hold, hold],
        out_specs=(wide, key, col, row),
        scratch_shapes=[pltpu.VMEM((tokens // CHUNK, 2 * HEAD_DIM, STATE), F32)],
        compiler_params=pltpu.CompilerParams(vmem_limit_bytes=32 << 20),
    )(x, keys, cols, rows, dy, state, later)


def mm(a, b, dims, out=F32):
    return lax.dot_general(a, b, (dims, ((), ())), preferred_element_type=out)


def squash_slope(values):
    logistic = jax.nn.sigmoid(values)
    return logistic * (1.0 + values * (1.0 - logistic))


def segment_numbers(lengths, seq_order, positions):
    seq_index = jnp.arange(lengths.shape[1], dtype=jnp.int32)
    picked = (seq_order[:, :, None] == seq_index).astype(jnp.int32)
    placed = jnp.sum(picked * lengths[:, None, :], axis=2)
    earlier = (seq_index[:, None] > seq_index[None, :]).astype(jnp.int32)
    begins = jnp.sum(earlier[None] * placed[:, None, :], axis=2)
    return jnp.sum((begins[:, None, :] <= positions[None, :, None]).astype(jnp.int32), axis=2)


def spread(values):
    return jnp.repeat(values, HEAD_DIM, axis=-1)


def chain(passing, state, axis, way, beside=()):
    count = lax.axis_size(axis)
    heads = passing.shape[1]
    beside = list(beside)
    done = []

    def pull(passing, state, steps):
        pairs = [(i, i + way * steps) for i in range(count) if 0 <= i + way * steps < count]
        far = lax.ppermute(state.astype(BF), axis, pairs)
        rows = jnp.pad(passing[:, None], ((0, 0), (0, 7), (0, STATE - heads)))
        passing = lax.ppermute(rows, axis, pairs)[:, 0, :heads]
        if beside:
            far, value = lax.optimization_barrier((far, beside.pop(0)))
            done.append(value)
        return passing, far.astype(F32)

    passing, state = pull(passing, state, 1)
    covered = 1
    while covered < count - 1:
        far_passing, far_state = pull(passing, state, covered)
        state = spread(passing)[..., None] * far_state + state
        passing = passing * far_passing
        covered = 2 * covered
    return state, done + beside


def groups_of(seq_count, head_count):
    return [
        [s * head_count + h for s in range(g, g + MEMBERS) for h in range(head_count)]
        for g in range(0, seq_count, MEMBERS)
    ]


def rms_scale(rows):
    return lax.rsqrt(jnp.mean(rows * rows, axis=-1, keepdims=True) + EPSILON)


def norm_back(grad_out, rows, gain, scale):
    weighted = grad_out * gain
    products = jnp.mean(weighted * rows, axis=-1, keepdims=True)
    return scale * weighted - rows * (scale * scale * scale * products)


def to_rows(features):
    count = lax.axis_size("head")
    lead, tokens, width = features.shape
    split = features.reshape(lead, count, tokens // count, width)
    return lax.all_to_all(split, "head", 1, 3, tiled=True)[:, 0]


def to_features(rows):
    count = lax.axis_size("head")
    lead, number, width = rows.shape
    split = rows.reshape(lead, 1, number, width)
    return lax.all_to_all(split, "head", 3, 1, tiled=True).reshape(
        lead, count * number, width // count
    )


def gather_features(features, jobs, arrays, collective_id):
    count = lax.axis_size("head")
    wide = features[0].shape[2] % 128 == 0
    own = [head_job(f.shape[1], f.shape[2], 1, wide) for f in features]
    found = cube_gather(own + jobs, list(features) + arrays, collective_id)
    whole = list(found[: len(own)])
    if not wide:
        whole = [
            w.transpose(0, 2, 1, 3).reshape(w.shape[0], w.shape[2], count * w.shape[3])
            for w in whole
        ]
    return whole, found[len(own) :]


def reduce_rows(partial_rows, collective_id):
    lead, tokens, width = partial_rows.shape
    count = lax.axis_size("head")
    number = tokens // count
    split = partial_rows.reshape(lead, count, number, width)
    return cube_reduce([head_job(number, width, -1)], [split], collective_id)[0]


def gather_group(rows, collective_id):
    lead, number, width = rows.shape
    count = lax.axis_size("head")
    whole = cube_gather([group_job(number, width, 1)], [rows], collective_id)[0]
    return whole.reshape(lead, MEMBERS, count * number, width)


def reduce_group(partial_rows, collective_id):
    lead, members, tokens, width = partial_rows.shape
    count = lax.axis_size("head")
    number = tokens // count
    split = partial_rows.reshape(lead, members * count, number, width)
    return cube_reduce([group_job(number, width, -1)], [split], collective_id)[0]


def slot_in_mesh(s, h):
    return s * lax.axis_size("head") + h


def in_rows(values):
    line = jnp.concatenate([v.reshape(-1) for v in values])
    return jnp.pad(line, (0, -line.shape[0] % 1024)).reshape(1, -1, 128)


def tied(value, *others):
    return lax.optimization_barrier((value, *others))[0]


def lane_padded(matrix):
    return jnp.pad(matrix, ((0, 0), (0, -matrix.shape[1] % 128)))


def body(
    hidden,
    output_grad,
    lengths,
    seq_order,
    routes,
    mix_gain,
    input_proj,
    state_proj,
    step_proj,
    conv_inner,
    conv_state,
    inner_bias,
    state_bias,
    step_bias,
    decay_rate,
    skip_gain,
    gate_gain,
    output_proj,
    moe_gain,
    router,
    expert_up,
    expert_down,
    shared_up,
    shared_down,
):
    seq_count, head_count = lax.axis_size("seq"), lax.axis_size("head")
    seq_rank, head_rank = lax.axis_index("seq"), lax.axis_index("head")
    micro, tokens, local_width = hidden.shape
    inner_local = conv_inner.shape[1]
    heads_local = step_bias.shape[0]
    pairs = heads_local // 2
    experts_local = expert_up.shape[0]
    shared_local = shared_down.shape[0]
    slice_rows = input_proj.shape[1]
    expert_total = experts_local * head_count
    capacity = 2 * tokens * TOPK // expert_total
    own_experts = experts_local // MEMBERS
    member = lax.rem(seq_rank, MEMBERS)
    row_count = tokens // head_count
    channels = inner_local + 2 * STATE
    groups = groups_of(seq_count, head_count)
    seq_groups = [list(range(g, g + MEMBERS)) for g in range(0, seq_count, MEMBERS)]

    first_shard = lane_padded(jnp.concatenate([input_proj[1], state_proj, step_proj], axis=1))
    gain_rows = jnp.pad(jnp.stack([mix_gain, moe_gain])[None], ((0, 0), (0, 6), (0, 0)))
    route_shard = jnp.pad(routes.transpose(0, 2, 1), ((0, 0), (0, 8 - TOPK), (0, 0)))
    (hidden_full, grad_full, gains), (first_full, route_group) = gather_features(
        [hidden, output_grad, gain_rows],
        [seq_job(slice_rows, first_shard.shape[1], 1), members_job(8, tokens)],
        [first_shard[None], route_shard],
        0,
    )
    first_full = first_full.reshape(D, -1)
    gains = gains[0, :2]
    conv_proj, step_full = first_full[:, :channels], first_full[:, channels : channels + heads_local]
    own_rows = partial(
        lax.dynamic_slice_in_dim, start_index=head_rank * row_count, slice_size=row_count, axis=1
    )
    resid_in = own_rows(hidden_full).astype(F32)
    grad_rows = own_rows(grad_full)

    second_shard = jnp.concatenate(
        [
            input_proj[0],
            output_proj.T,
            router,
            shared_up.reshape(slice_rows, 2 * shared_local),
            shared_down.T,
        ],
        axis=1,
    )
    second_full = lax.all_gather(tied(second_shard, first_full), "seq", axis=0, tiled=True)
    cuts = [inner_local, inner_local, expert_total, 2 * shared_local, shared_local]
    cuts = [sum(cuts[: i + 1]) for i in range(4)]
    proj_gate, out_t, router_full, shared_flat, shared_down_t = jnp.split(second_full, cuts, axis=1)
    expert_shard = jnp.concatenate([expert_up, expert_down.transpose(0, 2, 1)], axis=2)
    expert_shard = expert_shard.reshape(MEMBERS, own_experts, slice_rows, 3 * EFF)

    def return_expert(grads, *after):
        send = grads.reshape(seq_count, slice_rows, 3 * EFF)
        return lax.all_to_all(tied(send, *after), "seq", 0, 0, tiled=True)

    def fetch_expert(own, *after):
        send = jnp.tile(expert_shard[:, own], (seq_count // MEMBERS, 1, 1))
        return lax.all_to_all(tied(send, *after), "seq", 0, 0, tiled=True).reshape(D, 3 * EFF)

    experts = [fetch_expert(0, first_full)]
    hidden_wide = hidden_full.astype(F32)
    scale_mix = rms_scale(hidden_wide)
    normed = (hidden_wide * scale_mix * gains[0]).astype(BF)
    ahead = [(i, i + 1) for i in range(seq_count - 1)]
    behind = [(i + 1, i) for i in range(seq_count - 1)]
    edge = lax.ppermute(normed[:, tokens - EDGE :], "seq", ahead)

    conv_in = mm(normed, conv_proj, ((2,), (0,)))
    edge, conv_in = lax.optimization_barrier((edge, conv_in))
    conv_in = jnp.concatenate([mm(edge, conv_proj, ((2,), (0,))), conv_in], axis=1)
    step_raw = mm(normed, step_full, ((2,), (0,))) + step_bias
    gate_pre = mm(normed, proj_gate, ((2,), (0,)))
    conv_weight = jnp.concatenate([conv_inner, conv_state], axis=1)
    conv_offset = jnp.concatenate([inner_bias, state_bias])
    positions = seq_rank * tokens + jnp.arange(-EDGE, tokens + EDGE, dtype=jnp.int32)
    segment_wide = segment_numbers(lengths, seq_order, positions)
    segments = segment_wide[:, EDGE : EDGE + tokens]
    segment_before = segment_wide[:, EDGE - 1 : EDGE]

    def keep(offset, begin, count):
        now = segment_wide[:, EDGE + begin : EDGE + begin + count]
        return (now == segment_wide[:, EDGE + begin - offset : EDGE + begin - offset + count])[
            :, :, None
        ]

    conv_out = conv_offset + conv_in[:, EDGE:] * conv_weight[0]
    for offset in range(1, CONV):
        shifted = conv_in[:, EDGE - offset : EDGE - offset + tokens]
        conv_out = conv_out + jnp.where(keep(offset, 0, tokens), shifted * conv_weight[offset], 0.0)
    act = jax.nn.silu(conv_out)
    signal, keys = act[:, :, :inner_local], act[:, :, inner_local:]
    step_sizes = jax.nn.softplus(step_raw)
    log_decay = -step_sizes * decay_rate
    row_index = jnp.arange(tokens, dtype=jnp.int32)
    until = (row_index[:, None] <= row_index[None, :]).astype(F32)
    running = jnp.einsum("ji,mjh->mih", until, log_decay, precision=HIGHEST)
    same_start = segments == segment_before
    same_end = segments == segments[:, -1:]
    entry_weight = jnp.where(same_start[:, :, None], jnp.exp(running), 0.0)
    passing = entry_weight[:, -1]
    leave_weight = (
        jnp.where(same_end[:, :, None], jnp.exp(running[:, -1:] - running), 0.0) * step_sizes
    )
    local_state = jnp.einsum(
        "mtc,mtn->mcn", spread(leave_weight) * signal, keys[:, :, :STATE], precision=HIGHEST
    )
    def by_pair(values):
        return values.reshape(micro, tokens, pairs, 2).transpose(0, 2, 1, 3)

    def flag(values):
        return jnp.broadcast_to(
            values.astype(F32)[:, None, :, None], (micro, pairs, tokens, 1)
        )

    cols = jnp.concatenate(
        [
            by_pair(running),
            by_pair(step_sizes),
            flag(segments),
            flag(segment_before),
            jnp.zeros((micro, pairs, tokens, 2), F32),
        ],
        axis=3,
    )
    rows = cols.transpose(0, 1, 3, 2)
    state_in, (local_out,) = chain(
        passing, tied(local_state, experts[0]), "seq", 1, (scan_forward(signal, keys, cols, rows),)
    )
    grad_group = lax.all_gather(
        tied(grad_rows, state_in), ("seq", "head"), axis=1, tiled=True, axis_index_groups=groups
    ).reshape(micro, MEMBERS, tokens, D)
    skip_wide, entry_wide = spread(skip_gain), spread(entry_weight)
    from_state = jnp.einsum(
        "mtn,mcn->mtc", keys[:, :, STATE:], state_in, precision=HIGHEST
    )
    mixer_out = local_out + entry_wide * from_state + skip_wide * signal
    gate_act = jax.nn.silu(gate_pre)
    gated = mixer_out * gate_act
    squares = lax.psum(jnp.sum(gated * gated, axis=2), "head")
    scale_gate = lax.rsqrt(squares / INNER + EPSILON)[:, :, None]
    gate_normed = (gated * scale_gate * gate_gain).astype(BF)
    mix_rows = reduce_rows(mm(gate_normed, out_t, ((2,), (1,)), BF), 1)
    resid_mid = resid_in + mix_rows
    scale_moe = rms_scale(resid_mid)
    moe_rows = (resid_mid * scale_moe * gains[1]).astype(BF)
    moe_group = gather_group(moe_rows, 2)

    expert_ids = jnp.arange(expert_total, dtype=jnp.int32)
    experts += [fetch_expert(own, moe_group) for own in range(1, own_experts)]

    def dense_weights(route_lines, rows):
        logits = mm(rows, router_full, ((rows.ndim - 1,), (0,)))
        named = jnp.any(route_lines[..., None] == expert_ids, axis=-3)
        top = jnp.max(jnp.where(named, logits, -jnp.inf), axis=-1, keepdims=True)
        raised = jnp.where(named, jnp.exp(logits - top), 0.0)
        return named, raised / jnp.sum(raised, axis=-1, keepdims=True)

    named_group, weight_group = dense_weights(route_group[:, :, :TOPK], moe_group)
    first_own = head_rank * experts_local + member * own_experts
    slot_index = jnp.arange(capacity, dtype=jnp.int32)
    ffn_parts, back_parts, expert_grads, weight_grads = [], [], [], []
    block = (((3,), (2,)), ((0, 1), (0, 1)))
    block_t = (((2,), (2,)), ((0, 1), (0, 1)))

    def flat(a):
        return a.reshape(-1, a.shape[-1])

    moe_own = lax.dynamic_index_in_dim(moe_group, member, 1, False)
    grad_own = lax.dynamic_index_in_dim(grad_group, member, 1, False)
    shared_both = mm(moe_own, shared_flat, ((2,), (0,)))
    shared_gate, shared_linear = shared_both[..., :shared_local], shared_both[..., shared_local:]
    shared_act = (jax.nn.silu(shared_gate) * shared_linear).astype(BF)
    shared_out = mm(shared_act, shared_down_t, ((2,), (1,)))
    shared_grad_act = mm(grad_own, shared_down_t, ((2,), (0,)))
    shared_grad = jnp.concatenate(
        [
            shared_grad_act * shared_linear * squash_slope(shared_gate),
            shared_grad_act * jax.nn.silu(shared_gate),
        ],
        axis=-1,
    ).astype(BF)
    shared_back = mm(shared_grad, shared_flat, ((2,), (1,)))
    grad_shared_up = mm(moe_own, shared_grad, ((0, 1), (0, 1)), BF)
    grad_shared_down_t = mm(grad_own, shared_act, ((0, 1), (0, 1)), BF)

    expert_backs, slot_parts = [], []
    for own in range(own_experts):
        weights = tied(experts[own], *((expert_grads[-1], shared_out) if own else ()))
        chosen = (expert_ids == first_own + own).astype(F32)
        named = jnp.sum(named_group * chosen, axis=-1)
        weight = jnp.sum(weight_group * chosen, axis=-1)
        rank = mm(named.astype(BF), until.astype(BF), ((2,), (0,))).astype(jnp.int32) - 1
        pick = (rank[:, :, None, :] == slot_index[:, None]) & (named[:, :, None, :] > 0.0)
        slots = pick.astype(BF)
        slot_weight = jnp.sum(pick * weight[:, :, None, :], axis=-1, keepdims=True)
        slot_rows = lax.dot_general(slots, moe_group, block, preferred_element_type=BF)
        slot_grads = lax.dot_general(slots, grad_group, block, preferred_element_type=BF)
        up_own, down_t = weights[:, : 2 * EFF], weights[:, 2 * EFF :]
        both = mm(slot_rows, up_own, ((3,), (0,)))
        up_gate, up_linear = both[..., :EFF], both[..., EFF:]
        hidden_act = (jax.nn.silu(up_gate) * up_linear).astype(BF)
        made = mm(hidden_act, down_t, ((3,), (1,)))
        slot_dot = jnp.sum(slot_grads.astype(F32) * made, axis=-1, keepdims=True)
        weight_grads.append(jnp.sum(pick * slot_dot, axis=2))
        made_low = (made * slot_weight).astype(BF)
        slot_parts.append(slots)
        ffn_parts.append(made_low)
        grads_low = (slot_grads * slot_weight).astype(BF)
        act_grad = mm(grads_low, down_t, ((3,), (0,)))
        both_grad = jnp.concatenate(
            [act_grad * up_linear * squash_slope(up_gate), act_grad * jax.nn.silu(up_gate)], axis=-1
        ).astype(BF)
        back = mm(both_grad, up_own, ((3,), (1,)), BF)
        back_parts.append(back)
        expert_grads.append(
            jnp.concatenate(
                [
                    mm(flat(slot_rows), flat(both_grad), ((0,), (0,)), BF),
                    mm(flat(grads_low), flat(hidden_act), ((0,), (0,)), BF),
                ],
                axis=1,
            )
        )

    def group_partial(parts, own_part):
        total = lax.dot_general(
            jnp.concatenate(slot_parts, axis=2),
            jnp.concatenate(parts, axis=2),
            block_t,
            preferred_element_type=BF,
        )
        mine = lax.dynamic_slice_in_dim(total, member, 1, 1).astype(F32) + own_part[:, None]
        return lax.dynamic_update_slice_in_dim(total, mine.astype(BF), member, 1)

    weight_grad = lax.all_to_all(
        jnp.stack(weight_grads, axis=-1)
        .reshape(micro, MEMBERS * head_count, row_count, own_experts)
        .transpose(1, 0, 2, 3),
        ("seq", "head"),
        0,
        0,
        tiled=True,
        axis_index_groups=groups,
    )
    weight_grad = (
        weight_grad.reshape(MEMBERS, head_count, micro, row_count, own_experts)
        .transpose(2, 3, 1, 0, 4)
        .reshape(micro, row_count, expert_total)
    )
    expert_backs = [return_expert(grads) for grads in expert_grads[:-1]]
    back_parts[-1] = tied(back_parts[-1], *expert_backs)
    back_partial = group_partial(back_parts, shared_back)
    back_rows = reduce_group(back_partial, 3)
    ffn_partial = group_partial(ffn_parts, shared_out)
    route_rows = own_rows(routes).transpose(0, 2, 1)
    named_rows, weight_rows = dense_weights(route_rows, moe_rows)
    weight_grad = jnp.where(named_rows, weight_grad, 0.0)
    logit_grad = weight_rows * (
        weight_grad - jnp.sum(weight_rows * weight_grad, axis=-1, keepdims=True)
    )
    logit_grad = logit_grad.astype(BF)
    grad_router = mm(moe_rows, logit_grad, ((0, 1), (0, 1)))
    back_rows = back_rows + mm(logit_grad, router_full, ((2,), (1,)))
    grad_mid = norm_back(back_rows, resid_mid, gains[1], scale_moe) + grad_rows.astype(F32)
    grad_moe_gain = jnp.sum(back_rows * resid_mid * scale_moe, axis=(0, 1))

    grad_mid_low = grad_mid.astype(BF)
    row_dots = jnp.sum(grad_mid_low.astype(F32) * mix_rows, axis=2)
    grad_mix, row_dots = cube_gather(
        [head_job(row_count, D, 1), head_job(8, row_count, 1)],
        [grad_mid_low, jnp.broadcast_to(row_dots[:, None], (micro, 8, row_count))],
        4,
    )
    grad_mix = grad_mix.reshape(micro, tokens, D)
    grad_mid_features = to_features(grad_mid)
    grad_gate_normed = mm(grad_mix, out_t, ((2,), (0,)))
    weighted = grad_gate_normed * gate_gain
    products = row_dots[:, :, 0].reshape(micro, tokens, 1) / scale_gate
    grad_gated = scale_gate * weighted - gated * (
        scale_gate * scale_gate * scale_gate * products / INNER
    )
    grad_gate_gain = jnp.sum(grad_gate_normed * gated * scale_gate, axis=(0, 1))
    grad_mixer = grad_gated * gate_act
    grad_gate_low = (grad_gated * mixer_out * squash_slope(gate_pre)).astype(BF)
    entry_grad = jnp.einsum(
        "mtc,mtn->mcn", entry_wide * grad_mixer, keys[:, :, STATE:], precision=HIGHEST
    )
    grad_out_t = mm(grad_mix, gate_normed, ((0, 1), (0, 1)), BF)
    grad_gate_proj = mm(normed, grad_gate_low, ((0, 1), (0, 1)), BF)
    second_grads = lane_padded(
        jnp.concatenate([grad_gate_proj, grad_out_t, grad_shared_up, grad_shared_down_t], axis=1)
    ).reshape(1, seq_count, slice_rows, -1)
    ffn_partial = ffn_partial.reshape(micro, MEMBERS * head_count, row_count, D)
    ffn_rows, grad_second = cube_reduce(
        [group_job(row_count, D, -1), seq_job(slice_rows, second_grads.shape[3], -1)],
        [tied(ffn_partial, entry_grad), second_grads],
        5,
    )
    grad_gate_in = mm(tied(grad_gate_low, entry_grad), proj_gate, ((2,), (1,)))
    state_grad, (ffn_rows, grad_gate_in) = chain(
        passing, entry_grad, "seq", -1, (ffn_rows, grad_gate_in)
    )
    output = to_features((resid_mid + ffn_rows).astype(BF))
    expert_backs.append(return_expert(expert_grads[-1], state_grad))
    grad_signal, grad_keys, grad_cols, grad_rows_part = scan_backward(
        signal, keys, cols, rows, grad_mixer, state_in, state_grad
    )
    grad_skip = jnp.sum(
        jnp.sum(grad_mixer * signal, axis=(0, 1)).reshape(heads_local, HEAD_DIM), axis=1
    )
    grad_act = jnp.concatenate([grad_signal + skip_wide * grad_mixer, grad_keys], axis=2)
    small = grad_cols[..., : SEG] + grad_rows_part[:, :, :SEG].transpose(0, 1, 3, 2)

    def by_head(values):
        return values.transpose(0, 2, 1, 3).reshape(micro, tokens, heads_local)

    grad_running, grad_steps = by_head(small[..., RUN:STEP]), by_head(small[..., STEP:SEG])
    grad_log = jnp.einsum("ij,mjh->mih", until, grad_running, precision=HIGHEST)
    grad_decay = -jnp.sum(grad_log * step_sizes, axis=(0, 1))
    grad_step_raw = (grad_steps - grad_log * decay_rate) * jax.nn.sigmoid(step_raw)
    grad_step_bias = jnp.sum(grad_step_raw, axis=(0, 1))
    grad_step_low = grad_step_raw.astype(BF)
    grad_conv = grad_act * squash_slope(conv_out)
    grad_next = jnp.concatenate(
        [grad_conv, lax.ppermute(grad_conv[:, :EDGE], "seq", behind)], axis=1
    )
    grad_conv_offset = jnp.sum(grad_conv, axis=(0, 1))
    grad_pre = grad_conv * conv_weight[0]
    taps = [jnp.sum(grad_conv * conv_in[:, EDGE:], axis=(0, 1))]
    for offset in range(1, CONV):
        shifted = conv_in[:, EDGE - offset : EDGE - offset + tokens]
        taps.append(
            jnp.sum(jnp.where(keep(offset, 0, tokens), grad_conv * shifted, 0.0), axis=(0, 1))
        )
        grad_pre = grad_pre + jnp.where(
            keep(offset, offset, tokens),
            grad_next[:, offset : offset + tokens] * conv_weight[offset],
            0.0,
        )
    grad_conv_weight = jnp.stack(taps)
    grad_pre = grad_pre.astype(BF)

    grad_first = (
        grad_gate_in
        + mm(grad_pre, conv_proj, ((2,), (1,)))
        + mm(grad_step_low, step_full, ((2,), (1,)))
    )
    grad_first_sums = lax.psum(jnp.sum(grad_first * gains[0] * hidden_wide, axis=2), "head")
    grad_conv_proj = mm(normed, grad_pre, ((0, 1), (0, 1)), BF)
    grad_step_proj = mm(normed, grad_step_low, ((0, 1), (0, 1)), BF)
    first_grads = lane_padded(
        jnp.concatenate([grad_conv_proj, grad_step_proj, grad_router.astype(BF)], axis=1)
    ).reshape(1, seq_count, slice_rows, -1)
    wide = local_width % 128 == 0
    grad_first = grad_first.astype(BF)
    if not wide:
        grad_first = grad_first.reshape(micro, tokens, head_count, local_width)
        grad_first = grad_first.transpose(0, 2, 1, 3)
    first_grads = tied(first_grads, expert_backs[-1])
    first_features, grad_first_w = cube_reduce(
        [
            head_job(tokens, local_width, -1, wide),
            seq_job(slice_rows, first_grads.shape[3], -1),
        ],
        [grad_first, first_grads],
        6,
    )
    resid_features = hidden.astype(F32)
    grad_in = scale_mix * (first_features * mix_gain) - resid_features * (
        scale_mix * scale_mix * scale_mix * grad_first_sums[:, :, None] / D
    )
    input_grad = grad_in + grad_mid_features
    cuts = [inner_local, inner_local, 2 * shared_local]
    cuts = [sum(cuts[: i + 1]) for i in range(3)]
    gate_w, out_w, shared_up_w, shared_down_w = jnp.split(grad_second[0], cuts + [sum(cuts[-1:]) + shared_local], axis=1)[:4]
    grad_first_w = grad_first_w[0]
    inner_w, step_w = grad_first_w[:, :inner_local], grad_first_w[:, channels : channels + heads_local]
    over_heads = jnp.concatenate(
        [
            grad_first_w[:, inner_local:channels],
            grad_first_w[:, channels + heads_local : channels + heads_local + expert_total],
        ],
        axis=1,
    )
    expert_w = jnp.stack(
        [
            jnp.sum(
                back.reshape(seq_count // MEMBERS, MEMBERS, slice_rows, 3 * EFF).astype(F32), axis=0
            )
            for back in expert_backs
        ],
        axis=1,
    ).reshape(experts_local, slice_rows, 3 * EFF)
    own_sizes = [CONV * inner_local, inner_local, inner_local, heads_local, heads_local, heads_local]
    own_small = in_rows(
        [
            grad_conv_weight[:, :inner_local],
            grad_conv_offset[:inner_local],
            grad_gate_gain,
            grad_step_bias,
            grad_decay,
            grad_skip,
            jnp.sum(first_features * resid_features * scale_mix, axis=(0, 1)),
        ]
    )
    all_sizes = [CONV * 2 * STATE, 2 * STATE, D]
    all_small = in_rows(
        [grad_conv_weight[:, inner_local:], grad_conv_offset[inner_local:], grad_moe_gain]
    )
    seq_bits, head_bits = bits_in("seq", seq_count), bits_in("head", head_count)
    over_heads = lane_padded(over_heads)[None]

    def plain_job(array, bits, slot_of):
        return Job([((0, array.shape[1]), (0, array.shape[2]), bits)], slot_of)

    heads_found, own_found, all_found = cube_gather(
        [
            plain_job(over_heads, head_bits, slot_in_head),
            plain_job(own_small, seq_bits, slot_in_seq),
            plain_job(all_small, seq_bits + head_bits, slot_in_mesh),
        ],
        [over_heads, own_small, all_small],
        7,
    )
    over_heads = jnp.sum(heads_found[0], axis=0)
    state_w, router_w = over_heads[:, : 2 * STATE], over_heads[:, 2 * STATE : 2 * STATE + expert_total]

    def taken(found, sizes):
        return jnp.split(jnp.sum(found[0], axis=0).reshape(-1), [sum(sizes[: i + 1]) for i in range(len(sizes))])

    conv_inner_w, inner_bias_w, gate_gain_w, step_bias_w, decay_w, skip_w, mix_gain_w = taken(
        own_found, own_sizes
    )
    conv_state_w, state_bias_w, moe_gain_w, _ = taken(all_found, all_sizes)
    return (
        output,
        input_grad,
        mix_gain_w[:local_width],
        jnp.stack([gate_w, inner_w]),
        state_w,
        step_w,
        conv_inner_w.reshape(CONV, inner_local),
        conv_state_w.reshape(CONV, 2 * STATE),
        inner_bias_w,
        state_bias_w,
        step_bias_w,
        decay_w,
        skip_w,
        gate_gain_w,
        out_w.T,
        lax.dynamic_slice_in_dim(moe_gain_w, head_rank * local_width, local_width, 0),
        router_w,
        expert_w[:, :, : 2 * EFF],
        expert_w[:, :, 2 * EFF :].transpose(0, 2, 1),
        shared_up_w.reshape(slice_rows, 2, shared_local),
        shared_down_w.T,
    )


def solution(mesh):
    return jax.shard_map(
        body,
        mesh=mesh,
        in_specs=(
            P(None, "seq", "head"),
            P(None, "seq", "head"),
            P(),
            P(),
            P(None, "seq", None),
            P("head"),
            P(None, "seq", "head"),
            P("seq", None),
            P("seq", "head"),
            P(None, "head"),
            P(),
            P("head"),
            P(),
            P("head"),
            P("head"),
            P("head"),
            P("head"),
            P("head", "seq"),
            P("head"),
            P("seq", None),
            P("head", "seq", None),
            P("head", None, "seq"),
            P("seq", None, "head"),
            P("head", "seq"),
        ),
        out_specs=(
            P(None, "seq", "head"),
            P(None, "seq", "head"),
            P("head"),
            P(None, "seq", "head"),
            P("seq", None),
            P("seq", "head"),
            P(None, "head"),
            P(),
            P("head"),
            P(),
            P("head"),
            P("head"),
            P("head"),
            P("head"),
            P("head", "seq"),
            P("head"),
            P("seq", None),
            P("head", "seq", None),
            P("head", None, "seq"),
            P("seq", None, "head"),
            P("head", "seq"),
        ),
        check_vma=False,
    )
```

```python
import functools
from functools import partial

import jax
import jax.numpy as jnp
from jax import lax
from jax.experimental import pallas as pl
from jax.experimental.pallas import tpu as pltpu
from jax.sharding import PartitionSpec as P

D = 1536
HEAD_DIM = 64
STATE = 128
CONV = 4
TOPK = 6
EFF = 512
INNER = 3072
MEMBERS = 4
EDGE = 8
CHUNK = 128

EPSILON = 1e-05
HIGHEST = lax.Precision.HIGHEST
BF = jnp.bfloat16
F32 = jnp.float32
MESH = pl.DeviceIdType.MESH

def flips(bits):
    found = [(0, 0)]
    for axis, mask in bits:
        found += [(a ^ (mask * (axis == "seq")), b ^ (mask * (axis == "head"))) for a, b in found]
    return found


def joined(left, right):
    return (left[0] ^ right[0], left[1] ^ right[1])


def flip_of(bit):
    axis, mask = bit
    return (mask, 0) if axis == "seq" else (0, mask)


def toggled(place, mask):
    found, bit = place, 1
    while bit <= mask:
        if mask & bit:
            found = found + bit * (1 - 2 * lax.rem(lax.div(place, bit), 2))
        bit = 2 * bit
    return found


def across(me, masks):
    return (toggled(me[0], masks[0]), toggled(me[1], masks[1]))


def greet(jobs, me):
    bits = sorted({bit for job in jobs for bit in job.parts[0][2]})
    barrier = pltpu.get_barrier_semaphore()
    for bit in bits:
        pl.semaphore_signal(
            barrier, inc=1, device_id=across(me, flip_of(bit)), device_id_type=MESH
        )
    pl.semaphore_wait(barrier, len(bits))


class Job:
    def __init__(self, parts, slot_of, wide=False):
        self.parts, self.slot_of, self.wide = parts, slot_of, wide
        self.depth = len(parts[0][2])
        self.count = 1 << self.depth

    def view(self, ref, place, rows, columns, width):
        slot = self.slot_of(*place)
        if self.wide:
            at = columns[0] + slot * width
            if columns[0] % 128 == 0 and width % 128 == 0:
                at = pl.multiple_of(at, 128)
            return ref.at[:, pl.ds(*rows), pl.ds(at, columns[1])]
        return ref.at[:, slot, pl.ds(*rows), pl.ds(*columns)]

    def whole_shape(self, shape):
        lead, rows, columns = shape
        if self.wide:
            return (lead, rows, self.count * columns)
        return (lead, self.count, rows, columns)


def gather_kernel(jobs, *refs):
    me = (lax.axis_index("seq"), lax.axis_index("head"))
    number = len(jobs)
    x_refs, o_refs, sems = refs[:number], refs[number : 2 * number], refs[2 * number :]
    owns, copies, waited = [], {}, set()
    for j in range(number):
        load = pltpu.make_async_copy(x_refs[j], sems[4 * j + 3], sems[4 * j + 2].at[0])
        load.start()
        owns.append(load)
    greet(jobs, me)
    deepest_first = sorted(range(number), key=lambda j: -jobs[j].depth)
    turns = [(0, j) for j in range(number)]
    turns += [(step, j) for j in deepest_first for step in range(1, jobs[j].depth)]
    for step, j in turns:
        job = jobs[j]
        send_sem, recv_sem, own_sem, own_block = sems[4 * j : 4 * j + 4]
        x_ref, o_ref = x_refs[j], o_refs[j]
        width = x_ref.shape[2]
        for p, (rows, columns, order) in enumerate(job.parts):
            other = flip_of(order[step])
            for place, held in enumerate(flips(order[:step])):
                if place and (j, p, place) not in waited:
                    copies[j, p, place].wait_recv()
                    waited.add((j, p, place))
                dst = job.view(o_ref, across(me, held), rows, columns, width)
                src = dst if place else x_ref.at[:, pl.ds(*rows), pl.ds(*columns)]
                arriving = place + (1 << step)
                copy = pltpu.make_async_remote_copy(
                    src_ref=src,
                    dst_ref=dst,
                    send_sem=send_sem.at[p, arriving],
                    recv_sem=recv_sem.at[p, arriving],
                    device_id=across(me, other),
                    device_id_type=MESH,
                )
                copy.start()
                copies[j, p, arriving] = copy
        if step == 0:
            whole = ((0, x_ref.shape[1]), (0, width))
            owns[j].wait()
            owns[j] = pltpu.make_async_copy(
                own_block, job.view(o_ref, me, *whole, width), own_sem.at[1]
            )
            owns[j].start()
    for key, copy in copies.items():
        if key not in waited:
            copy.wait_recv()
    for copy in copies.values():
        copy.wait_send()
    for own in owns:
        own.wait()


def cube_gather(jobs, arrays, collective_id, weight=100 << 20):
    anywhere = pl.BlockSpec(memory_space=pl.ANY)
    scratch = []
    for job, x in zip(jobs, arrays, strict=True):
        for shape in ((len(job.parts), job.count),) * 2 + ((2,),):
            scratch.append(pltpu.SemaphoreType.DMA(shape))
        scratch.append(pltpu.VMEM(x.shape, x.dtype))
    return pl.pallas_call(
        functools.partial(gather_kernel, jobs),
        out_shape=tuple(
            jax.ShapeDtypeStruct(job.whole_shape(x.shape), x.dtype)
            for job, x in zip(jobs, arrays, strict=True)
        ),
        in_specs=[anywhere] * len(jobs),
        out_specs=(anywhere,) * len(jobs),
        scratch_shapes=scratch,
        compiler_params=pltpu.CompilerParams(
            collective_id=collective_id, has_side_effects=True, vmem_limit_bytes=32 << 20
        ),
        cost_estimate=pl.CostEstimate(flops=0, bytes_accessed=weight, transcendentals=0),
    )(*arrays)


def reduce_kernel(jobs, *refs):
    me = (lax.axis_index("seq"), lax.axis_index("head"))
    number = len(jobs)
    x_refs, o_refs, scratch = refs[:number], refs[number : 2 * number], refs[2 * number :]
    greet(jobs, me)
    loads, flying = {}, {}

    def base(job, step):
        return sum(1 << (job.depth - 1 - i) for i in range(step))

    def send(j, p, step, place):
        job, x_ref = jobs[j], x_refs[j]
        kept, stage, send_sem, recv_sem, own_sem = scratch[5 * j : 5 * j + 5]
        rows, columns, order = job.parts[p]
        other = flip_of(order[step])
        gone = joined(flips(order[step + 1 :])[place], other)
        if step == 0:
            src = job.view(x_ref, across(me, gone), rows, columns, stage.shape[3])
        else:
            source = base(job, step - 1) + flips(order[step:]).index(gone)
            src = stage.at[source, :, pl.ds(*rows), pl.ds(*columns)]
        target = base(job, step) + place
        copy = pltpu.make_async_remote_copy(
            src_ref=src,
            dst_ref=stage.at[target, :, pl.ds(*rows), pl.ds(*columns)],
            send_sem=send_sem.at[p, target],
            recv_sem=recv_sem.at[p, target],
            device_id=across(me, other),
            device_id_type=MESH,
        )
        copy.start()
        flying[j, p, step, place] = copy

    def add(j, p, step, place):
        job, o_ref = jobs[j], o_refs[j]
        kept, stage = scratch[5 * j : 5 * j + 2]
        rows, columns, order = job.parts[p]
        tile = 16 if rows[1] % 16 == 0 else 8
        target = base(job, step) + place
        left = flips(order[step + 1 :])[place]
        source = base(job, step - 1) + flips(order[step:]).index(left) if step else 0

        def one(i, carry):
            here = pl.ds(pl.multiple_of(rows[0] + i * tile, tile), tile)
            for m in range(stage.shape[1]):
                got = stage[target, m, here, pl.ds(*columns)].astype(F32)
                if step == 0:
                    mine = kept[place, m, here, pl.ds(*columns)]
                else:
                    mine = stage[source, m, here, pl.ds(*columns)]
                total = got + mine.astype(F32)
                if step + 1 == job.depth:
                    o_ref[m, here, pl.ds(*columns)] = total
                else:
                    stage[target, m, here, pl.ds(*columns)] = total.astype(stage.dtype)
            return carry

        lax.fori_loop(0, rows[1] // tile, one, 0)

    def sequence(job, p, step):
        order = job.parts[p][2]
        found = flips(order[step + 1 :])
        if step + 1 == job.depth:
            return [0]
        other, later = flip_of(order[step + 1]), flips(order[step + 2 :])
        return [found.index(joined(left, other)) for left in later] + [
            found.index(left) for left in later
        ]

    for j, job in enumerate(jobs):
        for p in range(len(job.parts)):
            for place in sequence(job, p, 0):
                send(j, p, 0, place)
    for j, job in enumerate(jobs):
        kept, stage, send_sem, recv_sem, own_sem = scratch[5 * j : 5 * j + 5]
        for p, (rows, columns, order) in enumerate(job.parts):
            for place, held in enumerate(flips(order[1:])):
                load = pltpu.make_async_copy(
                    job.view(x_refs[j], across(me, held), rows, columns, stage.shape[3]),
                    kept.at[place, :, pl.ds(*rows), pl.ds(*columns)],
                    own_sem.at[p, place],
                )
                load.start()
                loads[j, p, place] = load
    for step in range(max(job.depth for job in jobs)):
        for j, job in enumerate(jobs):
            if step >= job.depth:
                continue
            for p, (rows, columns, order) in enumerate(job.parts):
                places = sequence(job, p, step)
                for at, place in enumerate(places):
                    if step == 0:
                        loads[j, p, place].wait()
                    flying[j, p, step, place].wait_recv()
                    add(j, p, step, place)
                    if step + 1 < job.depth and at < len(places) // 2:
                        send(j, p, step + 1, at)
    for copy in flying.values():
        copy.wait_send()


def cube_reduce(jobs, arrays, collective_id, weight=100 << 20):
    out_shape, scratch = [], []
    for job, x in zip(jobs, arrays, strict=True):
        if job.wide:
            lead, rows, columns = x.shape[0], x.shape[1], x.shape[2] // job.count
        else:
            lead, _, rows, columns = x.shape
        out_shape.append(jax.ShapeDtypeStruct((lead, rows, columns), F32))
        scratch += [
            pltpu.VMEM((job.count // 2, lead, rows, columns), x.dtype),
            pltpu.VMEM((job.count - 1, lead, rows, columns), x.dtype),
            pltpu.SemaphoreType.DMA((len(job.parts), job.count - 1)),
            pltpu.SemaphoreType.DMA((len(job.parts), job.count - 1)),
            pltpu.SemaphoreType.DMA((len(job.parts), job.count // 2)),
        ]
    return pl.pallas_call(
        functools.partial(reduce_kernel, jobs),
        out_shape=tuple(out_shape),
        in_specs=[pl.BlockSpec(memory_space=pl.ANY)] * len(jobs),
        out_specs=(pl.BlockSpec(memory_space=pltpu.VMEM),) * len(jobs),
        scratch_shapes=scratch,
        compiler_params=pltpu.CompilerParams(
            collective_id=collective_id, has_side_effects=True, vmem_limit_bytes=52 << 20
        ),
        cost_estimate=pl.CostEstimate(flops=0, bytes_accessed=weight, transcendentals=0),
    )(*arrays)


def bits_in(axis, size):
    return [(axis, 1 << i) for i in range(size.bit_length() - 1)]


def thirds(rows, columns):
    if columns % 384:
        return [((0, rows), (0, columns))]
    third = columns // 3
    return [((0, rows), (i * third, third)) for i in range(3)]


def slot_in_head(s, h):
    return h


def slot_in_seq(s, h):
    return s


def slot_in_members(s, h):
    return lax.rem(s, MEMBERS)


def slot_in_group(s, h):
    return lax.rem(s, MEMBERS) * lax.axis_size("head") + h


def group_job(rows, columns, way):
    core = ("head", 1)
    links = bits_in("head", lax.axis_size("head"))[1:] + bits_in("seq", MEMBERS)
    parts = []
    for i, (r, c) in enumerate(thirds(rows, columns)):
        turned = links[i:] + links[:i]
        parts.append((r, c, (turned + [core])[::way]))
    return Job(parts, slot_in_group)


def head_job(rows, columns, way, wide=False):
    bits = bits_in("head", lax.axis_size("head"))
    order = (bits[1:] + bits[:1])[::way]
    return Job([(r, c, order) for r, c in thirds(rows, columns)], slot_in_head, wide)


def seq_job(rows, columns, way):
    bits = bits_in("seq", lax.axis_size("seq"))
    cut = rows * 7 // 12 // 16 * 16
    parts = []
    for _, some in thirds(rows, columns):
        parts.append(((0, cut), some, bits[::-1][::way]))
        parts.append(((cut, rows - cut), some, (bits[:1] + bits[:0:-1])[::way]))
    return Job(parts, slot_in_seq)


def members_job(rows, columns):
    return Job([((0, rows), (0, columns), bits_in("seq", MEMBERS))], slot_in_members)


def chain_kernel(way, widths, state_ref, pass_ref, out_ref, far, far_pass, low, near_pass, sems):
    count = lax.axis_size("seq")
    me, head = lax.axis_index("seq"), lax.axis_index("head")
    micro, heads = pass_ref.shape[0], pass_ref.shape[1]
    place = me if way == 1 else count - 1 - me
    barrier = pltpu.get_barrier_semaphore()
    expected = 0
    for width in sorted(set(widths)):
        for there, steps in ((place + width < count, width), (place >= width, -width)):
            expected = expected + there.astype(jnp.int32)

            @pl.when(there)
            def _():
                pl.semaphore_signal(
                    barrier, inc=1, device_id=(me + way * steps, head), device_id_type=MESH
                )

    pl.semaphore_wait(barrier, expected)

    def rows_of(h):
        return pl.ds(h * HEAD_DIM, HEAD_DIM)

    low[0] = state_ref[...].astype(BF)
    near_pass[0] = pass_ref[...]
    for hop, width in enumerate(widths):
        sends, gets = place + width < count, place >= width
        copies = [
            pltpu.make_async_remote_copy(
                src_ref=src.at[hop],
                dst_ref=dst.at[hop],
                send_sem=sems.at[0, i, hop],
                recv_sem=sems.at[1, i, hop],
                device_id=(me + way * width, head),
                device_id_type=MESH,
            )
            for i, (src, dst) in enumerate(((low, far), (near_pass, far_pass)))
        ]

        @pl.when(sends)
        def _():
            for copy in copies:
                copy.start()

        @pl.when(gets)
        def _():
            for copy in copies:
                copy.wait_recv()
            for m in range(micro):
                for h in range(heads):
                    got = far[hop, m, rows_of(h), :].astype(F32)
                    if hop:
                        near = near_pass[hop, m, h : h + 1, :]
                        got = out_ref[m, rows_of(h), :] + near * got
                    out_ref[m, rows_of(h), :] = got
                    if hop + 1 < len(widths):
                        low[hop + 1, m, rows_of(h), :] = got.astype(BF)
            if hop + 1 < len(widths):
                passed = far_pass[hop]
                near_pass[hop + 1] = passed * near_pass[hop] if hop else passed

        @pl.when(jnp.logical_not(gets))
        def _():
            if hop == 0:
                out_ref[...] = jnp.zeros_like(out_ref)
            if hop + 1 < len(widths):
                low[hop + 1] = out_ref[...].astype(BF)
                near_pass[hop + 1] = jnp.zeros_like(pass_ref)

        @pl.when(sends)
        def _():
            for copy in copies:
                copy.wait_send()


def chain(passing, state, way, collective_id):
    count = lax.axis_size("seq")
    widths, covered = [1], 1
    while covered < count - 1:
        widths.append(covered)
        covered = 2 * covered
    hops = len(widths)
    lines = jnp.broadcast_to(passing[:, :, None], passing.shape + (STATE,))
    vmem = pl.BlockSpec(memory_space=pltpu.VMEM)
    return pl.pallas_call(
        functools.partial(chain_kernel, way, widths),
        out_shape=jax.ShapeDtypeStruct(state.shape, F32),
        in_specs=[vmem, vmem],
        out_specs=vmem,
        scratch_shapes=[
            pltpu.VMEM((hops,) + state.shape, BF),
            pltpu.VMEM((hops,) + lines.shape, F32),
            pltpu.VMEM((hops,) + state.shape, BF),
            pltpu.VMEM((hops,) + lines.shape, F32),
            pltpu.SemaphoreType.DMA((2, 2, hops)),
        ],
        compiler_params=pltpu.CompilerParams(
            collective_id=collective_id, has_side_effects=True, vmem_limit_bytes=32 << 20
        ),
        cost_estimate=pl.CostEstimate(flops=0, bytes_accessed=100 << 20, transcendentals=0),
    )(state, lines)


RUN, STEP, SEG = 0, 2, 4


def dot(a, b, dims):
    return lax.dot_general(
        a.astype(BF), b.astype(BF), (dims, ((), ())), preferred_element_type=F32
    )


def split_low(a):
    high = a.astype(BF)
    return high, (a - high.astype(F32)).astype(BF)


def dot_fine(a, b, dims):
    (a_high, a_low), (b_high, b_low) = split_low(a), split_low(b)
    return dot(a_high, b_high, dims) + (dot(a_high, b_low, dims) + dot(a_low, b_high, dims))


NN = ((1,), (0,))
NT = ((1,), (1,))
TN = ((0,), (0,))


def chunk_parts(cols_ref, rows_ref, begin):
    here = pl.ds(begin, CHUNK)
    cols, rows = cols_ref[0, 0, here, :], rows_ref[0, 0, :, here]
    last = slice(CHUNK - 1, CHUNK)
    seg_c, seg_r, seg_end = cols[:, SEG : SEG + 1], rows[SEG : SEG + 1], cols[last, SEG : SEG + 1]
    if begin:
        before = cols_ref[0, 0, pl.ds(begin - 8, 8), :][7:8]
        seg_before, run_before = before[:, SEG : SEG + 1], [before[:, RUN + k : RUN + k + 1] for k in range(2)]
    else:
        seg_before, run_before = cols[:1, SEG + 1 : SEG + 2], [jnp.zeros((1, 1), F32)] * 2
    row = lax.broadcasted_iota(jnp.int32, (CHUNK, CHUNK), 0)
    column = lax.broadcasted_iota(jnp.int32, (CHUNK, CHUNK), 1)
    within = (row >= column) & (seg_c == seg_r)
    heads = []
    for k in range(2):
        run_c, run_r = cols[:, RUN + k : RUN + k + 1], rows[RUN + k : RUN + k + 1]
        run_end = run_c[CHUNK - 1 :]
        decay = jnp.where(within, jnp.exp(jnp.where(within, run_c - run_r, 0.0)), 0.0)
        enter = jnp.where(seg_c == seg_before, jnp.exp(run_c - run_before[k]), 0.0)
        leave = jnp.where(seg_c == seg_end, jnp.exp(run_end - run_c), 0.0)
        through = jnp.where(seg_end == seg_before, jnp.exp(run_end - run_before[k]), 0.0)
        heads.append((decay, enter, leave, through, cols[:, STEP + k : STEP + k + 1], rows[STEP + k : STEP + k + 1]))
    return heads


def of_pair(first, second, axis):
    shape = (first.shape[0], 2 * HEAD_DIM) if axis == 1 else (2 * HEAD_DIM, first.shape[1])
    return jnp.where(
        lax.broadcasted_iota(jnp.int32, shape, axis) < HEAD_DIM,
        jnp.broadcast_to(first, shape),
        jnp.broadcast_to(second, shape),
    )


def halves(value):
    low = lax.broadcasted_iota(jnp.int32, value.shape, 1) < HEAD_DIM
    return jnp.where(low, value, 0.0), jnp.where(low, 0.0, value)


def forward_kernel(x_ref, keys_ref, cols_ref, rows_ref, y_ref):
    state = jnp.zeros((2 * HEAD_DIM, STATE), F32)
    tokens = x_ref.shape[1]
    for begin in range(0, tokens, CHUNK):
        here = pl.ds(begin, CHUNK)
        x, write, read = x_ref[0, here, :], keys_ref[0, here, :STATE], keys_ref[0, here, STATE:]
        heads = chunk_parts(cols_ref, rows_ref, begin)
        scores = dot_fine(read, write, NT)
        split = halves(x)
        y = 0.0
        for k, (decay, enter, leave, through, step_c, step_r) in enumerate(heads):
            y = y + dot_fine(scores * decay * step_r, split[k], NN)
        if begin:
            y = y + of_pair(heads[0][1], heads[1][1], 1) * dot_fine(read, state, NT)
        y_ref[0, here, :] = y
        if begin + CHUNK < tokens:
            keep = of_pair(heads[0][2] * heads[0][4], heads[1][2] * heads[1][4], 1)
            state = of_pair(heads[0][3], heads[1][3], 0) * state + dot_fine(
                keep * x, write, TN
            )


def scan_forward(x, keys, cols, rows):
    micro, tokens, width = x.shape
    pairs = width // (2 * HEAD_DIM)
    wide = pl.BlockSpec((1, tokens, 2 * HEAD_DIM), lambda m, p: (m, 0, p))
    return pl.pallas_call(
        forward_kernel,
        grid=(micro, pairs),
        out_shape=jax.ShapeDtypeStruct((micro, tokens, width), F32),
        in_specs=[
            wide,
            pl.BlockSpec((1, tokens, 2 * STATE), lambda m, p: (m, 0, 0)),
            pl.BlockSpec((1, 1, tokens, 8), lambda m, p: (m, p, 0, 0)),
            pl.BlockSpec((1, 1, 8, tokens), lambda m, p: (m, p, 0, 0)),
        ],
        out_specs=wide,
        compiler_params=pltpu.CompilerParams(vmem_limit_bytes=32 << 20),
        cost_estimate=pl.CostEstimate(
            flops=micro * pairs * tokens * CHUNK * 2 * 700, bytes_accessed=micro * tokens * width * 12, transcendentals=0
        ),
    )(x, keys, cols, rows)


def backward_kernel(
    x_ref, keys_ref, cols_ref, rows_ref, dy_ref, state_ref, next_ref,
    dx_ref, dkeys_ref, dcols_ref, drows_ref, states
):
    tokens = x_ref.shape[1]
    chunks = tokens // CHUNK
    pair = pl.program_id(1)

    @pl.when(pair == 0)
    def _():
        dkeys_ref[...] = jnp.zeros_like(dkeys_ref)

    state = state_ref[0]
    for c in range(chunks):
        states[c] = state
        if c + 1 < chunks:
            here = pl.ds(c * CHUNK, CHUNK)
            heads = chunk_parts(cols_ref, rows_ref, c * CHUNK)
            keep = of_pair(heads[0][2] * heads[0][4], heads[1][2] * heads[1][4], 1)
            state = of_pair(heads[0][3], heads[1][3], 0) * state + dot_fine(
                keep * x_ref[0, here, :], keys_ref[0, here, :STATE], TN
            )
    later = next_ref[0]
    pending = [jnp.zeros((1, 1), F32)] * 2
    end_row = lax.broadcasted_iota(jnp.int32, (CHUNK, 1), 0) == CHUNK - 1
    lane8 = lax.broadcasted_iota(jnp.int32, (CHUNK, 8), 1)
    sub8 = lax.broadcasted_iota(jnp.int32, (8, CHUNK), 0)
    for c in reversed(range(chunks)):
        begin = c * CHUNK
        here = pl.ds(begin, CHUNK)
        x, write, read = x_ref[0, here, :], keys_ref[0, here, :STATE], keys_ref[0, here, STATE:]
        dy = dy_ref[0, here, :]
        state = states[c]
        heads = chunk_parts(cols_ref, rows_ref, begin)
        scores = dot_fine(read, write, NT)
        x_split, dy_split = halves(x), halves(dy)
        enter = of_pair(heads[0][1], heads[1][1], 1)
        leave = of_pair(heads[0][2], heads[1][2], 1)
        step = of_pair(heads[0][4], heads[1][4], 1)
        through = of_pair(heads[0][3], heads[1][3], 0)
        entered = enter * dy
        kept = leave * step * x
        from_later = dot_fine(write, later, NT)
        dx = leave * step * from_later
        dread = dot_fine(entered, state, NN)
        dwrite = dot_fine(kept, later, NN)
        weight_grad = halves(from_later * x)
        entry_grad = halves(entered * dot_fine(read, state, NT))
        kept_state = later * state * through
        dscores = 0.0
        dcols = jnp.zeros((CHUNK, 8), F32)
        drows = jnp.zeros((8, CHUNK), F32)
        for k, (decay, _, leave_k, through_k, step_c, step_r) in enumerate(heads):
            products = dot_fine(dy, x_split[k], NT)
            weighted = products * decay
            dx = dx + dot(scores * decay * step_r, dy_split[k], TN)
            dscores = dscores + weighted * step_r
            q = weighted * scores
            r = q * step_r
            dw = jnp.sum(weight_grad[k], axis=1, keepdims=True) * leave_k
            de = jnp.sum(entry_grad[k], axis=1, keepdims=True)
            drun = jnp.sum(r, axis=1, keepdims=True) + de - dw * step_c
            half = slice(k * HEAD_DIM, (k + 1) * HEAD_DIM)
            passed = jnp.sum(jnp.sum(kept_state[half], axis=1, keepdims=True), axis=0, keepdims=True)
            at_end = passed + jnp.sum(dw * step_c, axis=0, keepdims=True) + pending[k]
            pending[k] = -passed - jnp.sum(de, axis=0, keepdims=True)
            drun = drun + jnp.where(end_row, at_end, 0.0)
            dcols = dcols + jnp.where(lane8 == RUN + k, drun, 0.0) + jnp.where(lane8 == STEP + k, dw, 0.0)
            q_sum = jnp.sum(q, axis=0, keepdims=True)
            drows = drows + jnp.where(sub8 == STEP + k, q_sum, 0.0)
            drows = drows + jnp.where(sub8 == RUN + k, -q_sum * step_r, 0.0)
        dread = dread + dot_fine(dscores, write, NN)
        dwrite = dwrite + dot_fine(dscores, read, TN)
        later = through * later + dot_fine(entered, read, TN)
        dx_ref[0, here, :] = dx
        dkeys_ref[0, here, :STATE] += dwrite
        dkeys_ref[0, here, STATE:] += dread
        dcols_ref[0, 0, here, :] = dcols
        drows_ref[0, 0, :, here] = drows


def scan_backward(x, keys, cols, rows, dy, state, later):
    micro, tokens, width = x.shape
    pairs = width // (2 * HEAD_DIM)
    wide = pl.BlockSpec((1, tokens, 2 * HEAD_DIM), lambda m, p: (m, 0, p))
    key = pl.BlockSpec((1, tokens, 2 * STATE), lambda m, p: (m, 0, 0))
    col = pl.BlockSpec((1, 1, tokens, 8), lambda m, p: (m, p, 0, 0))
    row = pl.BlockSpec((1, 1, 8, tokens), lambda m, p: (m, p, 0, 0))
    hold = pl.BlockSpec((1, 2 * HEAD_DIM, STATE), lambda m, p: (m, p, 0))
    return pl.pallas_call(
        backward_kernel,
        grid=(micro, pairs),
        out_shape=(
            jax.ShapeDtypeStruct(x.shape, F32),
            jax.ShapeDtypeStruct(keys.shape, F32),
            jax.ShapeDtypeStruct(cols.shape, F32),
            jax.ShapeDtypeStruct(rows.shape, F32),
        ),
        in_specs=[wide, key, col, row, wide, hold, hold],
        out_specs=(wide, key, col, row),
        scratch_shapes=[pltpu.VMEM((tokens // CHUNK, 2 * HEAD_DIM, STATE), F32)],
        compiler_params=pltpu.CompilerParams(vmem_limit_bytes=32 << 20),
    )(x, keys, cols, rows, dy, state, later)


def mm(a, b, dims, out=F32):
    return lax.dot_general(a, b, (dims, ((), ())), preferred_element_type=out)


def squash_slope(values):
    logistic = jax.nn.sigmoid(values)
    return logistic * (1.0 + values * (1.0 - logistic))


def segment_numbers(lengths, seq_order, positions):
    seq_index = jnp.arange(lengths.shape[1], dtype=jnp.int32)
    picked = (seq_order[:, :, None] == seq_index).astype(jnp.int32)
    placed = jnp.sum(picked * lengths[:, None, :], axis=2)
    earlier = (seq_index[:, None] > seq_index[None, :]).astype(jnp.int32)
    begins = jnp.sum(earlier[None] * placed[:, None, :], axis=2)
    return jnp.sum((begins[:, None, :] <= positions[None, :, None]).astype(jnp.int32), axis=2)


def spread(values):
    return jnp.repeat(values, HEAD_DIM, axis=-1)


def groups_of(seq_count, head_count):
    return [
        [s * head_count + h for s in range(g, g + MEMBERS) for h in range(head_count)]
        for g in range(0, seq_count, MEMBERS)
    ]


def rms_scale(rows):
    return lax.rsqrt(jnp.mean(rows * rows, axis=-1, keepdims=True) + EPSILON)


def norm_back(grad_out, rows, gain, scale):
    weighted = grad_out * gain
    products = jnp.mean(weighted * rows, axis=-1, keepdims=True)
    return scale * weighted - rows * (scale * scale * scale * products)


def to_rows(features):
    count = lax.axis_size("head")
    lead, tokens, width = features.shape
    split = features.reshape(lead, count, tokens // count, width)
    return lax.all_to_all(split, "head", 1, 3, tiled=True)[:, 0]


def to_features(rows):
    count = lax.axis_size("head")
    lead, number, width = rows.shape
    split = rows.reshape(lead, 1, number, width)
    return lax.all_to_all(split, "head", 3, 1, tiled=True).reshape(
        lead, count * number, width // count
    )


def gather_features(features, jobs, arrays, collective_id):
    count = lax.axis_size("head")
    wide = features[0].shape[2] % 128 == 0
    own = [head_job(f.shape[1], f.shape[2], 1, wide) for f in features]
    found = cube_gather(own + jobs, list(features) + arrays, collective_id)
    whole = list(found[: len(own)])
    if not wide:
        whole = [
            w.transpose(0, 2, 1, 3).reshape(w.shape[0], w.shape[2], count * w.shape[3])
            for w in whole
        ]
    return whole, found[len(own) :]


def reduce_rows(partial_rows, collective_id):
    lead, tokens, width = partial_rows.shape
    count = lax.axis_size("head")
    number = tokens // count
    split = partial_rows.reshape(lead, count, number, width)
    return cube_reduce([head_job(number, width, -1)], [split], collective_id)[0]


def gather_group(rows, collective_id):
    lead, number, width = rows.shape
    count = lax.axis_size("head")
    whole = cube_gather([group_job(number, width, 1)], [rows], collective_id)[0]
    return whole.reshape(lead, MEMBERS, count * number, width)


def reduce_group(partial_rows, collective_id):
    lead, members, tokens, width = partial_rows.shape
    count = lax.axis_size("head")
    number = tokens // count
    split = partial_rows.reshape(lead, members * count, number, width)
    return cube_reduce([group_job(number, width, -1)], [split], collective_id)[0]


def slot_in_mesh(s, h):
    return s * lax.axis_size("head") + h


def in_rows(values):
    line = jnp.concatenate([v.reshape(-1) for v in values])
    return jnp.pad(line, (0, -line.shape[0] % 1024)).reshape(1, -1, 128)


def tied(value, *others):
    return lax.optimization_barrier((value, *others))[0]


def lane_padded(matrix):
    return jnp.pad(matrix, ((0, 0), (0, -matrix.shape[1] % 128)))


def body(
    hidden,
    output_grad,
    lengths,
    seq_order,
    routes,
    mix_gain,
    input_proj,
    state_proj,
    step_proj,
    conv_inner,
    conv_state,
    inner_bias,
    state_bias,
    step_bias,
    decay_rate,
    skip_gain,
    gate_gain,
    output_proj,
    moe_gain,
    router,
    expert_up,
    expert_down,
    shared_up,
    shared_down,
):
    seq_count, head_count = lax.axis_size("seq"), lax.axis_size("head")
    seq_rank, head_rank = lax.axis_index("seq"), lax.axis_index("head")
    micro, tokens, local_width = hidden.shape
    inner_local = conv_inner.shape[1]
    heads_local = step_bias.shape[0]
    pairs = heads_local // 2
    experts_local = expert_up.shape[0]
    shared_local = shared_down.shape[0]
    slice_rows = input_proj.shape[1]
    expert_total = experts_local * head_count
    capacity = 2 * tokens * TOPK // expert_total
    own_experts = experts_local // MEMBERS
    member = lax.rem(seq_rank, MEMBERS)
    row_count = tokens // head_count
    channels = inner_local + 2 * STATE
    groups = groups_of(seq_count, head_count)
    seq_groups = [list(range(g, g + MEMBERS)) for g in range(0, seq_count, MEMBERS)]

    first_shard = lane_padded(jnp.concatenate([input_proj[1], state_proj, step_proj], axis=1))
    gain_rows = jnp.pad(jnp.stack([mix_gain, moe_gain])[None], ((0, 0), (0, 6), (0, 0)))
    route_shard = jnp.pad(routes.transpose(0, 2, 1), ((0, 0), (0, 8 - TOPK), (0, 0)))
    (hidden_full, grad_full, gains), (first_full, route_group) = gather_features(
        [hidden, output_grad, gain_rows],
        [seq_job(slice_rows, first_shard.shape[1], 1), members_job(8, tokens)],
        [first_shard[None], route_shard],
        0,
    )
    first_full = first_full.reshape(D, -1)
    gains = gains[0, :2]
    conv_proj, step_full = first_full[:, :channels], first_full[:, channels : channels + heads_local]
    own_rows = partial(
        lax.dynamic_slice_in_dim, start_index=head_rank * row_count, slice_size=row_count, axis=1
    )
    resid_in = own_rows(hidden_full).astype(F32)
    grad_rows = own_rows(grad_full)

    second_shard = jnp.concatenate(
        [
            input_proj[0],
            output_proj.T,
            router,
            shared_up.reshape(slice_rows, 2 * shared_local),
            shared_down.T,
        ],
        axis=1,
    )
    second_full = lax.all_gather(tied(second_shard, first_full), "seq", axis=0, tiled=True)
    cuts = [inner_local, inner_local, expert_total, 2 * shared_local, shared_local]
    cuts = [sum(cuts[: i + 1]) for i in range(4)]
    proj_gate, out_t, router_full, shared_flat, shared_down_t = jnp.split(second_full, cuts, axis=1)
    expert_shard = jnp.concatenate([expert_up, expert_down.transpose(0, 2, 1)], axis=2)
    expert_shard = expert_shard.reshape(MEMBERS, own_experts, slice_rows, 3 * EFF)

    def return_expert(grads, *after):
        send = grads.reshape(seq_count, slice_rows, 3 * EFF)
        return lax.all_to_all(tied(send, *after), "seq", 0, 0, tiled=True)

    def fetch_expert(own, *after):
        send = jnp.tile(expert_shard[:, own], (seq_count // MEMBERS, 1, 1))
        return lax.all_to_all(tied(send, *after), "seq", 0, 0, tiled=True).reshape(D, 3 * EFF)

    hidden_wide = hidden_full.astype(F32)
    scale_mix = rms_scale(hidden_wide)
    normed = (hidden_wide * scale_mix * gains[0]).astype(BF)
    ahead = [(i, i + 1) for i in range(seq_count - 1)]
    behind = [(i + 1, i) for i in range(seq_count - 1)]
    edge = lax.ppermute(normed[:, tokens - EDGE :], "seq", ahead)

    conv_in = mm(normed, conv_proj, ((2,), (0,)))
    edge, conv_in = lax.optimization_barrier((edge, conv_in))
    conv_in = jnp.concatenate([mm(edge, conv_proj, ((2,), (0,))), conv_in], axis=1)
    step_raw = mm(normed, step_full, ((2,), (0,))) + step_bias
    gate_pre = mm(normed, proj_gate, ((2,), (0,)))
    conv_weight = jnp.concatenate([conv_inner, conv_state], axis=1)
    conv_offset = jnp.concatenate([inner_bias, state_bias])
    positions = seq_rank * tokens + jnp.arange(-EDGE, tokens + EDGE, dtype=jnp.int32)
    segment_wide = segment_numbers(lengths, seq_order, positions)
    segments = segment_wide[:, EDGE : EDGE + tokens]
    segment_before = segment_wide[:, EDGE - 1 : EDGE]

    def keep(offset, begin, count):
        now = segment_wide[:, EDGE + begin : EDGE + begin + count]
        return (now == segment_wide[:, EDGE + begin - offset : EDGE + begin - offset + count])[
            :, :, None
        ]

    conv_out = conv_offset + conv_in[:, EDGE:] * conv_weight[0]
    for offset in range(1, CONV):
        shifted = conv_in[:, EDGE - offset : EDGE - offset + tokens]
        conv_out = conv_out + jnp.where(keep(offset, 0, tokens), shifted * conv_weight[offset], 0.0)
    act = jax.nn.silu(conv_out)
    signal, keys = act[:, :, :inner_local], act[:, :, inner_local:]
    step_sizes = jax.nn.softplus(step_raw)
    log_decay = -step_sizes * decay_rate
    row_index = jnp.arange(tokens, dtype=jnp.int32)
    until = (row_index[:, None] <= row_index[None, :]).astype(F32)
    running = jnp.einsum("ji,mjh->mih", until, log_decay, precision=HIGHEST)
    same_start = segments == segment_before
    same_end = segments == segments[:, -1:]
    entry_weight = jnp.where(same_start[:, :, None], jnp.exp(running), 0.0)
    passing = entry_weight[:, -1]
    leave_weight = (
        jnp.where(same_end[:, :, None], jnp.exp(running[:, -1:] - running), 0.0) * step_sizes
    )
    local_state = jnp.einsum(
        "mtc,mtn->mcn", spread(leave_weight) * signal, keys[:, :, :STATE], precision=HIGHEST
    )
    def by_pair(values):
        return values.reshape(micro, tokens, pairs, 2).transpose(0, 2, 1, 3)

    def flag(values):
        return jnp.broadcast_to(
            values.astype(F32)[:, None, :, None], (micro, pairs, tokens, 1)
        )

    cols = jnp.concatenate(
        [
            by_pair(running),
            by_pair(step_sizes),
            flag(segments),
            flag(segment_before),
            jnp.zeros((micro, pairs, tokens, 2), F32),
        ],
        axis=3,
    )
    rows = cols.transpose(0, 1, 3, 2)
    state_in = chain(passing, local_state, 1, 8)
    experts = [fetch_expert(0, state_in)]
    local_out = scan_forward(signal, keys, cols, rows)
    grad_group = lax.all_gather(
        tied(grad_rows, state_in), ("seq", "head"), axis=1, tiled=True, axis_index_groups=groups
    ).reshape(micro, MEMBERS, tokens, D)
    skip_wide, entry_wide = spread(skip_gain), spread(entry_weight)
    from_state = jnp.einsum(
        "mtn,mcn->mtc", keys[:, :, STATE:], state_in, precision=HIGHEST
    )
    mixer_out = local_out + entry_wide * from_state + skip_wide * signal
    gate_act = jax.nn.silu(gate_pre)
    gated = mixer_out * gate_act
    squares = lax.psum(jnp.sum(gated * gated, axis=2), "head")
    scale_gate = lax.rsqrt(squares / INNER + EPSILON)[:, :, None]
    gate_normed = (gated * scale_gate * gate_gain).astype(BF)
    mix_rows = reduce_rows(mm(gate_normed, out_t, ((2,), (1,)), BF), 1)
    resid_mid = resid_in + mix_rows
    scale_moe = rms_scale(resid_mid)
    moe_rows = (resid_mid * scale_moe * gains[1]).astype(BF)
    moe_group = gather_group(moe_rows, 2)

    expert_ids = jnp.arange(expert_total, dtype=jnp.int32)
    experts += [fetch_expert(own, moe_group) for own in range(1, own_experts)]

    def dense_weights(route_lines, rows):
        logits = mm(rows, router_full, ((rows.ndim - 1,), (0,)))
        named = jnp.any(route_lines[..., None] == expert_ids, axis=-3)
        top = jnp.max(jnp.where(named, logits, -jnp.inf), axis=-1, keepdims=True)
        raised = jnp.where(named, jnp.exp(logits - top), 0.0)
        return named, raised / jnp.sum(raised, axis=-1, keepdims=True)

    named_group, weight_group = dense_weights(route_group[:, :, :TOPK], moe_group)
    first_own = head_rank * experts_local + member * own_experts
    slot_index = jnp.arange(capacity, dtype=jnp.int32)
    ffn_parts, back_parts, expert_grads, weight_grads = [], [], [], []
    block = (((3,), (2,)), ((0, 1), (0, 1)))
    block_t = (((2,), (2,)), ((0, 1), (0, 1)))

    def flat(a):
        return a.reshape(-1, a.shape[-1])

    expert_backs, slot_parts = [], []
    for own in range(own_experts):
        weights = tied(experts[own], *((expert_grads[-1],) if own else (moe_group,)))
        chosen = (expert_ids == first_own + own).astype(F32)
        named = jnp.sum(named_group * chosen, axis=-1)
        weight = jnp.sum(weight_group * chosen, axis=-1)
        rank = mm(named.astype(BF), until.astype(BF), ((2,), (0,))).astype(jnp.int32) - 1
        pick = (rank[:, :, None, :] == slot_index[:, None]) & (named[:, :, None, :] > 0.0)
        slots = pick.astype(BF)
        slot_weight = jnp.sum(pick * weight[:, :, None, :], axis=-1, keepdims=True)
        slot_rows = lax.dot_general(slots, moe_group, block, preferred_element_type=BF)
        slot_grads = lax.dot_general(slots, grad_group, block, preferred_element_type=BF)
        up_own, down_t = weights[:, : 2 * EFF], weights[:, 2 * EFF :]
        both = mm(slot_rows, up_own, ((3,), (0,)))
        up_gate, up_linear = both[..., :EFF], both[..., EFF:]
        hidden_act = (jax.nn.silu(up_gate) * up_linear).astype(BF)
        made = mm(hidden_act, down_t, ((3,), (1,)))
        slot_dot = jnp.sum(slot_grads.astype(F32) * made, axis=-1, keepdims=True)
        weight_grads.append(jnp.sum(pick * slot_dot, axis=2))
        made_low = (made * slot_weight).astype(BF)
        slot_parts.append(slots)
        ffn_parts.append(made_low)
        grads_low = (slot_grads * slot_weight).astype(BF)
        act_grad = mm(grads_low, down_t, ((3,), (0,)))
        both_grad = jnp.concatenate(
            [act_grad * up_linear * squash_slope(up_gate), act_grad * jax.nn.silu(up_gate)], axis=-1
        ).astype(BF)
        back = mm(both_grad, up_own, ((3,), (1,)), BF)
        back_parts.append(back)
        expert_grads.append(
            jnp.concatenate(
                [
                    mm(flat(slot_rows), flat(both_grad), ((0,), (0,)), BF),
                    mm(flat(grads_low), flat(hidden_act), ((0,), (0,)), BF),
                ],
                axis=1,
            )
        )

    moe_own = lax.dynamic_index_in_dim(tied(moe_group, back_parts[-1]), member, 1, False)
    grad_own = lax.dynamic_index_in_dim(grad_group, member, 1, False)
    shared_both = mm(moe_own, shared_flat, ((2,), (0,)))
    shared_gate, shared_linear = shared_both[..., :shared_local], shared_both[..., shared_local:]
    shared_act = (jax.nn.silu(shared_gate) * shared_linear).astype(BF)
    shared_out = mm(shared_act, shared_down_t, ((2,), (1,)))
    shared_grad_act = mm(grad_own, shared_down_t, ((2,), (0,)))
    shared_grad = jnp.concatenate(
        [
            shared_grad_act * shared_linear * squash_slope(shared_gate),
            shared_grad_act * jax.nn.silu(shared_gate),
        ],
        axis=-1,
    ).astype(BF)
    shared_back = mm(shared_grad, shared_flat, ((2,), (1,)))
    grad_shared_up = mm(moe_own, shared_grad, ((0, 1), (0, 1)), BF)
    grad_shared_down_t = mm(grad_own, shared_act, ((0, 1), (0, 1)), BF)

    def group_partial(parts, own_part):
        total = lax.dot_general(
            jnp.concatenate(slot_parts, axis=2),
            jnp.concatenate(parts, axis=2),
            block_t,
            preferred_element_type=BF,
        )
        mine = lax.dynamic_slice_in_dim(total, member, 1, 1).astype(F32) + own_part[:, None]
        return lax.dynamic_update_slice_in_dim(total, mine.astype(BF), member, 1)

    weight_grad = lax.all_to_all(
        jnp.stack(weight_grads, axis=-1)
        .reshape(micro, MEMBERS * head_count, row_count, own_experts)
        .transpose(1, 0, 2, 3),
        ("seq", "head"),
        0,
        0,
        tiled=True,
        axis_index_groups=groups,
    )
    weight_grad = (
        weight_grad.reshape(MEMBERS, head_count, micro, row_count, own_experts)
        .transpose(2, 3, 1, 0, 4)
        .reshape(micro, row_count, expert_total)
    )
    expert_backs = [return_expert(grads) for grads in expert_grads[:-1]]
    back_parts[-1] = tied(back_parts[-1], *expert_backs)
    back_partial = group_partial(back_parts, shared_back)
    back_rows = reduce_group(back_partial, 3)
    ffn_partial = group_partial(ffn_parts, shared_out)
    route_rows = own_rows(routes).transpose(0, 2, 1)
    named_rows, weight_rows = dense_weights(route_rows, moe_rows)
    weight_grad = jnp.where(named_rows, weight_grad, 0.0)
    logit_grad = weight_rows * (
        weight_grad - jnp.sum(weight_rows * weight_grad, axis=-1, keepdims=True)
    )
    logit_grad = logit_grad.astype(BF)
    grad_router = mm(moe_rows, logit_grad, ((0, 1), (0, 1)))
    back_rows = back_rows + mm(logit_grad, router_full, ((2,), (1,)))
    grad_mid = norm_back(back_rows, resid_mid, gains[1], scale_moe) + grad_rows.astype(F32)
    grad_moe_gain = jnp.sum(back_rows * resid_mid * scale_moe, axis=(0, 1))

    grad_mid_low = grad_mid.astype(BF)
    row_dots = jnp.sum(grad_mid_low.astype(F32) * mix_rows, axis=2)
    grad_mix, row_dots = cube_gather(
        [head_job(row_count, D, 1), head_job(8, row_count, 1)],
        [grad_mid_low, jnp.broadcast_to(row_dots[:, None], (micro, 8, row_count))],
        4,
    )
    grad_mix = grad_mix.reshape(micro, tokens, D)
    grad_mid_features = to_features(grad_mid)
    grad_gate_normed = mm(grad_mix, out_t, ((2,), (0,)))
    weighted = grad_gate_normed * gate_gain
    products = row_dots[:, :, 0].reshape(micro, tokens, 1) / scale_gate
    grad_gated = scale_gate * weighted - gated * (
        scale_gate * scale_gate * scale_gate * products / INNER
    )
    grad_gate_gain = jnp.sum(grad_gate_normed * gated * scale_gate, axis=(0, 1))
    grad_mixer = grad_gated * gate_act
    grad_gate_low = (grad_gated * mixer_out * squash_slope(gate_pre)).astype(BF)
    entry_grad = jnp.einsum(
        "mtc,mtn->mcn", entry_wide * grad_mixer, keys[:, :, STATE:], precision=HIGHEST
    )
    grad_out_t = mm(grad_mix, gate_normed, ((0, 1), (0, 1)), BF)
    grad_gate_proj = mm(normed, grad_gate_low, ((0, 1), (0, 1)), BF)
    second_grads = lane_padded(
        jnp.concatenate([grad_gate_proj, grad_out_t, grad_shared_up, grad_shared_down_t], axis=1)
    ).reshape(1, seq_count, slice_rows, -1)
    ffn_partial = ffn_partial.reshape(micro, MEMBERS * head_count, row_count, D)
    ffn_rows, grad_second = cube_reduce(
        [group_job(row_count, D, -1), seq_job(slice_rows, second_grads.shape[3], -1)],
        [tied(ffn_partial, entry_grad), second_grads],
        5,
    )
    grad_gate_in = mm(grad_gate_low, proj_gate, ((2,), (1,)))
    state_grad = chain(passing, tied(entry_grad, ffn_rows), -1, 9)
    output = to_features((resid_mid + ffn_rows).astype(BF))
    expert_backs.append(return_expert(expert_grads[-1], state_grad))
    grad_signal, grad_keys, grad_cols, grad_rows_part = scan_backward(
        signal, keys, cols, rows, grad_mixer, state_in, state_grad
    )
    grad_skip = jnp.sum(
        jnp.sum(grad_mixer * signal, axis=(0, 1)).reshape(heads_local, HEAD_DIM), axis=1
    )
    grad_act = jnp.concatenate([grad_signal + skip_wide * grad_mixer, grad_keys], axis=2)
    small = grad_cols[..., : SEG] + grad_rows_part[:, :, :SEG].transpose(0, 1, 3, 2)

    def by_head(values):
        return values.transpose(0, 2, 1, 3).reshape(micro, tokens, heads_local)

    grad_running, grad_steps = by_head(small[..., RUN:STEP]), by_head(small[..., STEP:SEG])
    grad_log = jnp.einsum("ij,mjh->mih", until, grad_running, precision=HIGHEST)
    grad_decay = -jnp.sum(grad_log * step_sizes, axis=(0, 1))
    grad_step_raw = (grad_steps - grad_log * decay_rate) * jax.nn.sigmoid(step_raw)
    grad_step_bias = jnp.sum(grad_step_raw, axis=(0, 1))
    grad_step_low = grad_step_raw.astype(BF)
    grad_conv = grad_act * squash_slope(conv_out)
    grad_next = jnp.concatenate(
        [grad_conv, lax.ppermute(grad_conv[:, :EDGE], "seq", behind)], axis=1
    )
    grad_conv_offset = jnp.sum(grad_conv, axis=(0, 1))
    grad_pre = grad_conv * conv_weight[0]
    taps = [jnp.sum(grad_conv * conv_in[:, EDGE:], axis=(0, 1))]
    for offset in range(1, CONV):
        shifted = conv_in[:, EDGE - offset : EDGE - offset + tokens]
        taps.append(
            jnp.sum(jnp.where(keep(offset, 0, tokens), grad_conv * shifted, 0.0), axis=(0, 1))
        )
        grad_pre = grad_pre + jnp.where(
            keep(offset, offset, tokens),
            grad_next[:, offset : offset + tokens] * conv_weight[offset],
            0.0,
        )
    grad_conv_weight = jnp.stack(taps)
    grad_pre = grad_pre.astype(BF)

    columns = first_full.shape[1]
    grad_all = jnp.concatenate([grad_pre, grad_step_low], axis=2)
    grad_all = jnp.pad(grad_all, ((0, 0), (0, 0), (0, columns - grad_all.shape[2])))
    grad_first = grad_gate_in + mm(grad_all, first_full, ((2,), (1,)))
    grad_first_sums = lax.psum(jnp.sum(grad_first * gains[0] * hidden_wide, axis=2), "head")
    first_grads = mm(normed, grad_all, ((0, 1), (0, 1)), BF).reshape(
        1, seq_count, slice_rows, columns
    )
    router_grads = lane_padded(grad_router.astype(BF)).reshape(1, seq_count, slice_rows, -1)
    wide = local_width % 128 == 0
    grad_first = grad_first.astype(BF)
    if not wide:
        grad_first = grad_first.reshape(micro, tokens, head_count, local_width)
        grad_first = grad_first.transpose(0, 2, 1, 3)
    first_grads = tied(first_grads, expert_backs[-1])
    first_features, grad_first_w, grad_router_w = cube_reduce(
        [
            head_job(tokens, local_width, -1, wide),
            seq_job(slice_rows, columns, -1),
            seq_job(slice_rows, router_grads.shape[3], -1),
        ],
        [grad_first, first_grads, router_grads],
        6,
    )
    resid_features = hidden.astype(F32)
    grad_in = scale_mix * (first_features * mix_gain) - resid_features * (
        scale_mix * scale_mix * scale_mix * grad_first_sums[:, :, None] / D
    )
    input_grad = grad_in + grad_mid_features
    cuts = [inner_local, inner_local, 2 * shared_local]
    cuts = [sum(cuts[: i + 1]) for i in range(3)]
    gate_w, out_w, shared_up_w, shared_down_w = jnp.split(grad_second[0], cuts + [sum(cuts[-1:]) + shared_local], axis=1)[:4]
    grad_first_w = grad_first_w[0]
    inner_w, step_w = grad_first_w[:, :inner_local], grad_first_w[:, channels : channels + heads_local]
    over_heads = jnp.concatenate(
        [
            grad_first_w[:, inner_local:channels],
            grad_router_w[0, :, :expert_total],
        ],
        axis=1,
    )
    expert_w = jnp.stack(
        [
            jnp.sum(
                back.reshape(seq_count // MEMBERS, MEMBERS, slice_rows, 3 * EFF).astype(F32), axis=0
            )
            for back in expert_backs
        ],
        axis=1,
    ).reshape(experts_local, slice_rows, 3 * EFF)
    own_sizes = [CONV * inner_local, inner_local, inner_local, heads_local, heads_local, heads_local]
    own_small = in_rows(
        [
            grad_conv_weight[:, :inner_local],
            grad_conv_offset[:inner_local],
            grad_gate_gain,
            grad_step_bias,
            grad_decay,
            grad_skip,
            jnp.sum(first_features * resid_features * scale_mix, axis=(0, 1)),
        ]
    )
    all_sizes = [CONV * 2 * STATE, 2 * STATE, D]
    all_small = in_rows(
        [grad_conv_weight[:, inner_local:], grad_conv_offset[inner_local:], grad_moe_gain]
    )
    seq_bits, head_bits = bits_in("seq", seq_count), bits_in("head", head_count)
    over_heads = lane_padded(over_heads)[None]

    def plain_job(array, bits, slot_of):
        return Job([((0, array.shape[1]), (0, array.shape[2]), bits)], slot_of)

    heads_found, own_found, all_found = cube_gather(
        [
            plain_job(over_heads, head_bits, slot_in_head),
            plain_job(own_small, seq_bits, slot_in_seq),
            plain_job(all_small, seq_bits + head_bits, slot_in_mesh),
        ],
        [over_heads, own_small, all_small],
        7,
    )
    over_heads = jnp.sum(heads_found[0], axis=0)
    state_w, router_w = over_heads[:, : 2 * STATE], over_heads[:, 2 * STATE : 2 * STATE + expert_total]

    def taken(found, sizes):
        return jnp.split(jnp.sum(found[0], axis=0).reshape(-1), [sum(sizes[: i + 1]) for i in range(len(sizes))])

    conv_inner_w, inner_bias_w, gate_gain_w, step_bias_w, decay_w, skip_w, mix_gain_w = taken(
        own_found, own_sizes
    )
    conv_state_w, state_bias_w, moe_gain_w, _ = taken(all_found, all_sizes)
    return (
        output,
        input_grad,
        mix_gain_w[:local_width],
        jnp.stack([gate_w, inner_w]),
        state_w,
        step_w,
        conv_inner_w.reshape(CONV, inner_local),
        conv_state_w.reshape(CONV, 2 * STATE),
        inner_bias_w,
        state_bias_w,
        step_bias_w,
        decay_w,
        skip_w,
        gate_gain_w,
        out_w.T,
        lax.dynamic_slice_in_dim(moe_gain_w, head_rank * local_width, local_width, 0),
        router_w,
        expert_w[:, :, : 2 * EFF],
        expert_w[:, :, 2 * EFF :].transpose(0, 2, 1),
        shared_up_w.reshape(slice_rows, 2, shared_local),
        shared_down_w.T,
    )


def solution(mesh):
    return jax.shard_map(
        body,
        mesh=mesh,
        in_specs=(
            P(None, "seq", "head"),
            P(None, "seq", "head"),
            P(),
            P(),
            P(None, "seq", None),
            P("head"),
            P(None, "seq", "head"),
            P("seq", None),
            P("seq", "head"),
            P(None, "head"),
            P(),
            P("head"),
            P(),
            P("head"),
            P("head"),
            P("head"),
            P("head"),
            P("head", "seq"),
            P("head"),
            P("seq", None),
            P("head", "seq", None),
            P("head", None, "seq"),
            P("seq", None, "head"),
            P("head", "seq"),
        ),
        out_specs=(
            P(None, "seq", "head"),
            P(None, "seq", "head"),
            P("head"),
            P(None, "seq", "head"),
            P("seq", None),
            P("seq", "head"),
            P(None, "head"),
            P(),
            P("head"),
            P(),
            P("head"),
            P("head"),
            P("head"),
            P("head"),
            P("head", "seq"),
            P("head"),
            P("seq", None),
            P("head", "seq", None),
            P("head", None, "seq"),
            P("seq", None, "head"),
            P("head", "seq"),
        ),
        check_vma=False,
    )
```

```python
import functools
from functools import partial

import jax
import jax.numpy as jnp
from jax import lax
from jax.experimental import pallas as pl
from jax.experimental.pallas import tpu as pltpu
from jax.sharding import PartitionSpec as P

D = 1536
HEAD_DIM = 64
STATE = 128
CONV = 4
TOPK = 6
EFF = 512
INNER = 3072
MEMBERS = 4
EDGE = 8
CHUNK = 128

EPSILON = 1e-05
HIGHEST = lax.Precision.HIGHEST
BF = jnp.bfloat16
F32 = jnp.float32
MESH = pl.DeviceIdType.MESH

def flips(bits):
    found = [(0, 0)]
    for axis, mask in bits:
        found += [(a ^ (mask * (axis == "seq")), b ^ (mask * (axis == "head"))) for a, b in found]
    return found


def joined(left, right):
    return (left[0] ^ right[0], left[1] ^ right[1])


def flip_of(bit):
    axis, mask = bit
    return (mask, 0) if axis == "seq" else (0, mask)


def toggled(place, mask):
    found, bit = place, 1
    while bit <= mask:
        if mask & bit:
            found = found + bit * (1 - 2 * lax.rem(lax.div(place, bit), 2))
        bit = 2 * bit
    return found


def across(me, masks):
    return (toggled(me[0], masks[0]), toggled(me[1], masks[1]))


def greet(jobs, me):
    bits = sorted({bit for job in jobs for bit in job.parts[0][2]})
    barrier = pltpu.get_barrier_semaphore()
    for bit in bits:
        pl.semaphore_signal(
            barrier, inc=1, device_id=across(me, flip_of(bit)), device_id_type=MESH
        )
    pl.semaphore_wait(barrier, len(bits))


class Job:
    def __init__(self, parts, slot_of, wide=False):
        self.parts, self.slot_of, self.wide = parts, slot_of, wide
        self.depth = len(parts[0][2])
        self.count = 1 << self.depth

    def view(self, ref, place, rows, columns, width):
        slot = self.slot_of(*place)
        if self.wide:
            at = columns[0] + slot * width
            if columns[0] % 128 == 0 and width % 128 == 0:
                at = pl.multiple_of(at, 128)
            return ref.at[:, pl.ds(*rows), pl.ds(at, columns[1])]
        return ref.at[:, slot, pl.ds(*rows), pl.ds(*columns)]

    def whole_shape(self, shape):
        lead, rows, columns = shape
        if self.wide:
            return (lead, rows, self.count * columns)
        return (lead, self.count, rows, columns)


def gather_kernel(jobs, *refs):
    me = (lax.axis_index("seq"), lax.axis_index("head"))
    number = len(jobs)
    x_refs, o_refs, sems = refs[:number], refs[number : 2 * number], refs[2 * number :]
    owns, copies, waited = [], {}, set()
    for j in range(number):
        load = pltpu.make_async_copy(x_refs[j], sems[4 * j + 3], sems[4 * j + 2].at[0])
        load.start()
        owns.append(load)
    greet(jobs, me)
    deepest_first = sorted(range(number), key=lambda j: -jobs[j].depth)
    turns = [(0, j) for j in range(number)]
    turns += [(step, j) for j in deepest_first for step in range(1, jobs[j].depth)]
    for step, j in turns:
        job = jobs[j]
        send_sem, recv_sem, own_sem, own_block = sems[4 * j : 4 * j + 4]
        x_ref, o_ref = x_refs[j], o_refs[j]
        width = x_ref.shape[2]
        for p, (rows, columns, order) in enumerate(job.parts):
            other = flip_of(order[step])
            for place, held in enumerate(flips(order[:step])):
                if place and (j, p, place) not in waited:
                    copies[j, p, place].wait_recv()
                    waited.add((j, p, place))
                dst = job.view(o_ref, across(me, held), rows, columns, width)
                src = dst if place else x_ref.at[:, pl.ds(*rows), pl.ds(*columns)]
                arriving = place + (1 << step)
                copy = pltpu.make_async_remote_copy(
                    src_ref=src,
                    dst_ref=dst,
                    send_sem=send_sem.at[p, arriving],
                    recv_sem=recv_sem.at[p, arriving],
                    device_id=across(me, other),
                    device_id_type=MESH,
                )
                copy.start()
                copies[j, p, arriving] = copy
        if step == 0:
            whole = ((0, x_ref.shape[1]), (0, width))
            owns[j].wait()
            owns[j] = pltpu.make_async_copy(
                own_block, job.view(o_ref, me, *whole, width), own_sem.at[1]
            )
            owns[j].start()
    for key, copy in copies.items():
        if key not in waited:
            copy.wait_recv()
    for copy in copies.values():
        copy.wait_send()
    for own in owns:
        own.wait()


def cube_gather(jobs, arrays, collective_id, weight=100 << 20):
    anywhere = pl.BlockSpec(memory_space=pl.ANY)
    scratch = []
    for job, x in zip(jobs, arrays, strict=True):
        for shape in ((len(job.parts), job.count),) * 2 + ((2,),):
            scratch.append(pltpu.SemaphoreType.DMA(shape))
        scratch.append(pltpu.VMEM(x.shape, x.dtype))
    return pl.pallas_call(
        functools.partial(gather_kernel, jobs),
        out_shape=tuple(
            jax.ShapeDtypeStruct(job.whole_shape(x.shape), x.dtype)
            for job, x in zip(jobs, arrays, strict=True)
        ),
        in_specs=[anywhere] * len(jobs),
        out_specs=(anywhere,) * len(jobs),
        scratch_shapes=scratch,
        compiler_params=pltpu.CompilerParams(
            collective_id=collective_id, has_side_effects=True, vmem_limit_bytes=32 << 20
        ),
        cost_estimate=pl.CostEstimate(flops=0, bytes_accessed=weight, transcendentals=0),
    )(*arrays)


def reduce_kernel(jobs, *refs):
    me = (lax.axis_index("seq"), lax.axis_index("head"))
    number = len(jobs)
    x_refs, o_refs, scratch = refs[:number], refs[number : 2 * number], refs[2 * number :]
    greet(jobs, me)
    loads, flying = {}, {}

    def base(job, step):
        return sum(1 << (job.depth - 1 - i) for i in range(step))

    def send(j, p, step, place):
        job, x_ref = jobs[j], x_refs[j]
        kept, stage, send_sem, recv_sem, own_sem = scratch[5 * j : 5 * j + 5]
        rows, columns, order = job.parts[p]
        other = flip_of(order[step])
        gone = joined(flips(order[step + 1 :])[place], other)
        if step == 0:
            src = job.view(x_ref, across(me, gone), rows, columns, stage.shape[3])
        else:
            source = base(job, step - 1) + flips(order[step:]).index(gone)
            src = stage.at[source, :, pl.ds(*rows), pl.ds(*columns)]
        target = base(job, step) + place
        copy = pltpu.make_async_remote_copy(
            src_ref=src,
            dst_ref=stage.at[target, :, pl.ds(*rows), pl.ds(*columns)],
            send_sem=send_sem.at[p, target],
            recv_sem=recv_sem.at[p, target],
            device_id=across(me, other),
            device_id_type=MESH,
        )
        copy.start()
        flying[j, p, step, place] = copy

    def add(j, p, step, place):
        job, o_ref = jobs[j], o_refs[j]
        kept, stage = scratch[5 * j : 5 * j + 2]
        rows, columns, order = job.parts[p]
        tile = 16 if rows[1] % 16 == 0 else 8
        target = base(job, step) + place
        left = flips(order[step + 1 :])[place]
        source = base(job, step - 1) + flips(order[step:]).index(left) if step else 0

        def one(i, carry):
            here = pl.ds(pl.multiple_of(rows[0] + i * tile, tile), tile)
            for m in range(stage.shape[1]):
                got = stage[target, m, here, pl.ds(*columns)].astype(F32)
                if step == 0:
                    mine = kept[place, m, here, pl.ds(*columns)]
                else:
                    mine = stage[source, m, here, pl.ds(*columns)]
                total = got + mine.astype(F32)
                if step + 1 == job.depth:
                    o_ref[m, here, pl.ds(*columns)] = total
                else:
                    stage[target, m, here, pl.ds(*columns)] = total.astype(stage.dtype)
            return carry

        lax.fori_loop(0, rows[1] // tile, one, 0)

    def sequence(job, p, step):
        order = job.parts[p][2]
        found = flips(order[step + 1 :])
        if step + 1 == job.depth:
            return [0]
        other, later = flip_of(order[step + 1]), flips(order[step + 2 :])
        return [found.index(joined(left, other)) for left in later] + [
            found.index(left) for left in later
        ]

    for j, job in enumerate(jobs):
        for p in range(len(job.parts)):
            for place in sequence(job, p, 0):
                send(j, p, 0, place)
    for j, job in enumerate(jobs):
        kept, stage, send_sem, recv_sem, own_sem = scratch[5 * j : 5 * j + 5]
        for p, (rows, columns, order) in enumerate(job.parts):
            for place, held in enumerate(flips(order[1:])):
                load = pltpu.make_async_copy(
                    job.view(x_refs[j], across(me, held), rows, columns, stage.shape[3]),
                    kept.at[place, :, pl.ds(*rows), pl.ds(*columns)],
                    own_sem.at[p, place],
                )
                load.start()
                loads[j, p, place] = load
    for step in range(max(job.depth for job in jobs)):
        for j, job in enumerate(jobs):
            if step >= job.depth:
                continue
            for p, (rows, columns, order) in enumerate(job.parts):
                places = sequence(job, p, step)
                for at, place in enumerate(places):
                    if step == 0:
                        loads[j, p, place].wait()
                    flying[j, p, step, place].wait_recv()
                    add(j, p, step, place)
                    if step + 1 < job.depth and at < len(places) // 2:
                        send(j, p, step + 1, at)
    for copy in flying.values():
        copy.wait_send()


def cube_reduce(jobs, arrays, collective_id, weight=100 << 20):
    out_shape, scratch = [], []
    for job, x in zip(jobs, arrays, strict=True):
        if job.wide:
            lead, rows, columns = x.shape[0], x.shape[1], x.shape[2] // job.count
        else:
            lead, _, rows, columns = x.shape
        out_shape.append(jax.ShapeDtypeStruct((lead, rows, columns), F32))
        scratch += [
            pltpu.VMEM((job.count // 2, lead, rows, columns), x.dtype),
            pltpu.VMEM((job.count - 1, lead, rows, columns), x.dtype),
            pltpu.SemaphoreType.DMA((len(job.parts), job.count - 1)),
            pltpu.SemaphoreType.DMA((len(job.parts), job.count - 1)),
            pltpu.SemaphoreType.DMA((len(job.parts), job.count // 2)),
        ]
    return pl.pallas_call(
        functools.partial(reduce_kernel, jobs),
        out_shape=tuple(out_shape),
        in_specs=[pl.BlockSpec(memory_space=pl.ANY)] * len(jobs),
        out_specs=(pl.BlockSpec(memory_space=pltpu.VMEM),) * len(jobs),
        scratch_shapes=scratch,
        compiler_params=pltpu.CompilerParams(
            collective_id=collective_id, has_side_effects=True, vmem_limit_bytes=52 << 20
        ),
        cost_estimate=pl.CostEstimate(flops=0, bytes_accessed=weight, transcendentals=0),
    )(*arrays)


def bits_in(axis, size):
    return [(axis, 1 << i) for i in range(size.bit_length() - 1)]


def thirds(rows, columns):
    if columns % 384:
        return [((0, rows), (0, columns))]
    third = columns // 3
    return [((0, rows), (i * third, third)) for i in range(3)]


def slot_in_head(s, h):
    return h


def slot_in_seq(s, h):
    return s


def slot_in_members(s, h):
    return lax.rem(s, MEMBERS)


def slot_in_group(s, h):
    return lax.rem(s, MEMBERS) * lax.axis_size("head") + h


def group_job(rows, columns, way):
    core = ("head", 1)
    links = bits_in("head", lax.axis_size("head"))[1:] + bits_in("seq", MEMBERS)
    parts = []
    for i, (r, c) in enumerate(thirds(rows, columns)):
        turned = links[i:] + links[:i]
        parts.append((r, c, (turned + [core])[::way]))
    return Job(parts, slot_in_group)


def head_job(rows, columns, way, wide=False):
    bits = bits_in("head", lax.axis_size("head"))
    order = (bits[1:] + bits[:1])[::way]
    return Job([(r, c, order) for r, c in thirds(rows, columns)], slot_in_head, wide)


def seq_job(rows, columns, way):
    bits = bits_in("seq", lax.axis_size("seq"))
    cut = rows * 7 // 12 // 16 * 16
    parts = []
    for _, some in thirds(rows, columns):
        parts.append(((0, cut), some, bits[::-1][::way]))
        parts.append(((cut, rows - cut), some, (bits[:1] + bits[:0:-1])[::way]))
    return Job(parts, slot_in_seq)


def members_job(rows, columns):
    return Job([((0, rows), (0, columns), bits_in("seq", MEMBERS))], slot_in_members)


def chain_kernel(way, widths, state_ref, pass_ref, out_ref, far, far_pass, low, near_pass, sems):
    count = lax.axis_size("seq")
    me, head = lax.axis_index("seq"), lax.axis_index("head")
    micro, heads = pass_ref.shape[0], pass_ref.shape[1]
    place = me if way == 1 else count - 1 - me
    barrier = pltpu.get_barrier_semaphore()
    expected = 0
    for width in sorted(set(widths)):
        for there, steps in ((place + width < count, width), (place >= width, -width)):
            expected = expected + there.astype(jnp.int32)

            @pl.when(there)
            def _():
                pl.semaphore_signal(
                    barrier, inc=1, device_id=(me + way * steps, head), device_id_type=MESH
                )

    pl.semaphore_wait(barrier, expected)

    def rows_of(h):
        return pl.ds(h * HEAD_DIM, HEAD_DIM)

    low[0] = state_ref[...].astype(BF)
    near_pass[0] = pass_ref[...]
    for hop, width in enumerate(widths):
        sends, gets = place + width < count, place >= width
        copies = [
            pltpu.make_async_remote_copy(
                src_ref=src.at[hop],
                dst_ref=dst.at[hop],
                send_sem=sems.at[0, i, hop],
                recv_sem=sems.at[1, i, hop],
                device_id=(me + way * width, head),
                device_id_type=MESH,
            )
            for i, (src, dst) in enumerate(((low, far), (near_pass, far_pass)))
        ]

        @pl.when(sends)
        def _():
            for copy in copies:
                copy.start()

        @pl.when(gets)
        def _():
            for copy in copies:
                copy.wait_recv()
            for m in range(micro):
                for h in range(heads):
                    got = far[hop, m, rows_of(h), :].astype(F32)
                    if hop:
                        near = near_pass[hop, m, h : h + 1, :]
                        got = out_ref[m, rows_of(h), :] + near * got
                    out_ref[m, rows_of(h), :] = got
                    if hop + 1 < len(widths):
                        low[hop + 1, m, rows_of(h), :] = got.astype(BF)
            if hop + 1 < len(widths):
                passed = far_pass[hop]
                near_pass[hop + 1] = passed * near_pass[hop] if hop else passed

        @pl.when(jnp.logical_not(gets))
        def _():
            if hop == 0:
                out_ref[...] = jnp.zeros_like(out_ref)
            if hop + 1 < len(widths):
                low[hop + 1] = out_ref[...].astype(BF)
                near_pass[hop + 1] = jnp.zeros_like(pass_ref)

        @pl.when(sends)
        def _():
            for copy in copies:
                copy.wait_send()


def chain(passing, state, way, collective_id):
    count = lax.axis_size("seq")
    widths, covered = [1], 1
    while covered < count - 1:
        widths.append(covered)
        covered = 2 * covered
    hops = len(widths)
    lines = jnp.broadcast_to(passing[:, :, None], passing.shape + (STATE,))
    vmem = pl.BlockSpec(memory_space=pltpu.VMEM)
    return pl.pallas_call(
        functools.partial(chain_kernel, way, widths),
        out_shape=jax.ShapeDtypeStruct(state.shape, F32),
        in_specs=[vmem, vmem],
        out_specs=vmem,
        scratch_shapes=[
            pltpu.VMEM((hops,) + state.shape, BF),
            pltpu.VMEM((hops,) + lines.shape, F32),
            pltpu.VMEM((hops,) + state.shape, BF),
            pltpu.VMEM((hops,) + lines.shape, F32),
            pltpu.SemaphoreType.DMA((2, 2, hops)),
        ],
        compiler_params=pltpu.CompilerParams(
            collective_id=collective_id, has_side_effects=True, vmem_limit_bytes=32 << 20
        ),
        cost_estimate=pl.CostEstimate(flops=0, bytes_accessed=100 << 20, transcendentals=0),
    )(state, lines)


RUN, STEP, SEG = 0, 2, 4


def dot(a, b, dims):
    return lax.dot_general(
        a.astype(BF), b.astype(BF), (dims, ((), ())), preferred_element_type=F32
    )


def split_low(a):
    high = a.astype(BF)
    return high, (a - high.astype(F32)).astype(BF)


def dot_fine(a, b, dims):
    (a_high, a_low), (b_high, b_low) = split_low(a), split_low(b)
    return dot(a_high, b_high, dims) + (dot(a_high, b_low, dims) + dot(a_low, b_high, dims))


NN = ((1,), (0,))
NT = ((1,), (1,))
TN = ((0,), (0,))


def chunk_parts(cols_ref, rows_ref, begin):
    here = pl.ds(begin, CHUNK)
    cols, rows = cols_ref[0, 0, here, :], rows_ref[0, 0, :, here]
    last = slice(CHUNK - 1, CHUNK)
    seg_c, seg_r, seg_end = cols[:, SEG : SEG + 1], rows[SEG : SEG + 1], cols[last, SEG : SEG + 1]
    if begin:
        before = cols_ref[0, 0, pl.ds(begin - 8, 8), :][7:8]
        seg_before, run_before = before[:, SEG : SEG + 1], [before[:, RUN + k : RUN + k + 1] for k in range(2)]
    else:
        seg_before, run_before = cols[:1, SEG + 1 : SEG + 2], [jnp.zeros((1, 1), F32)] * 2
    row = lax.broadcasted_iota(jnp.int32, (CHUNK, CHUNK), 0)
    column = lax.broadcasted_iota(jnp.int32, (CHUNK, CHUNK), 1)
    within = (row >= column) & (seg_c == seg_r)
    heads = []
    for k in range(2):
        run_c, run_r = cols[:, RUN + k : RUN + k + 1], rows[RUN + k : RUN + k + 1]
        run_end = run_c[CHUNK - 1 :]
        decay = jnp.where(within, jnp.exp(jnp.where(within, run_c - run_r, 0.0)), 0.0)
        enter = jnp.where(seg_c == seg_before, jnp.exp(run_c - run_before[k]), 0.0)
        leave = jnp.where(seg_c == seg_end, jnp.exp(run_end - run_c), 0.0)
        through = jnp.where(seg_end == seg_before, jnp.exp(run_end - run_before[k]), 0.0)
        heads.append((decay, enter, leave, through, cols[:, STEP + k : STEP + k + 1], rows[STEP + k : STEP + k + 1]))
    return heads


def of_pair(first, second, axis):
    shape = (first.shape[0], 2 * HEAD_DIM) if axis == 1 else (2 * HEAD_DIM, first.shape[1])
    return jnp.where(
        lax.broadcasted_iota(jnp.int32, shape, axis) < HEAD_DIM,
        jnp.broadcast_to(first, shape),
        jnp.broadcast_to(second, shape),
    )


def halves(value):
    low = lax.broadcasted_iota(jnp.int32, value.shape, 1) < HEAD_DIM
    return jnp.where(low, value, 0.0), jnp.where(low, 0.0, value)


def forward_kernel(x_ref, keys_ref, cols_ref, rows_ref, y_ref):
    state = jnp.zeros((2 * HEAD_DIM, STATE), F32)
    tokens = x_ref.shape[1]
    for begin in range(0, tokens, CHUNK):
        here = pl.ds(begin, CHUNK)
        x, write, read = x_ref[0, here, :], keys_ref[0, here, :STATE], keys_ref[0, here, STATE:]
        heads = chunk_parts(cols_ref, rows_ref, begin)
        scores = dot_fine(read, write, NT)
        split = halves(x)
        y = 0.0
        for k, (decay, enter, leave, through, step_c, step_r) in enumerate(heads):
            y = y + dot_fine(scores * decay * step_r, split[k], NN)
        if begin:
            y = y + of_pair(heads[0][1], heads[1][1], 1) * dot_fine(read, state, NT)
        y_ref[0, here, :] = y
        if begin + CHUNK < tokens:
            keep = of_pair(heads[0][2] * heads[0][4], heads[1][2] * heads[1][4], 1)
            state = of_pair(heads[0][3], heads[1][3], 0) * state + dot_fine(
                keep * x, write, TN
            )


def scan_forward(x, keys, cols, rows):
    micro, tokens, width = x.shape
    pairs = width // (2 * HEAD_DIM)
    wide = pl.BlockSpec((1, tokens, 2 * HEAD_DIM), lambda m, p: (m, 0, p))
    return pl.pallas_call(
        forward_kernel,
        grid=(micro, pairs),
        out_shape=jax.ShapeDtypeStruct((micro, tokens, width), F32),
        in_specs=[
            wide,
            pl.BlockSpec((1, tokens, 2 * STATE), lambda m, p: (m, 0, 0)),
            pl.BlockSpec((1, 1, tokens, 8), lambda m, p: (m, p, 0, 0)),
            pl.BlockSpec((1, 1, 8, tokens), lambda m, p: (m, p, 0, 0)),
        ],
        out_specs=wide,
        compiler_params=pltpu.CompilerParams(vmem_limit_bytes=32 << 20),
        cost_estimate=pl.CostEstimate(
            flops=micro * pairs * tokens * CHUNK * 2 * 700, bytes_accessed=micro * tokens * width * 12, transcendentals=0
        ),
    )(x, keys, cols, rows)


def backward_kernel(
    x_ref, keys_ref, cols_ref, rows_ref, dy_ref, state_ref, next_ref,
    dx_ref, dkeys_ref, dcols_ref, drows_ref, states
):
    tokens = x_ref.shape[1]
    chunks = tokens // CHUNK
    pair = pl.program_id(1)

    @pl.when(pair == 0)
    def _():
        dkeys_ref[...] = jnp.zeros_like(dkeys_ref)

    state = state_ref[0]
    for c in range(chunks):
        states[c] = state
        if c + 1 < chunks:
            here = pl.ds(c * CHUNK, CHUNK)
            heads = chunk_parts(cols_ref, rows_ref, c * CHUNK)
            keep = of_pair(heads[0][2] * heads[0][4], heads[1][2] * heads[1][4], 1)
            state = of_pair(heads[0][3], heads[1][3], 0) * state + dot_fine(
                keep * x_ref[0, here, :], keys_ref[0, here, :STATE], TN
            )
    later = next_ref[0]
    pending = [jnp.zeros((1, 1), F32)] * 2
    end_row = lax.broadcasted_iota(jnp.int32, (CHUNK, 1), 0) == CHUNK - 1
    lane8 = lax.broadcasted_iota(jnp.int32, (CHUNK, 8), 1)
    sub8 = lax.broadcasted_iota(jnp.int32, (8, CHUNK), 0)
    for c in reversed(range(chunks)):
        begin = c * CHUNK
        here = pl.ds(begin, CHUNK)
        x, write, read = x_ref[0, here, :], keys_ref[0, here, :STATE], keys_ref[0, here, STATE:]
        dy = dy_ref[0, here, :]
        state = states[c]
        heads = chunk_parts(cols_ref, rows_ref, begin)
        scores = dot_fine(read, write, NT)
        x_split, dy_split = halves(x), halves(dy)
        enter = of_pair(heads[0][1], heads[1][1], 1)
        leave = of_pair(heads[0][2], heads[1][2], 1)
        step = of_pair(heads[0][4], heads[1][4], 1)
        through = of_pair(heads[0][3], heads[1][3], 0)
        entered = enter * dy
        kept = leave * step * x
        from_later = dot_fine(write, later, NT)
        dx = leave * step * from_later
        dread = dot_fine(entered, state, NN)
        dwrite = dot_fine(kept, later, NN)
        weight_grad = halves(from_later * x)
        entry_grad = halves(entered * dot_fine(read, state, NT))
        kept_state = later * state * through
        dscores = 0.0
        dcols = jnp.zeros((CHUNK, 8), F32)
        drows = jnp.zeros((8, CHUNK), F32)
        for k, (decay, _, leave_k, through_k, step_c, step_r) in enumerate(heads):
            products = dot_fine(dy, x_split[k], NT)
            weighted = products * decay
            dx = dx + dot(scores * decay * step_r, dy_split[k], TN)
            dscores = dscores + weighted * step_r
            q = weighted * scores
            r = q * step_r
            dw = jnp.sum(weight_grad[k], axis=1, keepdims=True) * leave_k
            de = jnp.sum(entry_grad[k], axis=1, keepdims=True)
            drun = jnp.sum(r, axis=1, keepdims=True) + de - dw * step_c
            half = slice(k * HEAD_DIM, (k + 1) * HEAD_DIM)
            passed = jnp.sum(jnp.sum(kept_state[half], axis=1, keepdims=True), axis=0, keepdims=True)
            at_end = passed + jnp.sum(dw * step_c, axis=0, keepdims=True) + pending[k]
            pending[k] = -passed - jnp.sum(de, axis=0, keepdims=True)
            drun = drun + jnp.where(end_row, at_end, 0.0)
            dcols = dcols + jnp.where(lane8 == RUN + k, drun, 0.0) + jnp.where(lane8 == STEP + k, dw, 0.0)
            q_sum = jnp.sum(q, axis=0, keepdims=True)
            drows = drows + jnp.where(sub8 == STEP + k, q_sum, 0.0)
            drows = drows + jnp.where(sub8 == RUN + k, -q_sum * step_r, 0.0)
        dread = dread + dot_fine(dscores, write, NN)
        dwrite = dwrite + dot_fine(dscores, read, TN)
        later = through * later + dot_fine(entered, read, TN)
        dx_ref[0, here, :] = dx
        dkeys_ref[0, here, :STATE] += dwrite
        dkeys_ref[0, here, STATE:] += dread
        dcols_ref[0, 0, here, :] = dcols
        drows_ref[0, 0, :, here] = drows


def scan_backward(x, keys, cols, rows, dy, state, later):
    micro, tokens, width = x.shape
    pairs = width // (2 * HEAD_DIM)
    wide = pl.BlockSpec((1, tokens, 2 * HEAD_DIM), lambda m, p: (m, 0, p))
    key = pl.BlockSpec((1, tokens, 2 * STATE), lambda m, p: (m, 0, 0))
    col = pl.BlockSpec((1, 1, tokens, 8), lambda m, p: (m, p, 0, 0))
    row = pl.BlockSpec((1, 1, 8, tokens), lambda m, p: (m, p, 0, 0))
    hold = pl.BlockSpec((1, 2 * HEAD_DIM, STATE), lambda m, p: (m, p, 0))
    return pl.pallas_call(
        backward_kernel,
        grid=(micro, pairs),
        out_shape=(
            jax.ShapeDtypeStruct(x.shape, F32),
            jax.ShapeDtypeStruct(keys.shape, F32),
            jax.ShapeDtypeStruct(cols.shape, F32),
            jax.ShapeDtypeStruct(rows.shape, F32),
        ),
        in_specs=[wide, key, col, row, wide, hold, hold],
        out_specs=(wide, key, col, row),
        scratch_shapes=[pltpu.VMEM((tokens // CHUNK, 2 * HEAD_DIM, STATE), F32)],
        compiler_params=pltpu.CompilerParams(vmem_limit_bytes=32 << 20),
    )(x, keys, cols, rows, dy, state, later)


TILE = 256


def expert_kernel(first, capacity, lines_ref, cols_ref, rows_ref, grads_ref, weights_ref, *refs):
    before, refs = ((), refs) if first else (refs[:2], refs[2:])
    ffn_ref, back_ref, dots_ref, sums_ref, total, picked, given = refs
    tokens, width = rows_ref.shape[1], rows_ref.shape[2]
    block = pl.program_id(0)

    @pl.when(block == 0)
    def _():
        total[...] = jnp.zeros_like(total)

    slot = lax.broadcasted_iota(jnp.int32, (capacity, tokens), 0).astype(F32)
    pick = slot == lines_ref[0, 0:1, :]
    slots = jnp.where(pick, 1.0, 0.0).astype(BF)
    slot = lax.broadcasted_iota(jnp.int32, (tokens, capacity), 1).astype(F32)
    places = jnp.where(slot == cols_ref[0, :, 0:1], 1.0, 0.0).astype(BF)
    share = jnp.sum(jnp.where(pick, lines_ref[0, 1:2, :], 0.0), axis=1, keepdims=True)
    tiles = [slice(i, i + TILE) for i in range(0, width, TILE)]
    for tile in tiles:
        picked[:, tile] = dot(slots, rows_ref[0, :, tile], NN).astype(BF)
        given[:, tile] = dot(slots, grads_ref[0, :, tile], NN).astype(BF)
    both = dot(picked[...], weights_ref[:, : 2 * EFF], NN)
    gate, linear = both[:, :EFF], both[:, EFF:]
    logistic = jax.nn.sigmoid(gate)
    silu = gate * logistic
    act = (silu * linear).astype(BF)
    act_grad, made_dot = 0.0, 0.0
    for tile in tiles:
        down = weights_ref[tile, 2 * EFF :]
        made = dot(act, down, NT)
        grad = given[:, tile].astype(F32)
        made_dot = made_dot + jnp.sum(grad * made, axis=1, keepdims=True)
        out = dot(places, made * share, NN)
        if not first:
            out = out + before[0][0, :, tile].astype(F32)
        ffn_ref[0, :, tile] = out.astype(BF)
        grad = (grad * share).astype(BF)
        act_grad = act_grad + dot(grad, down, NN)
        total[tile, 2 * EFF :] += dot(grad, act, TN)
    dots = jnp.sum(jnp.where(pick, made_dot, 0.0), axis=0, keepdims=True)
    dots_ref[0] = jnp.broadcast_to(dots, dots_ref.shape[1:])
    both_grad = jnp.concatenate(
        [act_grad * linear * (logistic * (1.0 + gate * (1.0 - logistic))), act_grad * silu], axis=1
    ).astype(BF)
    for tile in tiles:
        back = dot(both_grad, weights_ref[tile, : 2 * EFF], NT)
        out = dot(places, back, NN)
        if not first:
            out = out + before[1][0, :, tile].astype(F32)
        back_ref[0, :, tile] = out.astype(BF)
        total[tile, : 2 * EFF] += dot(picked[:, tile], both_grad, TN)

    @pl.when(block == pl.num_programs(0) - 1)
    def _():
        for tile in tiles:
            sums_ref[tile, :] = total[tile, :].astype(BF)


def run_expert(capacity, lines, rows, grads, weights, before):
    blocks, tokens, width = rows.shape
    line = pl.BlockSpec((1, 8, tokens), lambda b: (b, 0, 0))
    wide = pl.BlockSpec((1, tokens, width), lambda b: (b, 0, 0))
    once = pl.Buffered(1)
    matrix = pl.BlockSpec(weights.shape, lambda b: (0, 0), pipeline_mode=once)
    whole = jax.ShapeDtypeStruct(rows.shape, BF)
    return pl.pallas_call(
        functools.partial(expert_kernel, not before, capacity),
        grid=(blocks,),
        out_shape=(
            whole,
            whole,
            jax.ShapeDtypeStruct(lines.shape, F32),
            jax.ShapeDtypeStruct(weights.shape, BF),
        ),
        in_specs=[
            line,
            pl.BlockSpec((1, tokens, 8), lambda b: (b, 0, 0)),
            wide,
            wide,
            matrix,
            *([wide] * len(before)),
        ],
        out_specs=(wide, wide, line, pl.BlockSpec(weights.shape, lambda b: (0, 0))),
        scratch_shapes=[
            pltpu.VMEM(weights.shape, F32),
            pltpu.VMEM((capacity, width), BF),
            pltpu.VMEM((capacity, width), BF),
        ],
        compiler_params=pltpu.CompilerParams(vmem_limit_bytes=58 << 20),
        cost_estimate=pl.CostEstimate(
            flops=blocks * capacity * width * (18 * EFF + 8 * tokens),
            bytes_accessed=blocks * tokens * width * 12,
            transcendentals=0,
        ),
    )(lines, lines.transpose(0, 2, 1), rows, grads, weights, *before)


def mm(a, b, dims, out=F32):
    return lax.dot_general(a, b, (dims, ((), ())), preferred_element_type=out)


def squash_slope(values):
    logistic = jax.nn.sigmoid(values)
    return logistic * (1.0 + values * (1.0 - logistic))


def segment_numbers(lengths, seq_order, positions):
    seq_index = jnp.arange(lengths.shape[1], dtype=jnp.int32)
    picked = (seq_order[:, :, None] == seq_index).astype(jnp.int32)
    placed = jnp.sum(picked * lengths[:, None, :], axis=2)
    earlier = (seq_index[:, None] > seq_index[None, :]).astype(jnp.int32)
    begins = jnp.sum(earlier[None] * placed[:, None, :], axis=2)
    return jnp.sum((begins[:, None, :] <= positions[None, :, None]).astype(jnp.int32), axis=2)


def spread(values):
    return jnp.repeat(values, HEAD_DIM, axis=-1)


def groups_of(seq_count, head_count):
    return [
        [s * head_count + h for s in range(g, g + MEMBERS) for h in range(head_count)]
        for g in range(0, seq_count, MEMBERS)
    ]


def rms_scale(rows):
    return lax.rsqrt(jnp.mean(rows * rows, axis=-1, keepdims=True) + EPSILON)


def norm_back(grad_out, rows, gain, scale):
    weighted = grad_out * gain
    products = jnp.mean(weighted * rows, axis=-1, keepdims=True)
    return scale * weighted - rows * (scale * scale * scale * products)


def to_rows(features):
    count = lax.axis_size("head")
    lead, tokens, width = features.shape
    split = features.reshape(lead, count, tokens // count, width)
    return lax.all_to_all(split, "head", 1, 3, tiled=True)[:, 0]


def to_features(rows):
    count = lax.axis_size("head")
    lead, number, width = rows.shape
    split = rows.reshape(lead, 1, number, width)
    return lax.all_to_all(split, "head", 3, 1, tiled=True).reshape(
        lead, count * number, width // count
    )


def gather_features(features, jobs, arrays, collective_id):
    count = lax.axis_size("head")
    wide = features[0].shape[2] % 128 == 0
    own = [head_job(f.shape[1], f.shape[2], 1, wide) for f in features]
    found = cube_gather(own + jobs, list(features) + arrays, collective_id)
    whole = list(found[: len(own)])
    if not wide:
        whole = [
            w.transpose(0, 2, 1, 3).reshape(w.shape[0], w.shape[2], count * w.shape[3])
            for w in whole
        ]
    return whole, found[len(own) :]


def reduce_rows(partial_rows, collective_id):
    lead, tokens, width = partial_rows.shape
    count = lax.axis_size("head")
    number = tokens // count
    split = partial_rows.reshape(lead, count, number, width)
    return cube_reduce([head_job(number, width, -1)], [split], collective_id)[0]


def gather_group(rows, collective_id):
    lead, number, width = rows.shape
    count = lax.axis_size("head")
    whole = cube_gather([group_job(number, width, 1)], [rows], collective_id)[0]
    return whole.reshape(lead, MEMBERS, count * number, width)


def reduce_group(partial_rows, collective_id):
    lead, members, tokens, width = partial_rows.shape
    count = lax.axis_size("head")
    number = tokens // count
    split = partial_rows.reshape(lead, members * count, number, width)
    return cube_reduce([group_job(number, width, -1)], [split], collective_id)[0]


def slot_in_mesh(s, h):
    return s * lax.axis_size("head") + h


def in_rows(values):
    line = jnp.concatenate([v.reshape(-1) for v in values])
    return jnp.pad(line, (0, -line.shape[0] % 1024)).reshape(1, -1, 128)


def tied(value, *others):
    return lax.optimization_barrier((value, *others))[0]


def lane_padded(matrix):
    return jnp.pad(matrix, ((0, 0), (0, -matrix.shape[1] % 128)))


def body(
    hidden,
    output_grad,
    lengths,
    seq_order,
    routes,
    mix_gain,
    input_proj,
    state_proj,
    step_proj,
    conv_inner,
    conv_state,
    inner_bias,
    state_bias,
    step_bias,
    decay_rate,
    skip_gain,
    gate_gain,
    output_proj,
    moe_gain,
    router,
    expert_up,
    expert_down,
    shared_up,
    shared_down,
):
    seq_count, head_count = lax.axis_size("seq"), lax.axis_size("head")
    seq_rank, head_rank = lax.axis_index("seq"), lax.axis_index("head")
    micro, tokens, local_width = hidden.shape
    inner_local = conv_inner.shape[1]
    heads_local = step_bias.shape[0]
    pairs = heads_local // 2
    experts_local = expert_up.shape[0]
    shared_local = shared_down.shape[0]
    slice_rows = input_proj.shape[1]
    expert_total = experts_local * head_count
    capacity = 2 * tokens * TOPK // expert_total
    own_experts = experts_local // MEMBERS
    member = lax.rem(seq_rank, MEMBERS)
    row_count = tokens // head_count
    channels = inner_local + 2 * STATE
    groups = groups_of(seq_count, head_count)
    seq_groups = [list(range(g, g + MEMBERS)) for g in range(0, seq_count, MEMBERS)]

    first_shard = lane_padded(jnp.concatenate([input_proj[1], state_proj, step_proj], axis=1))
    gain_rows = jnp.pad(jnp.stack([mix_gain, moe_gain])[None], ((0, 0), (0, 6), (0, 0)))
    route_shard = jnp.pad(routes.transpose(0, 2, 1), ((0, 0), (0, 8 - TOPK), (0, 0)))
    (hidden_full, grad_full, gains), (first_full, route_group) = gather_features(
        [hidden, output_grad, gain_rows],
        [seq_job(slice_rows, first_shard.shape[1], 1), members_job(8, tokens)],
        [first_shard[None], route_shard],
        0,
    )
    first_full = first_full.reshape(D, -1)
    gains = gains[0, :2]
    conv_proj, step_full = first_full[:, :channels], first_full[:, channels : channels + heads_local]
    own_rows = partial(
        lax.dynamic_slice_in_dim, start_index=head_rank * row_count, slice_size=row_count, axis=1
    )
    resid_in = own_rows(hidden_full).astype(F32)
    grad_rows = own_rows(grad_full)

    second_shard = jnp.concatenate(
        [
            input_proj[0],
            output_proj.T,
            router,
            shared_up.reshape(slice_rows, 2 * shared_local),
            shared_down.T,
        ],
        axis=1,
    )
    second_full = lax.all_gather(tied(second_shard, first_full), "seq", axis=0, tiled=True)
    cuts = [inner_local, inner_local, expert_total, 2 * shared_local, shared_local]
    cuts = [sum(cuts[: i + 1]) for i in range(4)]
    proj_gate, out_t, router_full, shared_flat, shared_down_t = jnp.split(second_full, cuts, axis=1)
    expert_shard = jnp.concatenate([expert_up, expert_down.transpose(0, 2, 1)], axis=2)
    expert_shard = expert_shard.reshape(MEMBERS, own_experts, slice_rows, 3 * EFF)

    def return_expert(grads, *after):
        send = grads.reshape(seq_count, slice_rows, 3 * EFF)
        return lax.all_to_all(tied(send, *after), "seq", 0, 0, tiled=True)

    def fetch_expert(own, *after):
        send = jnp.tile(expert_shard[:, own], (seq_count // MEMBERS, 1, 1))
        return lax.all_to_all(tied(send, *after), "seq", 0, 0, tiled=True).reshape(D, 3 * EFF)

    hidden_wide = hidden_full.astype(F32)
    scale_mix = rms_scale(hidden_wide)
    normed = (hidden_wide * scale_mix * gains[0]).astype(BF)
    ahead = [(i, i + 1) for i in range(seq_count - 1)]
    behind = [(i + 1, i) for i in range(seq_count - 1)]
    edge = lax.ppermute(normed[:, tokens - EDGE :], "seq", ahead)

    conv_in = mm(normed, conv_proj, ((2,), (0,)))
    edge, conv_in = lax.optimization_barrier((edge, conv_in))
    conv_in = jnp.concatenate([mm(edge, conv_proj, ((2,), (0,))), conv_in], axis=1)
    step_raw = mm(normed, step_full, ((2,), (0,))) + step_bias
    gate_pre = mm(normed, proj_gate, ((2,), (0,)))
    conv_weight = jnp.concatenate([conv_inner, conv_state], axis=1)
    conv_offset = jnp.concatenate([inner_bias, state_bias])
    positions = seq_rank * tokens + jnp.arange(-EDGE, tokens + EDGE, dtype=jnp.int32)
    segment_wide = segment_numbers(lengths, seq_order, positions)
    segments = segment_wide[:, EDGE : EDGE + tokens]
    segment_before = segment_wide[:, EDGE - 1 : EDGE]

    def keep(offset, begin, count):
        now = segment_wide[:, EDGE + begin : EDGE + begin + count]
        return (now == segment_wide[:, EDGE + begin - offset : EDGE + begin - offset + count])[
            :, :, None
        ]

    conv_out = conv_offset + conv_in[:, EDGE:] * conv_weight[0]
    for offset in range(1, CONV):
        shifted = conv_in[:, EDGE - offset : EDGE - offset + tokens]
        conv_out = conv_out + jnp.where(keep(offset, 0, tokens), shifted * conv_weight[offset], 0.0)
    act = jax.nn.silu(conv_out)
    signal, keys = act[:, :, :inner_local], act[:, :, inner_local:]
    step_sizes = jax.nn.softplus(step_raw)
    log_decay = -step_sizes * decay_rate
    row_index = jnp.arange(tokens, dtype=jnp.int32)
    until = (row_index[:, None] <= row_index[None, :]).astype(F32)
    running = jnp.einsum("ji,mjh->mih", until, log_decay, precision=HIGHEST)
    same_start = segments == segment_before
    same_end = segments == segments[:, -1:]
    entry_weight = jnp.where(same_start[:, :, None], jnp.exp(running), 0.0)
    passing = entry_weight[:, -1]
    leave_weight = (
        jnp.where(same_end[:, :, None], jnp.exp(running[:, -1:] - running), 0.0) * step_sizes
    )
    local_state = jnp.einsum(
        "mtc,mtn->mcn", spread(leave_weight) * signal, keys[:, :, :STATE], precision=HIGHEST
    )
    def by_pair(values):
        return values.reshape(micro, tokens, pairs, 2).transpose(0, 2, 1, 3)

    def flag(values):
        return jnp.broadcast_to(
            values.astype(F32)[:, None, :, None], (micro, pairs, tokens, 1)
        )

    cols = jnp.concatenate(
        [
            by_pair(running),
            by_pair(step_sizes),
            flag(segments),
            flag(segment_before),
            jnp.zeros((micro, pairs, tokens, 2), F32),
        ],
        axis=3,
    )
    rows = cols.transpose(0, 1, 3, 2)
    state_in = chain(passing, local_state, 1, 8)
    experts = [fetch_expert(0, state_in)]
    local_out = scan_forward(signal, keys, cols, rows)
    grad_group = lax.all_gather(
        tied(grad_rows, state_in), ("seq", "head"), axis=1, tiled=True, axis_index_groups=groups
    ).reshape(micro, MEMBERS, tokens, D)
    skip_wide, entry_wide = spread(skip_gain), spread(entry_weight)
    from_state = jnp.einsum(
        "mtn,mcn->mtc", keys[:, :, STATE:], state_in, precision=HIGHEST
    )
    mixer_out = local_out + entry_wide * from_state + skip_wide * signal
    gate_act = jax.nn.silu(gate_pre)
    gated = mixer_out * gate_act
    squares = lax.psum(jnp.sum(gated * gated, axis=2), "head")
    scale_gate = lax.rsqrt(squares / INNER + EPSILON)[:, :, None]
    gate_normed = (gated * scale_gate * gate_gain).astype(BF)
    mix_rows = reduce_rows(mm(gate_normed, out_t, ((2,), (1,)), BF), 1)
    resid_mid = resid_in + mix_rows
    scale_moe = rms_scale(resid_mid)
    moe_rows = (resid_mid * scale_moe * gains[1]).astype(BF)
    moe_group = gather_group(moe_rows, 2)

    expert_ids = jnp.arange(expert_total, dtype=jnp.int32)
    experts += [fetch_expert(own, moe_group) for own in range(1, own_experts)]

    def dense_weights(route_lines, rows):
        logits = mm(rows, router_full, ((rows.ndim - 1,), (0,)))
        named = jnp.any(route_lines[..., None] == expert_ids, axis=-3)
        top = jnp.max(jnp.where(named, logits, -jnp.inf), axis=-1, keepdims=True)
        raised = jnp.where(named, jnp.exp(logits - top), 0.0)
        return named, raised / jnp.sum(raised, axis=-1, keepdims=True)

    named_group, weight_group = dense_weights(route_group[:, :, :TOPK], moe_group)
    first_own = head_rank * experts_local + member * own_experts
    def shared_expert(after):
        moe_own = lax.dynamic_index_in_dim(tied(moe_group, after), member, 1, False)
        grad_own = lax.dynamic_index_in_dim(grad_group, member, 1, False)
        shared_both = mm(moe_own, shared_flat, ((2,), (0,)))
        shared_gate, shared_linear = shared_both[..., :shared_local], shared_both[..., shared_local:]
        shared_act = (jax.nn.silu(shared_gate) * shared_linear).astype(BF)
        shared_out = mm(shared_act, shared_down_t, ((2,), (1,)))
        shared_grad_act = mm(grad_own, shared_down_t, ((2,), (0,)))
        shared_grad = jnp.concatenate(
            [
                shared_grad_act * shared_linear * squash_slope(shared_gate),
                shared_grad_act * jax.nn.silu(shared_gate),
            ],
            axis=-1,
        ).astype(BF)
        shared_back = mm(shared_grad, shared_flat, ((2,), (1,)))
        grad_shared_up = mm(moe_own, shared_grad, ((0, 1), (0, 1)), BF)
        grad_shared_down_t = mm(grad_own, shared_act, ((0, 1), (0, 1)), BF)
        return shared_out, shared_back, grad_shared_up, grad_shared_down_t

    blocks = micro * MEMBERS
    sums, expert_grads, weight_grads, expert_backs = (), [], [], []
    for own in range(own_experts):
        chosen = (expert_ids == first_own + own).astype(F32)
        named = jnp.sum(named_group * chosen, axis=-1)
        weight = jnp.sum(weight_group * chosen, axis=-1)
        rank = mm(named.astype(BF), until.astype(BF), ((2,), (0,))) - 1.0
        lines = jnp.stack([jnp.where(named > 0.0, rank, -1.0), weight], axis=2)
        lines = jnp.pad(lines, ((0, 0), (0, 0), (0, 6), (0, 0))).reshape(blocks, 8, tokens)
        *sums, dots, grads = run_expert(
            capacity,
            lines,
            moe_group.reshape(blocks, tokens, D),
            grad_group.reshape(blocks, tokens, D),
            tied(experts[own], *((shared[1], expert_grads[-1]) if own else (moe_group,))),
            tuple(sums),
        )
        weight_grads.append(dots[:, 0].reshape(micro, MEMBERS, tokens))
        expert_grads.append(grads)
        if own == 0:
            shared = shared_expert(sums[1])
    shared_out, shared_back, grad_shared_up, grad_shared_down_t = shared
    ffn_sum, back_sum = [s.reshape(micro, MEMBERS, tokens, D) for s in sums]

    def group_partial(total, own_part):
        mine = lax.dynamic_slice_in_dim(total, member, 1, 1).astype(F32) + own_part[:, None]
        return lax.dynamic_update_slice_in_dim(total, mine.astype(BF), member, 1)

    expert_backs = [return_expert(grads) for grads in expert_grads[:-1]]
    weight_grad = lax.all_to_all(
        tied(jnp.stack(weight_grads, axis=-1), *expert_backs)
        .reshape(micro, MEMBERS * head_count, row_count, own_experts)
        .transpose(1, 0, 2, 3),
        ("seq", "head"),
        0,
        0,
        tiled=True,
        axis_index_groups=groups,
    )
    weight_grad = (
        weight_grad.reshape(MEMBERS, head_count, micro, row_count, own_experts)
        .transpose(2, 3, 1, 0, 4)
        .reshape(micro, row_count, expert_total)
    )
    back_partial = group_partial(back_sum, shared_back)
    back_rows = reduce_group(back_partial, 3)
    ffn_partial = group_partial(ffn_sum, shared_out)
    route_rows = own_rows(routes).transpose(0, 2, 1)
    named_rows, weight_rows = dense_weights(route_rows, moe_rows)
    weight_grad = jnp.where(named_rows, weight_grad, 0.0)
    logit_grad = weight_rows * (
        weight_grad - jnp.sum(weight_rows * weight_grad, axis=-1, keepdims=True)
    )
    logit_grad = logit_grad.astype(BF)
    grad_router = mm(moe_rows, logit_grad, ((0, 1), (0, 1)))
    back_rows = back_rows + mm(logit_grad, router_full, ((2,), (1,)))
    grad_mid = norm_back(back_rows, resid_mid, gains[1], scale_moe) + grad_rows.astype(F32)
    grad_moe_gain = jnp.sum(back_rows * resid_mid * scale_moe, axis=(0, 1))

    grad_mid_low = grad_mid.astype(BF)
    row_dots = jnp.sum(grad_mid_low.astype(F32) * mix_rows, axis=2)
    grad_mix, row_dots = cube_gather(
        [head_job(row_count, D, 1), head_job(8, row_count, 1)],
        [grad_mid_low, jnp.broadcast_to(row_dots[:, None], (micro, 8, row_count))],
        4,
    )
    grad_mix = grad_mix.reshape(micro, tokens, D)
    grad_mid_features = to_features(grad_mid)
    grad_gate_normed = mm(grad_mix, out_t, ((2,), (0,)))
    weighted = grad_gate_normed * gate_gain
    products = row_dots[:, :, 0].reshape(micro, tokens, 1) / scale_gate
    grad_gated = scale_gate * weighted - gated * (
        scale_gate * scale_gate * scale_gate * products / INNER
    )
    grad_gate_gain = jnp.sum(grad_gate_normed * gated * scale_gate, axis=(0, 1))
    grad_mixer = grad_gated * gate_act
    grad_gate_low = (grad_gated * mixer_out * squash_slope(gate_pre)).astype(BF)
    entry_grad = jnp.einsum(
        "mtc,mtn->mcn", entry_wide * grad_mixer, keys[:, :, STATE:], precision=HIGHEST
    )
    grad_out_t = mm(grad_mix, gate_normed, ((0, 1), (0, 1)), BF)
    grad_gate_proj = mm(normed, grad_gate_low, ((0, 1), (0, 1)), BF)
    second_grads = lane_padded(
        jnp.concatenate([grad_gate_proj, grad_out_t, grad_shared_up, grad_shared_down_t], axis=1)
    ).reshape(1, seq_count, slice_rows, -1)
    ffn_partial = ffn_partial.reshape(micro, MEMBERS * head_count, row_count, D)
    ffn_rows, grad_second = cube_reduce(
        [group_job(row_count, D, -1), seq_job(slice_rows, second_grads.shape[3], -1)],
        [tied(ffn_partial, entry_grad), second_grads],
        5,
    )
    grad_gate_in = mm(grad_gate_low, proj_gate, ((2,), (1,)))
    state_grad = chain(passing, tied(entry_grad, ffn_rows), -1, 9)
    output = to_features((resid_mid + ffn_rows).astype(BF))
    expert_backs.append(return_expert(expert_grads[-1], state_grad))
    grad_signal, grad_keys, grad_cols, grad_rows_part = scan_backward(
        signal, keys, cols, rows, grad_mixer, state_in, state_grad
    )
    grad_skip = jnp.sum(
        jnp.sum(grad_mixer * signal, axis=(0, 1)).reshape(heads_local, HEAD_DIM), axis=1
    )
    grad_act = jnp.concatenate([grad_signal + skip_wide * grad_mixer, grad_keys], axis=2)
    small = grad_cols[..., : SEG] + grad_rows_part[:, :, :SEG].transpose(0, 1, 3, 2)

    def by_head(values):
        return values.transpose(0, 2, 1, 3).reshape(micro, tokens, heads_local)

    grad_running, grad_steps = by_head(small[..., RUN:STEP]), by_head(small[..., STEP:SEG])
    grad_log = jnp.einsum("ij,mjh->mih", until, grad_running, precision=HIGHEST)
    grad_decay = -jnp.sum(grad_log * step_sizes, axis=(0, 1))
    grad_step_raw = (grad_steps - grad_log * decay_rate) * jax.nn.sigmoid(step_raw)
    grad_step_bias = jnp.sum(grad_step_raw, axis=(0, 1))
    grad_step_low = grad_step_raw.astype(BF)
    grad_conv = grad_act * squash_slope(conv_out)
    grad_next = jnp.concatenate(
        [grad_conv, lax.ppermute(grad_conv[:, :EDGE], "seq", behind)], axis=1
    )
    grad_conv_offset = jnp.sum(grad_conv, axis=(0, 1))
    grad_pre = grad_conv * conv_weight[0]
    taps = [jnp.sum(grad_conv * conv_in[:, EDGE:], axis=(0, 1))]
    for offset in range(1, CONV):
        shifted = conv_in[:, EDGE - offset : EDGE - offset + tokens]
        taps.append(
            jnp.sum(jnp.where(keep(offset, 0, tokens), grad_conv * shifted, 0.0), axis=(0, 1))
        )
        grad_pre = grad_pre + jnp.where(
            keep(offset, offset, tokens),
            grad_next[:, offset : offset + tokens] * conv_weight[offset],
            0.0,
        )
    grad_conv_weight = jnp.stack(taps)
    grad_pre = grad_pre.astype(BF)

    columns = first_full.shape[1]
    grad_all = jnp.concatenate([grad_pre, grad_step_low], axis=2)
    grad_all = jnp.pad(grad_all, ((0, 0), (0, 0), (0, columns - grad_all.shape[2])))
    grad_first = grad_gate_in + mm(grad_all, first_full, ((2,), (1,)))
    grad_first_sums = lax.psum(jnp.sum(grad_first * gains[0] * hidden_wide, axis=2), "head")
    first_grads = mm(normed, grad_all, ((0, 1), (0, 1)), BF).reshape(
        1, seq_count, slice_rows, columns
    )
    router_grads = lane_padded(grad_router.astype(BF)).reshape(1, seq_count, slice_rows, -1)
    wide = local_width % 128 == 0
    grad_first = grad_first.astype(BF)
    if not wide:
        grad_first = grad_first.reshape(micro, tokens, head_count, local_width)
        grad_first = grad_first.transpose(0, 2, 1, 3)
    first_grads = tied(first_grads, expert_backs[-1])
    first_features, grad_first_w, grad_router_w = cube_reduce(
        [
            head_job(tokens, local_width, -1, wide),
            seq_job(slice_rows, columns, -1),
            seq_job(slice_rows, router_grads.shape[3], -1),
        ],
        [grad_first, first_grads, router_grads],
        6,
    )
    resid_features = hidden.astype(F32)
    grad_in = scale_mix * (first_features * mix_gain) - resid_features * (
        scale_mix * scale_mix * scale_mix * grad_first_sums[:, :, None] / D
    )
    input_grad = grad_in + grad_mid_features
    cuts = [inner_local, inner_local, 2 * shared_local]
    cuts = [sum(cuts[: i + 1]) for i in range(3)]
    gate_w, out_w, shared_up_w, shared_down_w = jnp.split(grad_second[0], cuts + [sum(cuts[-1:]) + shared_local], axis=1)[:4]
    grad_first_w = grad_first_w[0]
    inner_w, step_w = grad_first_w[:, :inner_local], grad_first_w[:, channels : channels + heads_local]
    over_heads = jnp.concatenate(
        [
            grad_first_w[:, inner_local:channels],
            grad_router_w[0, :, :expert_total],
        ],
        axis=1,
    )
    expert_w = jnp.stack(
        [
            jnp.sum(
                back.reshape(seq_count // MEMBERS, MEMBERS, slice_rows, 3 * EFF).astype(F32), axis=0
            )
            for back in expert_backs
        ],
        axis=1,
    ).reshape(experts_local, slice_rows, 3 * EFF)
    own_sizes = [CONV * inner_local, inner_local, inner_local, heads_local, heads_local, heads_local]
    own_small = in_rows(
        [
            grad_conv_weight[:, :inner_local],
            grad_conv_offset[:inner_local],
            grad_gate_gain,
            grad_step_bias,
            grad_decay,
            grad_skip,
            jnp.sum(first_features * resid_features * scale_mix, axis=(0, 1)),
        ]
    )
    all_sizes = [CONV * 2 * STATE, 2 * STATE, D]
    all_small = in_rows(
        [grad_conv_weight[:, inner_local:], grad_conv_offset[inner_local:], grad_moe_gain]
    )
    seq_bits, head_bits = bits_in("seq", seq_count), bits_in("head", head_count)
    over_heads = lane_padded(over_heads)[None]

    def plain_job(array, bits, slot_of):
        return Job([((0, array.shape[1]), (0, array.shape[2]), bits)], slot_of)

    heads_found, own_found, all_found = cube_gather(
        [
            plain_job(over_heads, head_bits, slot_in_head),
            plain_job(own_small, seq_bits, slot_in_seq),
            plain_job(all_small, seq_bits + head_bits, slot_in_mesh),
        ],
        [over_heads, own_small, all_small],
        7,
    )
    over_heads = jnp.sum(heads_found[0], axis=0)
    state_w, router_w = over_heads[:, : 2 * STATE], over_heads[:, 2 * STATE : 2 * STATE + expert_total]

    def taken(found, sizes):
        return jnp.split(jnp.sum(found[0], axis=0).reshape(-1), [sum(sizes[: i + 1]) for i in range(len(sizes))])

    conv_inner_w, inner_bias_w, gate_gain_w, step_bias_w, decay_w, skip_w, mix_gain_w = taken(
        own_found, own_sizes
    )
    conv_state_w, state_bias_w, moe_gain_w, _ = taken(all_found, all_sizes)
    return (
        output,
        input_grad,
        mix_gain_w[:local_width],
        jnp.stack([gate_w, inner_w]),
        state_w,
        step_w,
        conv_inner_w.reshape(CONV, inner_local),
        conv_state_w.reshape(CONV, 2 * STATE),
        inner_bias_w,
        state_bias_w,
        step_bias_w,
        decay_w,
        skip_w,
        gate_gain_w,
        out_w.T,
        lax.dynamic_slice_in_dim(moe_gain_w, head_rank * local_width, local_width, 0),
        router_w,
        expert_w[:, :, : 2 * EFF],
        expert_w[:, :, 2 * EFF :].transpose(0, 2, 1),
        shared_up_w.reshape(slice_rows, 2, shared_local),
        shared_down_w.T,
    )


def solution(mesh):
    return jax.shard_map(
        body,
        mesh=mesh,
        in_specs=(
            P(None, "seq", "head"),
            P(None, "seq", "head"),
            P(),
            P(),
            P(None, "seq", None),
            P("head"),
            P(None, "seq", "head"),
            P("seq", None),
            P("seq", "head"),
            P(None, "head"),
            P(),
            P("head"),
            P(),
            P("head"),
            P("head"),
            P("head"),
            P("head"),
            P("head", "seq"),
            P("head"),
            P("seq", None),
            P("head", "seq", None),
            P("head", None, "seq"),
            P("seq", None, "head"),
            P("head", "seq"),
        ),
        out_specs=(
            P(None, "seq", "head"),
            P(None, "seq", "head"),
            P("head"),
            P(None, "seq", "head"),
            P("seq", None),
            P("seq", "head"),
            P(None, "head"),
            P(),
            P("head"),
            P(),
            P("head"),
            P("head"),
            P("head"),
            P("head"),
            P("head", "seq"),
            P("head"),
            P("seq", None),
            P("head", "seq", None),
            P("head", None, "seq"),
            P("seq", None, "head"),
            P("head", "seq"),
        ),
        check_vma=False,
    )
```

```python
import functools
from functools import partial

import jax
import jax.numpy as jnp
from jax import lax
from jax.experimental import pallas as pl
from jax.experimental.pallas import tpu as pltpu
from jax.sharding import PartitionSpec as P

D = 1536
HEAD_DIM = 64
STATE = 128
CONV = 4
TOPK = 6
EFF = 512
INNER = 3072
MEMBERS = 4
EDGE = 8
CHUNK = 128

EPSILON = 1e-05
HIGHEST = lax.Precision.HIGHEST
BF = jnp.bfloat16
F32 = jnp.float32
MESH = pl.DeviceIdType.MESH

def flips(bits):
    found = [(0, 0)]
    for axis, mask in bits:
        found += [(a ^ (mask * (axis == "seq")), b ^ (mask * (axis == "head"))) for a, b in found]
    return found


def joined(left, right):
    return (left[0] ^ right[0], left[1] ^ right[1])


def flip_of(bit):
    axis, mask = bit
    return (mask, 0) if axis == "seq" else (0, mask)


def toggled(place, mask):
    found, bit = place, 1
    while bit <= mask:
        if mask & bit:
            found = found + bit * (1 - 2 * lax.rem(lax.div(place, bit), 2))
        bit = 2 * bit
    return found


def across(me, masks):
    return (toggled(me[0], masks[0]), toggled(me[1], masks[1]))


def greet(jobs, me):
    bits = sorted({bit for job in jobs for bit in job.parts[0][2]})
    barrier = pltpu.get_barrier_semaphore()
    for bit in bits:
        pl.semaphore_signal(
            barrier, inc=1, device_id=across(me, flip_of(bit)), device_id_type=MESH
        )
    pl.semaphore_wait(barrier, len(bits))


class Job:
    def __init__(self, parts, slot_of, wide=False):
        self.parts, self.slot_of, self.wide = parts, slot_of, wide
        self.depth = len(parts[0][2])
        self.count = 1 << self.depth

    def view(self, ref, place, rows, columns, width):
        slot = self.slot_of(*place)
        if self.wide:
            at = columns[0] + slot * width
            if columns[0] % 128 == 0 and width % 128 == 0:
                at = pl.multiple_of(at, 128)
            return ref.at[:, pl.ds(*rows), pl.ds(at, columns[1])]
        return ref.at[:, slot, pl.ds(*rows), pl.ds(*columns)]

    def whole_shape(self, shape):
        lead, rows, columns = shape
        if self.wide:
            return (lead, rows, self.count * columns)
        return (lead, self.count, rows, columns)


def gather_kernel(jobs, in_turns, *refs):
    me = (lax.axis_index("seq"), lax.axis_index("head"))
    number = len(jobs)
    x_refs, o_refs, sems = refs[:number], refs[number : 2 * number], refs[2 * number :]
    owns, copies, waited = [], {}, set()
    for j in range(number):
        load = pltpu.make_async_copy(x_refs[j], sems[4 * j + 3], sems[4 * j + 2].at[0])
        load.start()
        owns.append(load)
    greet(jobs, me)
    deepest_first = sorted(range(number), key=lambda j: -jobs[j].depth)
    turns = [(0, j) for j in range(number)]
    turns += [(step, j) for j in deepest_first for step in range(1, jobs[j].depth)]
    if in_turns:
        turns.sort()
    for step, j in turns:
        job = jobs[j]
        send_sem, recv_sem, own_sem, own_block = sems[4 * j : 4 * j + 4]
        x_ref, o_ref = x_refs[j], o_refs[j]
        width = x_ref.shape[2]
        for p, (rows, columns, order) in enumerate(job.parts):
            other = flip_of(order[step])
            for place, held in enumerate(flips(order[:step])):
                if place and (j, p, place) not in waited:
                    copies[j, p, place].wait_recv()
                    waited.add((j, p, place))
                dst = job.view(o_ref, across(me, held), rows, columns, width)
                src = dst if place else x_ref.at[:, pl.ds(*rows), pl.ds(*columns)]
                arriving = place + (1 << step)
                copy = pltpu.make_async_remote_copy(
                    src_ref=src,
                    dst_ref=dst,
                    send_sem=send_sem.at[p, arriving],
                    recv_sem=recv_sem.at[p, arriving],
                    device_id=across(me, other),
                    device_id_type=MESH,
                )
                copy.start()
                copies[j, p, arriving] = copy
        if step == 0:
            whole = ((0, x_ref.shape[1]), (0, width))
            owns[j].wait()
            owns[j] = pltpu.make_async_copy(
                own_block, job.view(o_ref, me, *whole, width), own_sem.at[1]
            )
            owns[j].start()
    for key, copy in copies.items():
        if key not in waited:
            copy.wait_recv()
    for copy in copies.values():
        copy.wait_send()
    for own in owns:
        own.wait()


def cube_gather(jobs, arrays, collective_id, in_turns=False, weight=100 << 20):
    anywhere = pl.BlockSpec(memory_space=pl.ANY)
    scratch = []
    for job, x in zip(jobs, arrays, strict=True):
        for shape in ((len(job.parts), job.count),) * 2 + ((2,),):
            scratch.append(pltpu.SemaphoreType.DMA(shape))
        scratch.append(pltpu.VMEM(x.shape, x.dtype))
    return pl.pallas_call(
        functools.partial(gather_kernel, jobs, in_turns),
        out_shape=tuple(
            jax.ShapeDtypeStruct(job.whole_shape(x.shape), x.dtype)
            for job, x in zip(jobs, arrays, strict=True)
        ),
        in_specs=[anywhere] * len(jobs),
        out_specs=(anywhere,) * len(jobs),
        scratch_shapes=scratch,
        compiler_params=pltpu.CompilerParams(
            collective_id=collective_id, has_side_effects=True, vmem_limit_bytes=32 << 20
        ),
        cost_estimate=pl.CostEstimate(flops=0, bytes_accessed=weight, transcendentals=0),
    )(*arrays)


def reduce_kernel(jobs, *refs):
    me = (lax.axis_index("seq"), lax.axis_index("head"))
    number = len(jobs)
    x_refs, o_refs, scratch = refs[:number], refs[number : 2 * number], refs[2 * number :]
    greet(jobs, me)
    loads, flying = {}, {}

    def base(job, step):
        return sum(1 << (job.depth - 1 - i) for i in range(step))

    def send(j, p, step, place):
        job, x_ref = jobs[j], x_refs[j]
        kept, stage, send_sem, recv_sem, own_sem = scratch[5 * j : 5 * j + 5]
        rows, columns, order = job.parts[p]
        other = flip_of(order[step])
        gone = joined(flips(order[step + 1 :])[place], other)
        if step == 0:
            src = job.view(x_ref, across(me, gone), rows, columns, stage.shape[3])
        else:
            source = base(job, step - 1) + flips(order[step:]).index(gone)
            src = stage.at[source, :, pl.ds(*rows), pl.ds(*columns)]
        target = base(job, step) + place
        copy = pltpu.make_async_remote_copy(
            src_ref=src,
            dst_ref=stage.at[target, :, pl.ds(*rows), pl.ds(*columns)],
            send_sem=send_sem.at[p, target],
            recv_sem=recv_sem.at[p, target],
            device_id=across(me, other),
            device_id_type=MESH,
        )
        copy.start()
        flying[j, p, step, place] = copy

    def add(j, p, step, place):
        job, o_ref = jobs[j], o_refs[j]
        kept, stage = scratch[5 * j : 5 * j + 2]
        rows, columns, order = job.parts[p]
        tile = 16 if rows[1] % 16 == 0 else 8
        target = base(job, step) + place
        left = flips(order[step + 1 :])[place]
        source = base(job, step - 1) + flips(order[step:]).index(left) if step else 0

        def one(i, carry):
            here = pl.ds(pl.multiple_of(rows[0] + i * tile, tile), tile)
            for m in range(stage.shape[1]):
                got = stage[target, m, here, pl.ds(*columns)].astype(F32)
                if step == 0:
                    mine = kept[place, m, here, pl.ds(*columns)]
                else:
                    mine = stage[source, m, here, pl.ds(*columns)]
                total = got + mine.astype(F32)
                if step + 1 == job.depth:
                    o_ref[m, here, pl.ds(*columns)] = total
                else:
                    stage[target, m, here, pl.ds(*columns)] = total.astype(stage.dtype)
            return carry

        lax.fori_loop(0, rows[1] // tile, one, 0)

    def sequence(job, p, step):
        order = job.parts[p][2]
        found = flips(order[step + 1 :])
        if step + 1 == job.depth:
            return [0]
        other, later = flip_of(order[step + 1]), flips(order[step + 2 :])
        return [found.index(joined(left, other)) for left in later] + [
            found.index(left) for left in later
        ]

    for j, job in enumerate(jobs):
        for p in range(len(job.parts)):
            for place in sequence(job, p, 0):
                send(j, p, 0, place)
    for j, job in enumerate(jobs):
        kept, stage, send_sem, recv_sem, own_sem = scratch[5 * j : 5 * j + 5]
        for p, (rows, columns, order) in enumerate(job.parts):
            for place, held in enumerate(flips(order[1:])):
                load = pltpu.make_async_copy(
                    job.view(x_refs[j], across(me, held), rows, columns, stage.shape[3]),
                    kept.at[place, :, pl.ds(*rows), pl.ds(*columns)],
                    own_sem.at[p, place],
                )
                load.start()
                loads[j, p, place] = load
    for step in range(max(job.depth for job in jobs)):
        for j, job in enumerate(jobs):
            if step >= job.depth:
                continue
            for p, (rows, columns, order) in enumerate(job.parts):
                places = sequence(job, p, step)
                for at, place in enumerate(places):
                    if step == 0:
                        loads[j, p, place].wait()
                    flying[j, p, step, place].wait_recv()
                    add(j, p, step, place)
                    if step + 1 < job.depth and at < len(places) // 2:
                        send(j, p, step + 1, at)
    for copy in flying.values():
        copy.wait_send()


def cube_reduce(jobs, arrays, collective_id, weight=100 << 20):
    out_shape, scratch = [], []
    for job, x in zip(jobs, arrays, strict=True):
        if job.wide:
            lead, rows, columns = x.shape[0], x.shape[1], x.shape[2] // job.count
        else:
            lead, _, rows, columns = x.shape
        out_shape.append(jax.ShapeDtypeStruct((lead, rows, columns), F32))
        scratch += [
            pltpu.VMEM((job.count // 2, lead, rows, columns), x.dtype),
            pltpu.VMEM((job.count - 1, lead, rows, columns), x.dtype),
            pltpu.SemaphoreType.DMA((len(job.parts), job.count - 1)),
            pltpu.SemaphoreType.DMA((len(job.parts), job.count - 1)),
            pltpu.SemaphoreType.DMA((len(job.parts), job.count // 2)),
        ]
    return pl.pallas_call(
        functools.partial(reduce_kernel, jobs),
        out_shape=tuple(out_shape),
        in_specs=[pl.BlockSpec(memory_space=pl.ANY)] * len(jobs),
        out_specs=(pl.BlockSpec(memory_space=pltpu.VMEM),) * len(jobs),
        scratch_shapes=scratch,
        compiler_params=pltpu.CompilerParams(
            collective_id=collective_id, has_side_effects=True, vmem_limit_bytes=52 << 20
        ),
        cost_estimate=pl.CostEstimate(flops=0, bytes_accessed=weight, transcendentals=0),
    )(*arrays)


def bits_in(axis, size):
    return [(axis, 1 << i) for i in range(size.bit_length() - 1)]


def thirds(rows, columns):
    if columns % 384:
        return [((0, rows), (0, columns))]
    third = columns // 3
    return [((0, rows), (i * third, third)) for i in range(3)]


def slot_in_head(s, h):
    return h


def slot_in_seq(s, h):
    return s


def slot_in_members(s, h):
    return lax.rem(s, MEMBERS)


def slot_in_group(s, h):
    return lax.rem(s, MEMBERS) * lax.axis_size("head") + h


def group_job(rows, columns, way):
    core = ("head", 1)
    links = bits_in("head", lax.axis_size("head"))[1:] + bits_in("seq", MEMBERS)
    parts = []
    for i, (r, c) in enumerate(thirds(rows, columns)):
        turned = links[i:] + links[:i]
        parts.append((r, c, (turned + [core])[::way]))
    return Job(parts, slot_in_group)


def head_job(rows, columns, way, wide=False):
    bits = bits_in("head", lax.axis_size("head"))
    order = (bits[1:] + bits[:1])[::way]
    return Job([(r, c, order) for r, c in thirds(rows, columns)], slot_in_head, wide)


def seq_job(rows, columns, way):
    bits = bits_in("seq", lax.axis_size("seq"))
    cut = rows * 7 // 12 // 16 * 16
    parts = []
    for _, some in thirds(rows, columns):
        parts.append(((0, cut), some, bits[::-1][::way]))
        parts.append(((cut, rows - cut), some, (bits[:1] + bits[:0:-1])[::way]))
    return Job(parts, slot_in_seq)


def members_job(rows, columns):
    return Job([((0, rows), (0, columns), bits_in("seq", MEMBERS))], slot_in_members)


def chain_kernel(way, widths, state_ref, pass_ref, out_ref, far, far_pass, low, near_pass, sems):
    count = lax.axis_size("seq")
    me, head = lax.axis_index("seq"), lax.axis_index("head")
    micro, heads = pass_ref.shape[0], pass_ref.shape[1]
    place = me if way == 1 else count - 1 - me
    barrier = pltpu.get_barrier_semaphore()
    expected = 0
    for width in sorted(set(widths)):
        for there, steps in ((place + width < count, width), (place >= width, -width)):
            expected = expected + there.astype(jnp.int32)

            @pl.when(there)
            def _():
                pl.semaphore_signal(
                    barrier, inc=1, device_id=(me + way * steps, head), device_id_type=MESH
                )

    pl.semaphore_wait(barrier, expected)

    def rows_of(h):
        return pl.ds(h * HEAD_DIM, HEAD_DIM)

    low[0] = state_ref[...].astype(BF)
    near_pass[0] = pass_ref[...]
    for hop, width in enumerate(widths):
        sends, gets = place + width < count, place >= width
        copies = [
            pltpu.make_async_remote_copy(
                src_ref=src.at[hop],
                dst_ref=dst.at[hop],
                send_sem=sems.at[0, i, hop],
                recv_sem=sems.at[1, i, hop],
                device_id=(me + way * width, head),
                device_id_type=MESH,
            )
            for i, (src, dst) in enumerate(((low, far), (near_pass, far_pass)))
        ]

        @pl.when(sends)
        def _():
            for copy in copies:
                copy.start()

        @pl.when(gets)
        def _():
            for copy in copies:
                copy.wait_recv()
            for m in range(micro):
                for h in range(heads):
                    got = far[hop, m, rows_of(h), :].astype(F32)
                    if hop:
                        near = near_pass[hop, m, h : h + 1, :]
                        got = out_ref[m, rows_of(h), :] + near * got
                    out_ref[m, rows_of(h), :] = got
                    if hop + 1 < len(widths):
                        low[hop + 1, m, rows_of(h), :] = got.astype(BF)
            if hop + 1 < len(widths):
                passed = far_pass[hop]
                near_pass[hop + 1] = passed * near_pass[hop] if hop else passed

        @pl.when(jnp.logical_not(gets))
        def _():
            if hop == 0:
                out_ref[...] = jnp.zeros_like(out_ref)
            if hop + 1 < len(widths):
                low[hop + 1] = out_ref[...].astype(BF)
                near_pass[hop + 1] = jnp.zeros_like(pass_ref)

        @pl.when(sends)
        def _():
            for copy in copies:
                copy.wait_send()


def chain(passing, state, way, collective_id):
    count = lax.axis_size("seq")
    widths, covered = [1], 1
    while covered < count - 1:
        widths.append(covered)
        covered = 2 * covered
    hops = len(widths)
    lines = jnp.broadcast_to(passing[:, :, None], passing.shape + (STATE,))
    vmem = pl.BlockSpec(memory_space=pltpu.VMEM)
    return pl.pallas_call(
        functools.partial(chain_kernel, way, widths),
        out_shape=jax.ShapeDtypeStruct(state.shape, F32),
        in_specs=[vmem, vmem],
        out_specs=vmem,
        scratch_shapes=[
            pltpu.VMEM((hops,) + state.shape, BF),
            pltpu.VMEM((hops,) + lines.shape, F32),
            pltpu.VMEM((hops,) + state.shape, BF),
            pltpu.VMEM((hops,) + lines.shape, F32),
            pltpu.SemaphoreType.DMA((2, 2, hops)),
        ],
        compiler_params=pltpu.CompilerParams(
            collective_id=collective_id, has_side_effects=True, vmem_limit_bytes=32 << 20
        ),
        cost_estimate=pl.CostEstimate(flops=0, bytes_accessed=100 << 20, transcendentals=0),
    )(state, lines)


RUN, STEP, SEG = 0, 2, 4


def dot(a, b, dims):
    return lax.dot_general(
        a.astype(BF), b.astype(BF), (dims, ((), ())), preferred_element_type=F32
    )


def split_low(a):
    high = a.astype(BF)
    return high, (a - high.astype(F32)).astype(BF)


def dot_fine(a, b, dims):
    (a_high, a_low), (b_high, b_low) = split_low(a), split_low(b)
    return dot(a_high, b_high, dims) + (dot(a_high, b_low, dims) + dot(a_low, b_high, dims))


NN = ((1,), (0,))
NT = ((1,), (1,))
TN = ((0,), (0,))


def chunk_parts(cols_ref, rows_ref, begin):
    here = pl.ds(begin, CHUNK)
    cols, rows = cols_ref[0, 0, here, :], rows_ref[0, 0, :, here]
    last = slice(CHUNK - 1, CHUNK)
    seg_c, seg_r, seg_end = cols[:, SEG : SEG + 1], rows[SEG : SEG + 1], cols[last, SEG : SEG + 1]
    if begin:
        before = cols_ref[0, 0, pl.ds(begin - 8, 8), :][7:8]
        seg_before, run_before = before[:, SEG : SEG + 1], [before[:, RUN + k : RUN + k + 1] for k in range(2)]
    else:
        seg_before, run_before = cols[:1, SEG + 1 : SEG + 2], [jnp.zeros((1, 1), F32)] * 2
    row = lax.broadcasted_iota(jnp.int32, (CHUNK, CHUNK), 0)
    column = lax.broadcasted_iota(jnp.int32, (CHUNK, CHUNK), 1)
    within = (row >= column) & (seg_c == seg_r)
    heads = []
    for k in range(2):
        run_c, run_r = cols[:, RUN + k : RUN + k + 1], rows[RUN + k : RUN + k + 1]
        run_end = run_c[CHUNK - 1 :]
        decay = jnp.where(within, jnp.exp(jnp.where(within, run_c - run_r, 0.0)), 0.0)
        enter = jnp.where(seg_c == seg_before, jnp.exp(run_c - run_before[k]), 0.0)
        leave = jnp.where(seg_c == seg_end, jnp.exp(run_end - run_c), 0.0)
        through = jnp.where(seg_end == seg_before, jnp.exp(run_end - run_before[k]), 0.0)
        heads.append((decay, enter, leave, through, cols[:, STEP + k : STEP + k + 1], rows[STEP + k : STEP + k + 1]))
    return heads


def of_pair(first, second, axis):
    shape = (first.shape[0], 2 * HEAD_DIM) if axis == 1 else (2 * HEAD_DIM, first.shape[1])
    return jnp.where(
        lax.broadcasted_iota(jnp.int32, shape, axis) < HEAD_DIM,
        jnp.broadcast_to(first, shape),
        jnp.broadcast_to(second, shape),
    )


def halves(value):
    low = lax.broadcasted_iota(jnp.int32, value.shape, 1) < HEAD_DIM
    return jnp.where(low, value, 0.0), jnp.where(low, 0.0, value)


def forward_kernel(x_ref, keys_ref, cols_ref, rows_ref, y_ref):
    state = jnp.zeros((2 * HEAD_DIM, STATE), F32)
    tokens = x_ref.shape[1]
    for begin in range(0, tokens, CHUNK):
        here = pl.ds(begin, CHUNK)
        x, write, read = x_ref[0, here, :], keys_ref[0, here, :STATE], keys_ref[0, here, STATE:]
        heads = chunk_parts(cols_ref, rows_ref, begin)
        scores = dot_fine(read, write, NT)
        split = halves(x)
        y = 0.0
        for k, (decay, enter, leave, through, step_c, step_r) in enumerate(heads):
            y = y + dot_fine(scores * decay * step_r, split[k], NN)
        if begin:
            y = y + of_pair(heads[0][1], heads[1][1], 1) * dot_fine(read, state, NT)
        y_ref[0, here, :] = y
        if begin + CHUNK < tokens:
            keep = of_pair(heads[0][2] * heads[0][4], heads[1][2] * heads[1][4], 1)
            state = of_pair(heads[0][3], heads[1][3], 0) * state + dot_fine(
                keep * x, write, TN
            )


def scan_forward(x, keys, cols, rows):
    micro, tokens, width = x.shape
    pairs = width // (2 * HEAD_DIM)
    wide = pl.BlockSpec((1, tokens, 2 * HEAD_DIM), lambda m, p: (m, 0, p))
    return pl.pallas_call(
        forward_kernel,
        grid=(micro, pairs),
        out_shape=jax.ShapeDtypeStruct((micro, tokens, width), F32),
        in_specs=[
            wide,
            pl.BlockSpec((1, tokens, 2 * STATE), lambda m, p: (m, 0, 0)),
            pl.BlockSpec((1, 1, tokens, 8), lambda m, p: (m, p, 0, 0)),
            pl.BlockSpec((1, 1, 8, tokens), lambda m, p: (m, p, 0, 0)),
        ],
        out_specs=wide,
        compiler_params=pltpu.CompilerParams(vmem_limit_bytes=32 << 20),
        cost_estimate=pl.CostEstimate(
            flops=micro * pairs * tokens * CHUNK * 2 * 700, bytes_accessed=micro * tokens * width * 12, transcendentals=0
        ),
    )(x, keys, cols, rows)


def backward_kernel(
    x_ref, keys_ref, cols_ref, rows_ref, dy_ref, state_ref, next_ref,
    dx_ref, dkeys_ref, dcols_ref, drows_ref, states
):
    tokens = x_ref.shape[1]
    chunks = tokens // CHUNK
    pair = pl.program_id(1)

    @pl.when(pair == 0)
    def _():
        dkeys_ref[...] = jnp.zeros_like(dkeys_ref)

    state = state_ref[0]
    for c in range(chunks):
        states[c] = state
        if c + 1 < chunks:
            here = pl.ds(c * CHUNK, CHUNK)
            heads = chunk_parts(cols_ref, rows_ref, c * CHUNK)
            keep = of_pair(heads[0][2] * heads[0][4], heads[1][2] * heads[1][4], 1)
            state = of_pair(heads[0][3], heads[1][3], 0) * state + dot_fine(
                keep * x_ref[0, here, :], keys_ref[0, here, :STATE], TN
            )
    later = next_ref[0]
    pending = [jnp.zeros((1, 1), F32)] * 2
    end_row = lax.broadcasted_iota(jnp.int32, (CHUNK, 1), 0) == CHUNK - 1
    lane8 = lax.broadcasted_iota(jnp.int32, (CHUNK, 8), 1)
    sub8 = lax.broadcasted_iota(jnp.int32, (8, CHUNK), 0)
    for c in reversed(range(chunks)):
        begin = c * CHUNK
        here = pl.ds(begin, CHUNK)
        x, write, read = x_ref[0, here, :], keys_ref[0, here, :STATE], keys_ref[0, here, STATE:]
        dy = dy_ref[0, here, :]
        state = states[c]
        heads = chunk_parts(cols_ref, rows_ref, begin)
        scores = dot_fine(read, write, NT)
        x_split, dy_split = halves(x), halves(dy)
        enter = of_pair(heads[0][1], heads[1][1], 1)
        leave = of_pair(heads[0][2], heads[1][2], 1)
        step = of_pair(heads[0][4], heads[1][4], 1)
        through = of_pair(heads[0][3], heads[1][3], 0)
        entered = enter * dy
        kept = leave * step * x
        from_later = dot_fine(write, later, NT)
        dx = leave * step * from_later
        dread = dot_fine(entered, state, NN)
        dwrite = dot_fine(kept, later, NN)
        weight_grad = halves(from_later * x)
        entry_grad = halves(entered * dot_fine(read, state, NT))
        kept_state = later * state * through
        dscores = 0.0
        dcols = jnp.zeros((CHUNK, 8), F32)
        drows = jnp.zeros((8, CHUNK), F32)
        for k, (decay, _, leave_k, through_k, step_c, step_r) in enumerate(heads):
            products = dot_fine(dy, x_split[k], NT)
            weighted = products * decay
            dx = dx + dot(scores * decay * step_r, dy_split[k], TN)
            dscores = dscores + weighted * step_r
            q = weighted * scores
            r = q * step_r
            dw = jnp.sum(weight_grad[k], axis=1, keepdims=True) * leave_k
            de = jnp.sum(entry_grad[k], axis=1, keepdims=True)
            drun = jnp.sum(r, axis=1, keepdims=True) + de - dw * step_c
            half = slice(k * HEAD_DIM, (k + 1) * HEAD_DIM)
            passed = jnp.sum(jnp.sum(kept_state[half], axis=1, keepdims=True), axis=0, keepdims=True)
            at_end = passed + jnp.sum(dw * step_c, axis=0, keepdims=True) + pending[k]
            pending[k] = -passed - jnp.sum(de, axis=0, keepdims=True)
            drun = drun + jnp.where(end_row, at_end, 0.0)
            dcols = dcols + jnp.where(lane8 == RUN + k, drun, 0.0) + jnp.where(lane8 == STEP + k, dw, 0.0)
            q_sum = jnp.sum(q, axis=0, keepdims=True)
            drows = drows + jnp.where(sub8 == STEP + k, q_sum, 0.0)
            drows = drows + jnp.where(sub8 == RUN + k, -q_sum * step_r, 0.0)
        dread = dread + dot_fine(dscores, write, NN)
        dwrite = dwrite + dot_fine(dscores, read, TN)
        later = through * later + dot_fine(entered, read, TN)
        dx_ref[0, here, :] = dx
        dkeys_ref[0, here, :STATE] += dwrite
        dkeys_ref[0, here, STATE:] += dread
        dcols_ref[0, 0, here, :] = dcols
        drows_ref[0, 0, :, here] = drows


def scan_backward(x, keys, cols, rows, dy, state, later):
    micro, tokens, width = x.shape
    pairs = width // (2 * HEAD_DIM)
    wide = pl.BlockSpec((1, tokens, 2 * HEAD_DIM), lambda m, p: (m, 0, p))
    key = pl.BlockSpec((1, tokens, 2 * STATE), lambda m, p: (m, 0, 0))
    col = pl.BlockSpec((1, 1, tokens, 8), lambda m, p: (m, p, 0, 0))
    row = pl.BlockSpec((1, 1, 8, tokens), lambda m, p: (m, p, 0, 0))
    hold = pl.BlockSpec((1, 2 * HEAD_DIM, STATE), lambda m, p: (m, p, 0))
    return pl.pallas_call(
        backward_kernel,
        grid=(micro, pairs),
        out_shape=(
            jax.ShapeDtypeStruct(x.shape, F32),
            jax.ShapeDtypeStruct(keys.shape, F32),
            jax.ShapeDtypeStruct(cols.shape, F32),
            jax.ShapeDtypeStruct(rows.shape, F32),
        ),
        in_specs=[wide, key, col, row, wide, hold, hold],
        out_specs=(wide, key, col, row),
        scratch_shapes=[pltpu.VMEM((tokens // CHUNK, 2 * HEAD_DIM, STATE), F32)],
        compiler_params=pltpu.CompilerParams(vmem_limit_bytes=32 << 20),
    )(x, keys, cols, rows, dy, state, later)


TILE = 512


def expert_kernel(first, capacity, lines_ref, cols_ref, rows_ref, grads_ref, weights_ref, *refs):
    before, refs = ((), refs) if first else (refs[:2], refs[2:])
    ffn_ref, back_ref, dots_ref, sums_ref, total, picked, given = refs
    tokens, width = rows_ref.shape[1], rows_ref.shape[2]
    block = pl.program_id(0)

    @pl.when(block == 0)
    def _():
        total[...] = jnp.zeros_like(total)

    slot = lax.broadcasted_iota(jnp.int32, (capacity, tokens), 0).astype(F32)
    pick = slot == lines_ref[0, 0:1, :]
    slots = jnp.where(pick, 1.0, 0.0).astype(BF)
    slot = lax.broadcasted_iota(jnp.int32, (tokens, capacity), 1).astype(F32)
    places = jnp.where(slot == cols_ref[0, :, 0:1], 1.0, 0.0).astype(BF)
    share = jnp.sum(jnp.where(pick, lines_ref[0, 1:2, :], 0.0), axis=1, keepdims=True)
    tiles = [slice(i, i + TILE) for i in range(0, width, TILE)]
    for tile in tiles:
        picked[:, tile] = dot(slots, rows_ref[0, :, tile], NN).astype(BF)
        given[:, tile] = dot(slots, grads_ref[0, :, tile], NN).astype(BF)
    both = dot(picked[...], weights_ref[:, : 2 * EFF], NN)
    gate, linear = both[:, :EFF], both[:, EFF:]
    logistic = jax.nn.sigmoid(gate)
    silu = gate * logistic
    act = (silu * linear).astype(BF)
    act_grad, made_dot = 0.0, 0.0
    for tile in tiles:
        down = weights_ref[tile, 2 * EFF :]
        made = dot(act, down, NT)
        grad = given[:, tile].astype(F32)
        made_dot = made_dot + jnp.sum(grad * made, axis=1, keepdims=True)
        out = dot(places, made * share, NN)
        if not first:
            out = out + before[0][0, :, tile].astype(F32)
        ffn_ref[0, :, tile] = out.astype(BF)
        grad = (grad * share).astype(BF)
        act_grad = act_grad + dot(grad, down, NN)
        total[tile, 2 * EFF :] += dot(grad, act, TN)
    dots = jnp.sum(jnp.where(pick, made_dot, 0.0), axis=0, keepdims=True)
    dots_ref[0] = jnp.broadcast_to(dots, dots_ref.shape[1:])
    both_grad = jnp.concatenate(
        [act_grad * linear * (logistic * (1.0 + gate * (1.0 - logistic))), act_grad * silu], axis=1
    ).astype(BF)
    for tile in tiles:
        back = dot(both_grad, weights_ref[tile, : 2 * EFF], NT)
        out = dot(places, back, NN)
        if not first:
            out = out + before[1][0, :, tile].astype(F32)
        back_ref[0, :, tile] = out.astype(BF)
        total[tile, : 2 * EFF] += dot(picked[:, tile], both_grad, TN)

    @pl.when(block == pl.num_programs(0) - 1)
    def _():
        for tile in tiles:
            sums_ref[tile, :] = total[tile, :].astype(BF)


def run_expert(capacity, lines, rows, grads, weights, before):
    blocks, tokens, width = rows.shape
    line = pl.BlockSpec((1, 8, tokens), lambda b: (b, 0, 0))
    wide = pl.BlockSpec((1, tokens, width), lambda b: (b, 0, 0))
    once = pl.Buffered(1)
    matrix = pl.BlockSpec(weights.shape, lambda b: (0, 0), pipeline_mode=once)
    whole = jax.ShapeDtypeStruct(rows.shape, BF)
    return pl.pallas_call(
        functools.partial(expert_kernel, not before, capacity),
        grid=(blocks,),
        out_shape=(
            whole,
            whole,
            jax.ShapeDtypeStruct(lines.shape, F32),
            jax.ShapeDtypeStruct(weights.shape, BF),
        ),
        in_specs=[
            line,
            pl.BlockSpec((1, tokens, 8), lambda b: (b, 0, 0)),
            wide,
            wide,
            matrix,
            *([wide] * len(before)),
        ],
        out_specs=(wide, wide, line, pl.BlockSpec(weights.shape, lambda b: (0, 0))),
        scratch_shapes=[
            pltpu.VMEM(weights.shape, F32),
            pltpu.VMEM((capacity, width), BF),
            pltpu.VMEM((capacity, width), BF),
        ],
        compiler_params=pltpu.CompilerParams(vmem_limit_bytes=58 << 20),
        cost_estimate=pl.CostEstimate(
            flops=blocks * capacity * width * (18 * EFF + 8 * tokens),
            bytes_accessed=blocks * tokens * width * 12,
            transcendentals=0,
        ),
    )(lines, lines.transpose(0, 2, 1), rows, grads, weights, *before)


def mm(a, b, dims, out=F32):
    return lax.dot_general(a, b, (dims, ((), ())), preferred_element_type=out)


def squash_slope(values):
    logistic = jax.nn.sigmoid(values)
    return logistic * (1.0 + values * (1.0 - logistic))


def segment_numbers(lengths, seq_order, positions):
    seq_index = jnp.arange(lengths.shape[1], dtype=jnp.int32)
    picked = (seq_order[:, :, None] == seq_index).astype(jnp.int32)
    placed = jnp.sum(picked * lengths[:, None, :], axis=2)
    earlier = (seq_index[:, None] > seq_index[None, :]).astype(jnp.int32)
    begins = jnp.sum(earlier[None] * placed[:, None, :], axis=2)
    return jnp.sum((begins[:, None, :] <= positions[None, :, None]).astype(jnp.int32), axis=2)


def spread(values):
    return jnp.repeat(values, HEAD_DIM, axis=-1)


def groups_of(seq_count, head_count):
    return [
        [s * head_count + h for s in range(g, g + MEMBERS) for h in range(head_count)]
        for g in range(0, seq_count, MEMBERS)
    ]


def rms_scale(rows):
    return lax.rsqrt(jnp.mean(rows * rows, axis=-1, keepdims=True) + EPSILON)


def norm_back(grad_out, rows, gain, scale):
    weighted = grad_out * gain
    products = jnp.mean(weighted * rows, axis=-1, keepdims=True)
    return scale * weighted - rows * (scale * scale * scale * products)


def to_rows(features):
    count = lax.axis_size("head")
    lead, tokens, width = features.shape
    split = features.reshape(lead, count, tokens // count, width)
    return lax.all_to_all(split, "head", 1, 3, tiled=True)[:, 0]


def to_features(rows):
    count = lax.axis_size("head")
    lead, number, width = rows.shape
    split = rows.reshape(lead, 1, number, width)
    return lax.all_to_all(split, "head", 3, 1, tiled=True).reshape(
        lead, count * number, width // count
    )


def gather_features(features, jobs, arrays, collective_id):
    count = lax.axis_size("head")
    wide = features[0].shape[2] % 128 == 0
    own = [head_job(f.shape[1], f.shape[2], 1, wide) for f in features]
    found = cube_gather(own + jobs, list(features) + arrays, collective_id)
    whole = list(found[: len(own)])
    if not wide:
        whole = [
            w.transpose(0, 2, 1, 3).reshape(w.shape[0], w.shape[2], count * w.shape[3])
            for w in whole
        ]
    return whole, found[len(own) :]


def reduce_rows(partial_rows, collective_id):
    lead, tokens, width = partial_rows.shape
    count = lax.axis_size("head")
    number = tokens // count
    split = partial_rows.reshape(lead, count, number, width)
    return cube_reduce([head_job(number, width, -1)], [split], collective_id)[0]


def gather_group(rows, collective_id):
    lead, number, width = rows.shape
    count = lax.axis_size("head")
    whole = cube_gather([group_job(number, width, 1)], [rows], collective_id)[0]
    return whole.reshape(lead, MEMBERS, count * number, width)


def reduce_group(partial_rows, collective_id):
    lead, members, tokens, width = partial_rows.shape
    count = lax.axis_size("head")
    number = tokens // count
    split = partial_rows.reshape(lead, members * count, number, width)
    return cube_reduce([group_job(number, width, -1)], [split], collective_id)[0]


def slot_in_mesh(s, h):
    return s * lax.axis_size("head") + h


def in_rows(values):
    line = jnp.concatenate([v.reshape(-1) for v in values])
    return jnp.pad(line, (0, -line.shape[0] % 1024)).reshape(1, -1, 128)


def tied(value, *others):
    return lax.optimization_barrier((value, *others))[0]


def lane_padded(matrix):
    return jnp.pad(matrix, ((0, 0), (0, -matrix.shape[1] % 128)))


def body(
    hidden,
    output_grad,
    lengths,
    seq_order,
    routes,
    mix_gain,
    input_proj,
    state_proj,
    step_proj,
    conv_inner,
    conv_state,
    inner_bias,
    state_bias,
    step_bias,
    decay_rate,
    skip_gain,
    gate_gain,
    output_proj,
    moe_gain,
    router,
    expert_up,
    expert_down,
    shared_up,
    shared_down,
):
    seq_count, head_count = lax.axis_size("seq"), lax.axis_size("head")
    seq_rank, head_rank = lax.axis_index("seq"), lax.axis_index("head")
    micro, tokens, local_width = hidden.shape
    inner_local = conv_inner.shape[1]
    heads_local = step_bias.shape[0]
    pairs = heads_local // 2
    experts_local = expert_up.shape[0]
    shared_local = shared_down.shape[0]
    slice_rows = input_proj.shape[1]
    expert_total = experts_local * head_count
    capacity = 2 * tokens * TOPK // expert_total
    own_experts = experts_local // MEMBERS
    member = lax.rem(seq_rank, MEMBERS)
    row_count = tokens // head_count
    channels = inner_local + 2 * STATE
    groups = groups_of(seq_count, head_count)
    seq_groups = [list(range(g, g + MEMBERS)) for g in range(0, seq_count, MEMBERS)]

    first_shard = lane_padded(jnp.concatenate([input_proj[1], state_proj, step_proj], axis=1))
    gain_rows = jnp.pad(jnp.stack([mix_gain, moe_gain])[None], ((0, 0), (0, 6), (0, 0)))
    route_shard = jnp.pad(routes.transpose(0, 2, 1), ((0, 0), (0, 8 - TOPK), (0, 0)))
    (hidden_full, grad_full, gains), (first_full, route_group) = gather_features(
        [hidden, output_grad, gain_rows],
        [seq_job(slice_rows, first_shard.shape[1], 1), members_job(8, tokens)],
        [first_shard[None], route_shard],
        0,
    )
    first_full = first_full.reshape(D, -1)
    gains = gains[0, :2]
    conv_proj, step_full = first_full[:, :channels], first_full[:, channels : channels + heads_local]
    own_rows = partial(
        lax.dynamic_slice_in_dim, start_index=head_rank * row_count, slice_size=row_count, axis=1
    )
    resid_in = own_rows(hidden_full).astype(F32)
    grad_rows = own_rows(grad_full)

    second_shard = jnp.concatenate([input_proj[0], output_proj.T, router], axis=1)
    second_full = lax.all_gather(tied(second_shard, first_full), "seq", axis=0, tiled=True)
    proj_gate, out_t, router_full = jnp.split(second_full, [inner_local, 2 * inner_local], axis=1)
    expert_shard = jnp.concatenate([expert_up, expert_down.transpose(0, 2, 1)], axis=2)
    expert_shard = expert_shard.reshape(MEMBERS, own_experts, slice_rows, 3 * EFF)

    def return_expert(grads, *after):
        send = grads.reshape(seq_count, slice_rows, 3 * EFF)
        return lax.all_to_all(tied(send, *after), "seq", 0, 0, tiled=True)

    def fetch_expert(own, *after):
        send = jnp.tile(expert_shard[:, own], (seq_count // MEMBERS, 1, 1))
        return lax.all_to_all(tied(send, *after), "seq", 0, 0, tiled=True).reshape(D, 3 * EFF)

    hidden_wide = hidden_full.astype(F32)
    scale_mix = rms_scale(hidden_wide)
    normed = (hidden_wide * scale_mix * gains[0]).astype(BF)
    ahead = [(i, i + 1) for i in range(seq_count - 1)]
    behind = [(i + 1, i) for i in range(seq_count - 1)]
    edge = lax.ppermute(normed[:, tokens - EDGE :], "seq", ahead)

    conv_in = mm(normed, conv_proj, ((2,), (0,)))
    edge, conv_in = lax.optimization_barrier((edge, conv_in))
    conv_in = jnp.concatenate([mm(edge, conv_proj, ((2,), (0,))), conv_in], axis=1)
    step_raw = mm(normed, step_full, ((2,), (0,))) + step_bias
    gate_pre = mm(normed, proj_gate, ((2,), (0,)))
    conv_weight = jnp.concatenate([conv_inner, conv_state], axis=1)
    conv_offset = jnp.concatenate([inner_bias, state_bias])
    positions = seq_rank * tokens + jnp.arange(-EDGE, tokens + EDGE, dtype=jnp.int32)
    segment_wide = segment_numbers(lengths, seq_order, positions)
    segments = segment_wide[:, EDGE : EDGE + tokens]
    segment_before = segment_wide[:, EDGE - 1 : EDGE]

    def keep(offset, begin, count):
        now = segment_wide[:, EDGE + begin : EDGE + begin + count]
        return (now == segment_wide[:, EDGE + begin - offset : EDGE + begin - offset + count])[
            :, :, None
        ]

    conv_out = conv_offset + conv_in[:, EDGE:] * conv_weight[0]
    for offset in range(1, CONV):
        shifted = conv_in[:, EDGE - offset : EDGE - offset + tokens]
        conv_out = conv_out + jnp.where(keep(offset, 0, tokens), shifted * conv_weight[offset], 0.0)
    act = jax.nn.silu(conv_out)
    signal, keys = act[:, :, :inner_local], act[:, :, inner_local:]
    step_sizes = jax.nn.softplus(step_raw)
    log_decay = -step_sizes * decay_rate
    row_index = jnp.arange(tokens, dtype=jnp.int32)
    until = (row_index[:, None] <= row_index[None, :]).astype(F32)
    running = jnp.einsum("ji,mjh->mih", until, log_decay, precision=HIGHEST)
    same_start = segments == segment_before
    same_end = segments == segments[:, -1:]
    entry_weight = jnp.where(same_start[:, :, None], jnp.exp(running), 0.0)
    passing = entry_weight[:, -1]
    leave_weight = (
        jnp.where(same_end[:, :, None], jnp.exp(running[:, -1:] - running), 0.0) * step_sizes
    )
    local_state = jnp.einsum(
        "mtc,mtn->mcn", spread(leave_weight) * signal, keys[:, :, :STATE], precision=HIGHEST
    )
    def by_pair(values):
        return values.reshape(micro, tokens, pairs, 2).transpose(0, 2, 1, 3)

    def flag(values):
        return jnp.broadcast_to(
            values.astype(F32)[:, None, :, None], (micro, pairs, tokens, 1)
        )

    cols = jnp.concatenate(
        [
            by_pair(running),
            by_pair(step_sizes),
            flag(segments),
            flag(segment_before),
            jnp.zeros((micro, pairs, tokens, 2), F32),
        ],
        axis=3,
    )
    rows = cols.transpose(0, 1, 3, 2)
    state_in = chain(passing, local_state, 1, 8)
    experts = [fetch_expert(0, state_in)]
    local_out = scan_forward(signal, keys, cols, rows)
    shared_shard = jnp.concatenate(
        [shared_up.reshape(slice_rows, 2 * shared_local), shared_down.T], axis=1
    )
    grad_group = lax.all_gather(
        tied(grad_rows, state_in), ("seq", "head"), axis=1, tiled=True, axis_index_groups=groups
    ).reshape(micro, MEMBERS, tokens, D)
    skip_wide, entry_wide = spread(skip_gain), spread(entry_weight)
    from_state = jnp.einsum(
        "mtn,mcn->mtc", keys[:, :, STATE:], state_in, precision=HIGHEST
    )
    mixer_out = local_out + entry_wide * from_state + skip_wide * signal
    gate_act = jax.nn.silu(gate_pre)
    gated = mixer_out * gate_act
    squares = lax.psum(jnp.sum(gated * gated, axis=2), "head")
    scale_gate = lax.rsqrt(squares / INNER + EPSILON)[:, :, None]
    gate_normed = (gated * scale_gate * gate_gain).astype(BF)
    mix_rows = reduce_rows(mm(gate_normed, out_t, ((2,), (1,)), BF), 1)
    resid_mid = resid_in + mix_rows
    scale_moe = rms_scale(resid_mid)
    moe_rows = (resid_mid * scale_moe * gains[1]).astype(BF)
    moe_group = gather_group(moe_rows, 2)

    expert_ids = jnp.arange(expert_total, dtype=jnp.int32)
    shared_full = lax.all_gather(tied(shared_shard, moe_group), "seq", axis=0, tiled=True)
    shared_flat, shared_down_t = jnp.split(shared_full, [2 * shared_local], axis=1)
    experts += [fetch_expert(own, moe_group) for own in range(1, own_experts)]

    def dense_weights(route_lines, rows):
        logits = mm(rows, router_full, ((rows.ndim - 1,), (0,)))
        named = jnp.any(route_lines[..., None] == expert_ids, axis=-3)
        top = jnp.max(jnp.where(named, logits, -jnp.inf), axis=-1, keepdims=True)
        raised = jnp.where(named, jnp.exp(logits - top), 0.0)
        return named, raised / jnp.sum(raised, axis=-1, keepdims=True)

    named_group, weight_group = dense_weights(route_group[:, :, :TOPK], moe_group)
    first_own = head_rank * experts_local + member * own_experts
    def shared_expert(after):
        moe_own = lax.dynamic_index_in_dim(tied(moe_group, after), member, 1, False)
        grad_own = lax.dynamic_index_in_dim(grad_group, member, 1, False)
        shared_both = mm(moe_own, shared_flat, ((2,), (0,)))
        shared_gate, shared_linear = shared_both[..., :shared_local], shared_both[..., shared_local:]
        shared_act = (jax.nn.silu(shared_gate) * shared_linear).astype(BF)
        shared_out = mm(shared_act, shared_down_t, ((2,), (1,)))
        shared_grad_act = mm(grad_own, shared_down_t, ((2,), (0,)))
        shared_grad = jnp.concatenate(
            [
                shared_grad_act * shared_linear * squash_slope(shared_gate),
                shared_grad_act * jax.nn.silu(shared_gate),
            ],
            axis=-1,
        ).astype(BF)
        shared_back = mm(shared_grad, shared_flat, ((2,), (1,)))
        grad_shared_up = mm(moe_own, shared_grad, ((0, 1), (0, 1)), BF)
        grad_shared_down_t = mm(grad_own, shared_act, ((0, 1), (0, 1)), BF)
        return shared_out, shared_back, grad_shared_up, grad_shared_down_t

    blocks = micro * MEMBERS
    sums, expert_grads, weight_grads, expert_backs = (), [], [], []
    for own in range(own_experts):
        chosen = (expert_ids == first_own + own).astype(F32)
        named = jnp.sum(named_group * chosen, axis=-1)
        weight = jnp.sum(weight_group * chosen, axis=-1)
        rank = mm(named.astype(BF), until.astype(BF), ((2,), (0,))) - 1.0
        lines = jnp.stack([jnp.where(named > 0.0, rank, -1.0), weight], axis=2)
        lines = jnp.pad(lines, ((0, 0), (0, 0), (0, 6), (0, 0))).reshape(blocks, 8, tokens)
        *sums, dots, grads = run_expert(
            capacity,
            lines,
            moe_group.reshape(blocks, tokens, D),
            grad_group.reshape(blocks, tokens, D),
            tied(experts[own], *((shared[1], expert_grads[-1]) if own else (moe_group,))),
            tuple(sums),
        )
        weight_grads.append(dots[:, 0].reshape(micro, MEMBERS, tokens))
        expert_grads.append(grads)
        if own == 0:
            shared = shared_expert(sums[1])
    shared_out, shared_back, grad_shared_up, grad_shared_down_t = shared
    ffn_sum, back_sum = [s.reshape(micro, MEMBERS, tokens, D) for s in sums]

    def group_partial(total, own_part):
        mine = lax.dynamic_slice_in_dim(total, member, 1, 1).astype(F32) + own_part[:, None]
        return lax.dynamic_update_slice_in_dim(total, mine.astype(BF), member, 1)

    expert_backs = [return_expert(grads) for grads in expert_grads[:-1]]
    weight_grad = lax.all_to_all(
        tied(jnp.stack(weight_grads, axis=-1), *expert_backs)
        .reshape(micro, MEMBERS * head_count, row_count, own_experts)
        .transpose(1, 0, 2, 3),
        ("seq", "head"),
        0,
        0,
        tiled=True,
        axis_index_groups=groups,
    )
    weight_grad = (
        weight_grad.reshape(MEMBERS, head_count, micro, row_count, own_experts)
        .transpose(2, 3, 1, 0, 4)
        .reshape(micro, row_count, expert_total)
    )
    back_partial = group_partial(back_sum, shared_back)
    back_rows = reduce_group(back_partial, 3)
    ffn_partial = group_partial(ffn_sum, shared_out)
    route_rows = own_rows(routes).transpose(0, 2, 1)
    named_rows, weight_rows = dense_weights(route_rows, moe_rows)
    weight_grad = jnp.where(named_rows, weight_grad, 0.0)
    logit_grad = weight_rows * (
        weight_grad - jnp.sum(weight_rows * weight_grad, axis=-1, keepdims=True)
    )
    logit_grad = logit_grad.astype(BF)
    grad_router = mm(moe_rows, logit_grad, ((0, 1), (0, 1)))
    back_rows = back_rows + mm(logit_grad, router_full, ((2,), (1,)))
    grad_mid = norm_back(back_rows, resid_mid, gains[1], scale_moe) + grad_rows.astype(F32)
    grad_moe_gain = jnp.sum(back_rows * resid_mid * scale_moe, axis=(0, 1))

    grad_mid_low = grad_mid.astype(BF)
    row_dots = jnp.sum(grad_mid_low.astype(F32) * mix_rows, axis=2)
    grad_mix, row_dots = cube_gather(
        [head_job(row_count, D, 1), head_job(8, row_count, 1)],
        [grad_mid_low, jnp.broadcast_to(row_dots[:, None], (micro, 8, row_count))],
        4,
    )
    grad_mix = grad_mix.reshape(micro, tokens, D)
    grad_mid_features = to_features(grad_mid)
    grad_gate_normed = mm(grad_mix, out_t, ((2,), (0,)))
    weighted = grad_gate_normed * gate_gain
    products = row_dots[:, :, 0].reshape(micro, tokens, 1) / scale_gate
    grad_gated = scale_gate * weighted - gated * (
        scale_gate * scale_gate * scale_gate * products / INNER
    )
    grad_gate_gain = jnp.sum(grad_gate_normed * gated * scale_gate, axis=(0, 1))
    grad_mixer = grad_gated * gate_act
    grad_gate_low = (grad_gated * mixer_out * squash_slope(gate_pre)).astype(BF)
    entry_grad = jnp.einsum(
        "mtc,mtn->mcn", entry_wide * grad_mixer, keys[:, :, STATE:], precision=HIGHEST
    )
    grad_out_t = mm(grad_mix, gate_normed, ((0, 1), (0, 1)), BF)
    grad_gate_proj = mm(normed, grad_gate_low, ((0, 1), (0, 1)), BF)
    second_grads = lane_padded(
        jnp.concatenate([grad_gate_proj, grad_out_t, grad_shared_up, grad_shared_down_t], axis=1)
    ).reshape(1, seq_count, slice_rows, -1)
    ffn_partial = ffn_partial.reshape(micro, MEMBERS * head_count, row_count, D)
    ffn_rows, grad_second = cube_reduce(
        [group_job(row_count, D, -1), seq_job(slice_rows, second_grads.shape[3], -1)],
        [tied(ffn_partial, entry_grad), second_grads],
        5,
    )
    grad_gate_in = mm(grad_gate_low, proj_gate, ((2,), (1,)))
    state_grad = chain(passing, tied(entry_grad, ffn_rows), -1, 9)
    output = to_features((resid_mid + ffn_rows).astype(BF))
    expert_backs.append(return_expert(expert_grads[-1], state_grad))
    grad_signal, grad_keys, grad_cols, grad_rows_part = scan_backward(
        signal, keys, cols, rows, grad_mixer, state_in, state_grad
    )
    grad_skip = jnp.sum(
        jnp.sum(grad_mixer * signal, axis=(0, 1)).reshape(heads_local, HEAD_DIM), axis=1
    )
    grad_act = jnp.concatenate([grad_signal + skip_wide * grad_mixer, grad_keys], axis=2)
    small = grad_cols[..., : SEG] + grad_rows_part[:, :, :SEG].transpose(0, 1, 3, 2)

    def by_head(values):
        return values.transpose(0, 2, 1, 3).reshape(micro, tokens, heads_local)

    grad_running, grad_steps = by_head(small[..., RUN:STEP]), by_head(small[..., STEP:SEG])
    grad_log = jnp.einsum("ij,mjh->mih", until, grad_running, precision=HIGHEST)
    grad_decay = -jnp.sum(grad_log * step_sizes, axis=(0, 1))
    grad_step_raw = (grad_steps - grad_log * decay_rate) * jax.nn.sigmoid(step_raw)
    grad_step_bias = jnp.sum(grad_step_raw, axis=(0, 1))
    grad_step_low = grad_step_raw.astype(BF)
    grad_conv = grad_act * squash_slope(conv_out)
    grad_next = jnp.concatenate(
        [grad_conv, lax.ppermute(grad_conv[:, :EDGE], "seq", behind)], axis=1
    )
    grad_conv_offset = jnp.sum(grad_conv, axis=(0, 1))
    grad_pre = grad_conv * conv_weight[0]
    taps = [jnp.sum(grad_conv * conv_in[:, EDGE:], axis=(0, 1))]
    for offset in range(1, CONV):
        shifted = conv_in[:, EDGE - offset : EDGE - offset + tokens]
        taps.append(
            jnp.sum(jnp.where(keep(offset, 0, tokens), grad_conv * shifted, 0.0), axis=(0, 1))
        )
        grad_pre = grad_pre + jnp.where(
            keep(offset, offset, tokens),
            grad_next[:, offset : offset + tokens] * conv_weight[offset],
            0.0,
        )
    grad_conv_weight = jnp.stack(taps)
    grad_pre = grad_pre.astype(BF)

    columns = first_full.shape[1]
    grad_all = jnp.concatenate([grad_pre, grad_step_low], axis=2)
    grad_all = jnp.pad(grad_all, ((0, 0), (0, 0), (0, columns - grad_all.shape[2])))
    grad_first = grad_gate_in + mm(grad_all, first_full, ((2,), (1,)))
    grad_first_sums = lax.psum(jnp.sum(grad_first * gains[0] * hidden_wide, axis=2), "head")
    first_grads = mm(normed, grad_all, ((0, 1), (0, 1)), BF).reshape(
        1, seq_count, slice_rows, columns
    )
    router_grads = lane_padded(grad_router.astype(BF)).reshape(1, seq_count, slice_rows, -1)
    wide = local_width % 128 == 0
    grad_first = grad_first.astype(BF)
    if not wide:
        grad_first = grad_first.reshape(micro, tokens, head_count, local_width)
        grad_first = grad_first.transpose(0, 2, 1, 3)
    first_grads = tied(first_grads, expert_backs[-1])
    first_features, grad_first_w, grad_router_w = cube_reduce(
        [
            head_job(tokens, local_width, -1, wide),
            seq_job(slice_rows, columns, -1),
            seq_job(slice_rows, router_grads.shape[3], -1),
        ],
        [grad_first, first_grads, router_grads],
        6,
    )
    resid_features = hidden.astype(F32)
    grad_in = scale_mix * (first_features * mix_gain) - resid_features * (
        scale_mix * scale_mix * scale_mix * grad_first_sums[:, :, None] / D
    )
    input_grad = grad_in + grad_mid_features
    cuts = [inner_local, inner_local, 2 * shared_local]
    cuts = [sum(cuts[: i + 1]) for i in range(3)]
    gate_w, out_w, shared_up_w, shared_down_w = jnp.split(grad_second[0], cuts + [sum(cuts[-1:]) + shared_local], axis=1)[:4]
    grad_first_w = grad_first_w[0]
    inner_w, step_w = grad_first_w[:, :inner_local], grad_first_w[:, channels : channels + heads_local]
    over_heads = jnp.concatenate(
        [
            grad_first_w[:, inner_local:channels],
            grad_router_w[0, :, :expert_total],
        ],
        axis=1,
    )
    expert_w = jnp.stack(
        [
            jnp.sum(
                back.reshape(seq_count // MEMBERS, MEMBERS, slice_rows, 3 * EFF).astype(F32), axis=0
            )
            for back in expert_backs
        ],
        axis=1,
    ).reshape(experts_local, slice_rows, 3 * EFF)
    own_sizes = [CONV * inner_local, inner_local, inner_local, heads_local, heads_local, heads_local]
    own_small = in_rows(
        [
            grad_conv_weight[:, :inner_local],
            grad_conv_offset[:inner_local],
            grad_gate_gain,
            grad_step_bias,
            grad_decay,
            grad_skip,
            jnp.sum(first_features * resid_features * scale_mix, axis=(0, 1)),
        ]
    )
    all_sizes = [CONV * 2 * STATE, 2 * STATE, D]
    all_small = in_rows(
        [grad_conv_weight[:, inner_local:], grad_conv_offset[inner_local:], grad_moe_gain]
    )
    seq_bits, head_bits = bits_in("seq", seq_count), bits_in("head", head_count)
    over_heads = lane_padded(over_heads)[None]

    def plain_job(array, bits, slot_of):
        return Job([((0, array.shape[1]), (0, array.shape[2]), bits)], slot_of)

    heads_found, own_found, all_found = cube_gather(
        [
            plain_job(over_heads, head_bits, slot_in_head),
            plain_job(own_small, seq_bits, slot_in_seq),
            plain_job(all_small, seq_bits + head_bits, slot_in_mesh),
        ],
        [over_heads, own_small, all_small],
        7,
        True,
    )
    over_heads = jnp.sum(heads_found[0], axis=0)
    state_w, router_w = over_heads[:, : 2 * STATE], over_heads[:, 2 * STATE : 2 * STATE + expert_total]

    def taken(found, sizes):
        return jnp.split(jnp.sum(found[0], axis=0).reshape(-1), [sum(sizes[: i + 1]) for i in range(len(sizes))])

    conv_inner_w, inner_bias_w, gate_gain_w, step_bias_w, decay_w, skip_w, mix_gain_w = taken(
        own_found, own_sizes
    )
    conv_state_w, state_bias_w, moe_gain_w, _ = taken(all_found, all_sizes)
    return (
        output,
        input_grad,
        mix_gain_w[:local_width],
        jnp.stack([gate_w, inner_w]),
        state_w,
        step_w,
        conv_inner_w.reshape(CONV, inner_local),
        conv_state_w.reshape(CONV, 2 * STATE),
        inner_bias_w,
        state_bias_w,
        step_bias_w,
        decay_w,
        skip_w,
        gate_gain_w,
        out_w.T,
        lax.dynamic_slice_in_dim(moe_gain_w, head_rank * local_width, local_width, 0),
        router_w,
        expert_w[:, :, : 2 * EFF],
        expert_w[:, :, 2 * EFF :].transpose(0, 2, 1),
        shared_up_w.reshape(slice_rows, 2, shared_local),
        shared_down_w.T,
    )


def solution(mesh):
    return jax.shard_map(
        body,
        mesh=mesh,
        in_specs=(
            P(None, "seq", "head"),
            P(None, "seq", "head"),
            P(),
            P(),
            P(None, "seq", None),
            P("head"),
            P(None, "seq", "head"),
            P("seq", None),
            P("seq", "head"),
            P(None, "head"),
            P(),
            P("head"),
            P(),
            P("head"),
            P("head"),
            P("head"),
            P("head"),
            P("head", "seq"),
            P("head"),
            P("seq", None),
            P("head", "seq", None),
            P("head", None, "seq"),
            P("seq", None, "head"),
            P("head", "seq"),
        ),
        out_specs=(
            P(None, "seq", "head"),
            P(None, "seq", "head"),
            P("head"),
            P(None, "seq", "head"),
            P("seq", None),
            P("seq", "head"),
            P(None, "head"),
            P(),
            P("head"),
            P(),
            P("head"),
            P("head"),
            P("head"),
            P("head"),
            P("head", "seq"),
            P("head"),
            P("seq", None),
            P("head", "seq", None),
            P("head", None, "seq"),
            P("seq", None, "head"),
            P("head", "seq"),
        ),
        check_vma=False,
    )
```
